32 devices in a mesh: exp: 8 (over z, x), seq: 4 (over y, core).
Axes of the slice: x: 2, y: 2, z: 4, core: 2. Of those that a mesh axis runs over, the one named last changes fastest.
Arguments:
- tokens: bfloat16 [16, 2048, 768], P('exp', 'seq'), may hold values from -6 to 6
- query_weight: bfloat16 [768, 768], P(('exp', 'seq')), may hold values from -0.21875 to 0.21875
- key_weight: bfloat16 [768, 768], P(('exp', 'seq')), may hold values from -0.21875 to 0.21875
- value_weight: bfloat16 [768, 768], P(('exp', 'seq')), may hold values from -0.21875 to 0.21875
- out_weight: bfloat16 [768, 768], P(('exp', 'seq')), may hold values from -3.5 to 3.5
- router_weight: bfloat16 [768, 8], P(('exp', 'seq')), may hold values from -0.15625 to 0.15625
- attn_gain: bfloat16 [768], P(('exp', 'seq')), may hold values from 0.5 to 1.5
- moe_gain: bfloat16 [768], P(('exp', 'seq')), may hold values from 0.5 to 1.5
- bias_table: float32 [32, 12], replicated, may hold values from -4 to 4
- expert_in: bfloat16 [8, 768, 3072], P('exp', None, 'seq'), may hold values from -0.21875 to 0.21875
- expert_out: bfloat16 [8, 3072, 768], P('exp', 'seq'), may hold values from -1.5 to 1.5
- expert_id: int32 [16, 2048], P('exp', 'seq'), may hold values from 0 to 7, as said below
- slot_id: int32 [16, 2048], P('exp', 'seq'), may hold values from 0 to 160, as said below
- bucket_id: int32 [4095], replicated, may hold values from 0 to 31, as said below
- cotangent: bfloat16 [16, 2048, 768], P('exp', 'seq'), may hold values from -6 to 6
Outputs:
- output: bfloat16 [16, 2048, 768], P('exp', 'seq')
- input_grad: float32 [16, 2048, 768], P('exp', 'seq')
- query_weight_grad: float32 [768, 768], P(('exp', 'seq'))
- key_weight_grad: float32 [768, 768], P(('exp', 'seq'))
- value_weight_grad: float32 [768, 768], P(('exp', 'seq'))
- out_weight_grad: float32 [768, 768], P(('exp', 'seq'))
- router_weight_grad: float32 [768, 8], P(('exp', 'seq'))
- attn_gain_grad: float32 [768], P(('exp', 'seq'))
- moe_gain_grad: float32 [768], P(('exp', 'seq'))
- bias_table_grad: float32 [32, 12], replicated
- expert_in_grad: float32 [8, 768, 3072], P('exp', None, 'seq')
- expert_out_grad: float32 [8, 3072, 768], P('exp', 'seq')
The draws below stay inside these ranges and needn't reach their ends.
Inputs may be any that keep to these rules, and one draw needn't show every extreme that they name: `expert_id`: in the tokens of one device (sequences n with equal n // 2, positions with equal p // 512), some expert is named by more than 160 tokens. slot_id is the number of earlier tokens of the same device with the same expert_id, earlier meaning a lower sequence, then a lower position; it is 160 where that number is 160 or more, and the token is then dropped. `bucket_id`: for offsets o - (2047) of zero or more the bucket is below 16, for negative ones 32 // 2 or more; on each side it never falls as the offset's magnitude grows.
All inputs are finite; a program needn't handle non-finite values.
Results may differ from the reference program's by a relative error of at most 0.015.
Values may be sent and summed in bfloat16 or wider, within the bound.
A program may use at most 256 MiB of HBM per device.

```python
from functools import partial
import jax
import jax.numpy as jnp
from jax import lax

D = 768
HEADS = 12
HEAD_DIM = 64
FF = 3072
BUCKETS = 32
SEQ_LEN = 2048
SEQS = 2
STRETCH = 512
TOK_DEV = 1024
SEQ_ALL = 16
EXPERTS = 8
CAP = 160
N_SEQ = 4


def route_plan(key):
    hot_expert = jax.random.randint(jax.random.fold_in(key, 101), (), 0, EXPERTS)
    block_total = EXPERTS * (SEQ_LEN // STRETCH)

    def one_block(block_key):
        base_key, order_key, other_key = jax.random.split(block_key, 3)
        uniform_ids = jax.random.randint(base_key, (TOK_DEV,), 0, EXPERTS)
        shuffled = jax.random.permutation(order_key, TOK_DEV)
        ranking = jnp.zeros((TOK_DEV,), jnp.int32).at[shuffled].set(jnp.arange(TOK_DEV, dtype=jnp.int32))
        second_expert = jax.random.randint(other_key, (), 0, EXPERTS)
        chosen_ids = jnp.where(ranking < 2 * CAP, hot_expert, jnp.where(ranking < 3 * CAP + 2, second_expert, uniform_ids))
        indicator = (chosen_ids[:, None] == jnp.arange(EXPERTS)[None, :]).astype(jnp.int32)
        earlier = jnp.cumsum(indicator, axis=0) - indicator
        slot_rank = jnp.minimum(jnp.sum(earlier * indicator, axis=1), CAP)
        return (chosen_ids.astype(jnp.int32), slot_rank.astype(jnp.int32))
    chosen_ids, slot_rank = jax.vmap(one_block)(jax.random.split(jax.random.fold_in(key, 202), block_total))

    def arrange(flat_ids):
        arranged = flat_ids.reshape(EXPERTS, SEQ_LEN // STRETCH, SEQS, STRETCH)
        return jnp.transpose(arranged, (0, 2, 1, 3)).reshape(SEQS * EXPERTS, SEQ_LEN)
    return (arrange(chosen_ids), arrange(slot_rank))


def draw_expert_id(key, part):
    return route_plan(key)[0]


def draw_slot_id(key, part):
    return route_plan(key)[1]


def draw_bucket_id(key, part):
    key = jax.random.fold_in(key, 7)

    def boundaries(side_key):
        near_key, far_key = jax.random.split(side_key)
        near = jnp.sort(jax.random.permutation(near_key, 15)[:8] + 1)
        far = jnp.sort(jax.random.permutation(far_key, SEQ_LEN - 16)[:7] + 16)
        return jnp.concatenate([near, far]).astype(jnp.int32)
    ahead = boundaries(jax.random.fold_in(key, 1))
    behind = boundaries(jax.random.fold_in(key, 2))
    offset = jnp.arange(2 * SEQ_LEN - 1, dtype=jnp.int32) - (SEQ_LEN - 1)
    distance = jnp.abs(offset)
    ahead_count = jnp.sum((distance[:, None] >= ahead[None, :]).astype(jnp.int32), axis=1)
    behind_count = jnp.sum((distance[:, None] >= behind[None, :]).astype(jnp.int32), axis=1)
    return jnp.where(offset >= 0, ahead_count, BUCKETS // 2 + behind_count).astype(jnp.int32)


def raised(drawn, key, source, target, shards_of, factor):
    owner, partner = [(jnp.arange(drawn.shape[axis_at]) // (drawn.shape[axis_at] // shards_of)).reshape([-1 if axis == axis_at else 1 for axis in range(drawn.ndim)]) for axis_at in (source, target)]
    chosen = jax.random.permutation(key, shards_of)[partner]
    strong = (owner == chosen) | (owner == (partner + shards_of // 2) % shards_of)
    return jnp.where(strong, factor * drawn, drawn)


def block_levels(own_key, shape, cuts, low, high):
    factor_of, own = 1.0, jax.random.fold_in(own_key, 6)
    for dim, blocks in cuts:
        steps = jnp.exp(jax.random.uniform(jax.random.fold_in(own, dim), (blocks,), jnp.float32, low / len(cuts), high / len(cuts)))
        factor_of = factor_of * jnp.repeat(steps, shape[dim] // blocks).reshape([-1 if axis == dim else 1 for axis in range(len(shape))])
    return factor_of


def centred(own_key, shape, spread, most, cuts=(), kind=jnp.bfloat16):
    level = block_levels(own_key, shape, cuts, -0.22, 0.18) if cuts else 1.0
    entries = jax.random.normal(own_key, shape, jnp.float32) * spread * level
    return jnp.minimum(jnp.maximum(entries, -most), most).astype(kind)


def noise_with(stream_key, dims, scale, bound, cuts, heavy, held_as=jnp.bfloat16):
    entries = scale * jax.random.normal(stream_key, dims, jnp.float32)
    if cuts:
        entries = entries * block_levels(stream_key, dims, cuts, -0.22, 0.18)
    return jnp.clip(raised(entries, jax.random.fold_in(stream_key, 3), *heavy), -bound, bound).astype(held_as)


def setup_inputs(seed: int = 0) -> dict:
    arg_keys = jax.random.split(jax.random.key(seed), 16)
    tokens = noise_with(arg_keys[0], (SEQ_ALL, SEQ_LEN, D), 1.0, 6.0, ((0, 8), (1, 4)), (0, 2, 8, 2.0))
    query_weight = centred(arg_keys[1], (D, D), D ** -0.5, 0.21875, ((0, 32),))
    key_weight = centred(arg_keys[2], (D, D), D ** -0.5, 0.21875, ((0, 32),))
    value_weight = centred(arg_keys[3], (D, D), D ** -0.5, 0.21875, ((0, 32),))
    out_weight = centred(arg_keys[4], (D, D), (max(D // 256, 1)) ** -0.5, 3.5, ((0, 32),))
    router_weight = centred(arg_keys[5], (D, EXPERTS), (2 * D) ** -0.5, 0.15625, ((0, 32),))
    attn_gain = jnp.clip(1.0 + 0.1 * jax.random.normal(arg_keys[6], (D,), jnp.float32), 0.5, 1.5).astype(jnp.bfloat16)
    moe_gain = jnp.clip(1.0 + 0.1 * jax.random.normal(arg_keys[7], (D,), jnp.float32), 0.5, 1.5).astype(jnp.bfloat16)
    bias_table = centred(arg_keys[8], (BUCKETS, HEADS), 1.0, 4.0, (), jnp.float32)
    expert_in = centred(arg_keys[9], (EXPERTS, D, FF), D ** -0.5, 0.21875, ((0, 8), (2, 4)))
    expert_out = centred(arg_keys[10], (EXPERTS, FF, D), (max(FF // (3 * EXPERTS * EXPERTS), 1)) ** -0.5, 1.5, ((0, 8), (1, 4)))
    expert_id = draw_expert_id(jax.random.fold_in(arg_keys[15], 71), 0)
    slot_id = draw_slot_id(jax.random.fold_in(arg_keys[15], 71), 0)
    bucket_id = draw_bucket_id(jax.random.fold_in(arg_keys[15], 71), 0)
    cotangent = centred(arg_keys[14], (SEQ_ALL, SEQ_LEN, D), 1.0, 6.0, ((0, 8), (1, 4)))
    return {"tokens": tokens, "query_weight": query_weight, "key_weight": key_weight, "value_weight": value_weight, "out_weight": out_weight, "router_weight": router_weight, "attn_gain": attn_gain, "moe_gain": moe_gain, "bias_table": bias_table, "expert_in": expert_in, "expert_out": expert_out, "expert_id": expert_id, "slot_id": slot_id, "bucket_id": bucket_id, "cotangent": cotangent}


@jax.custom_vjp
def low(v):
    return lax.optimization_barrier(v.astype(jnp.bfloat16)).astype(jnp.float32)

@jax.custom_vjp
def low_back(v):
    return v

def low_keep(v):
    return (low(v), None)

def low_pass(kept, grad):
    return (grad,)

def back_keep(v):
    return (v, None)

def back_low(kept, grad):
    return (low(grad),)
low.defvjp(low_keep, low_pass)
low_back.defvjp(back_keep, back_low)
epsilon = 1e-06
score_scale = 0.125
highest = lax.Precision.HIGHEST

def matmul_high(left, right):
    return jnp.dot(left, right, precision=highest, preferred_element_type=jnp.float32)

def norm_rows(values, gain):
    return values * lax.rsqrt(lax.optimization_barrier(jnp.mean(values * values, axis=-1, keepdims=True)) + epsilon) * gain

def attend_sequence(weights, sequence):
    query_weight, key_weight, value_weight, out_weight, attn_gain, offsets = weights
    normed = low(norm_rows(sequence, attn_gain))
    queries = low_back(low(matmul_high(normed, query_weight))).reshape(SEQ_LEN, HEADS, HEAD_DIM)
    keys = low_back(low(matmul_high(normed, key_weight))).reshape(SEQ_LEN, HEADS, HEAD_DIM)
    values = low_back(low(matmul_high(normed, value_weight))).reshape(SEQ_LEN, HEADS, HEAD_DIM)
    positions = jnp.arange(SEQ_LEN, dtype=jnp.int32)
    offset_index = positions[:, None] - positions[None, :] + (SEQ_LEN - 1)
    bias = jnp.transpose(offsets[offset_index], (2, 0, 1))
    raw = jnp.einsum('qhd,khd->hqk', queries, keys, precision=highest)
    scores = low_back(raw * score_scale + bias)
    probs = jax.nn.softmax(scores, axis=-1)
    mixed = jnp.einsum('hqk,khd->qhd', low(probs), values, precision=highest).reshape(SEQ_LEN, D)
    branch = low_back(matmul_high(low_back(low(mixed)), out_weight))
    return sequence + branch

def expert_apply(operands):
    rows, first, second = operands
    pre = low_back(matmul_high(rows, first))
    act = low_back(low(jax.nn.gelu(pre)))
    return low_back(low(matmul_high(act, second)))

def reference(tokens, query_weight, key_weight, value_weight, out_weight, router_weight, attn_gain, moe_gain, bias_table, expert_in, expert_out, expert_id, slot_id, bucket_id, cotangent):
    operands = tuple((item.astype(jnp.float32) for item in (tokens, query_weight, key_weight, value_weight, out_weight, router_weight, attn_gain, moe_gain, bias_table, expert_in, expert_out)))
    group_total = EXPERTS * N_SEQ
    total_slots = group_total * EXPERTS * CAP

    def forward(tokens_f, query_f, key_f, value_f, out_f, router_f, attn_gain_f, moe_gain_f, table_f, first_f, second_f):
        offsets = matmul_high(jax.nn.one_hot(bucket_id, BUCKETS, dtype=jnp.float32), table_f)
        weights = (query_f, key_f, value_f, out_f, attn_gain_f, offsets)
        hidden = lax.map(jax.checkpoint(partial(attend_sequence, weights)), tokens_f)
        moe_in = low(norm_rows(hidden, moe_gain_f))
        logits = low_back(matmul_high(moe_in, router_f))
        gates = jax.nn.softmax(logits, axis=-1)
        picked = jax.nn.one_hot(expert_id, EXPERTS, dtype=jnp.float32)
        gate = lax.optimization_barrier(jnp.sum(gates * picked, axis=-1))
        seq_group = (jnp.arange(SEQ_ALL, dtype=jnp.int32) // SEQS)[:, None] * N_SEQ
        pos_group = (jnp.arange(SEQ_LEN, dtype=jnp.int32) // STRETCH)[None, :]
        groups = seq_group + pos_group
        position = jnp.where(slot_id < CAP, (groups * EXPERTS + expert_id) * CAP + slot_id, total_slots).astype(jnp.int32)
        sent = low_back(moe_in).reshape(-1, D)
        buffer = jnp.zeros((total_slots + 1, D), jnp.float32).at[position.reshape(-1)].add(sent)
        rows = buffer[:total_slots].reshape(group_total, EXPERTS, CAP, D).transpose(1, 0, 2, 3)
        results = lax.map(jax.checkpoint(expert_apply), (rows, first_f, second_f))
        flat = results.transpose(1, 0, 2, 3).reshape(total_slots, D)
        flat = jnp.concatenate([flat, jnp.zeros((1, D), jnp.float32)], axis=0)
        returned = flat[position]
        return hidden + gate[..., None] * returned
    result, pullback = jax.vjp(forward, *operands)
    grads = pullback(cotangent.astype(jnp.float32))
    return (result.astype(jnp.bfloat16), grads[0], grads[1], grads[2], grads[3], grads[4], grads[5], grads[6], grads[7], grads[8], grads[9], grads[10])
```

```python
import functools
import jax
import jax.numpy as jnp
import numpy as np
from jax import lax
from jax.experimental import pallas as pl
from jax.experimental.pallas import tpu as pltpu
NT=(((1,),(1,)),((),()))
NN=(((1,),(0,)),((),()))
LOG2E=1.4426950408889634
MIB=1024*1024

def lane_iota(rows):
    return lax.broadcasted_iota(jnp.int32,(rows,128),1)

def dup_head(values,head):
    values=values.astype(jnp.float32)
    turned=pltpu.roll(values,64,1)
    low=lane_iota(values.shape[0])<64
    return jnp.where(low,values,turned) if head==0 else jnp.where(low,turned,values)

def three_parts(column):
    first=column.astype(jnp.bfloat16).astype(jnp.float32)
    rest=column-first
    second=rest.astype(jnp.bfloat16).astype(jnp.float32)
    return first,second,rest-second

def columns_at(lanes,start,parts,other):
    out=other
    for place,part in enumerate(parts):
        out=jnp.where(lanes==start+place,part,out)
    return out

def split_query(query,head,scale):
    both=dup_head(query,head)*scale
    high=both.astype(jnp.bfloat16).astype(jnp.float32)
    return jnp.where(lane_iota(query.shape[0])<64,high,both-high).astype(jnp.bfloat16)

def fill_strip(strip,vector,rows,width):
    full=width+rows
    step=8
    spread=jnp.broadcast_to(vector,(rows,full))
    turned=pltpu.roll(spread,0,1,stride=1,stride_axis=0)
    strip[...]=turned[:,rows:]

def forward_kernel(heads,length,block,scale,q_ref,k_ref,v_ref,bias_ref,out_ref,o32_ref,lse_ref,strip,kd,va):
    strip_width=strip.shape[1]
    for head in range(heads):
        fill_strip(strip,bias_ref[head:head+1,:],block,strip_width)
        lanes=lane_iota(length)
        kd[...]=dup_head(k_ref[...],head).astype(jnp.bfloat16)
        va[...]=jnp.where(lanes<64,dup_head(v_ref[...],head),jnp.where(lanes==64,1.0,0.0)).astype(jnp.bfloat16)
        def body(step,carry):
            rows=pl.ds(pl.multiple_of(step*block,block),block)
            qa=split_query(q_ref[rows,:],head,scale)
            raw=lax.dot_general(qa,kd[...],NT,preferred_element_type=jnp.float32)
            start=pl.multiple_of(length-block-step*block,block)
            scores=raw+strip[:,pl.ds(start,length)]
            top=jnp.max(scores,axis=1,keepdims=True)
            weights=jnp.exp2(scores-top).astype(jnp.bfloat16)
            mixed=jnp.dot(weights,va[...],preferred_element_type=jnp.float32)
            total=mixed[:,64:65]
            result=mixed/total
            log_total=top+jnp.log2(total)
            lse_ref[rows,:]=jnp.where(lane_iota(block)==head,log_total,lse_ref[rows,:]) if head else jnp.broadcast_to(log_total,(block,128))
            if head==0:
                o32_ref[rows,:]=result
            else:
                both=jnp.where(lane_iota(block)<64,o32_ref[rows,:],pltpu.roll(result,64,1))
                o32_ref[rows,:]=both
            return carry
        lax.fori_loop(0,length//block,body,0)
    out_ref[...]=o32_ref[...].astype(jnp.bfloat16)

def attend(q,k,v,bias_vec,heads,chunk_ids,block=256):
    length=q.shape[0]
    scale=LOG2E/8
    spec=lambda c: pl.BlockSpec((length,128),lambda i,c=c:(0,c))
    full=pl.BlockSpec((length,128),lambda i:(0,0))
    width=2*length-block
    return pl.pallas_call(
        functools.partial(forward_kernel,heads,length,block,scale),
        grid=(1,),
        in_specs=[spec(chunk_ids[0]),spec(chunk_ids[1]),spec(chunk_ids[2]),pl.BlockSpec(bias_vec.shape,lambda i:(0,0))],
        out_specs=[full,full,full],
        out_shape=[jax.ShapeDtypeStruct((length,128),jnp.bfloat16),jax.ShapeDtypeStruct((length,128),jnp.float32),jax.ShapeDtypeStruct((length,128),jnp.float32)],
        scratch_shapes=[pltpu.VMEM((block,width),jnp.float32),pltpu.VMEM((length,128),jnp.bfloat16),pltpu.VMEM((length,128),jnp.bfloat16)],
        compiler_params=pltpu.CompilerParams(vmem_limit_bytes=56*MIB),
        name="attend_forward",
    )(q,k,v,bias_vec)

def backward_kernel(heads,length,bq,bk,scale,q_ref,k_ref,v_ref,do_ref,o32_ref,lse_ref,bias_ref,dqt_ref,dk_ref,dv_ref,diag_ref,strip,grads,ka,va,kt,qa,da,dd,qd,dk_acc,dv_acc):
    width=strip.shape[1]
    full_width=2*length
    lanes=lane_iota(length)
    for head in range(heads):
        fill_strip(strip,bias_ref[head:head+1,:],bk,width)
        grads[...]=jnp.zeros_like(grads)
        kd=dup_head(k_ref[...],head)
        ka[:,:128]=kd.astype(jnp.bfloat16)
        ka[:,128:]=jnp.where(lanes<3,1.0,0.0).astype(jnp.bfloat16)
        kt[...]=jnp.transpose(kd)[:64,:].astype(jnp.bfloat16)
        va[...]=jnp.where(lanes<64,dup_head(v_ref[...],head),jnp.where(lanes<67,1.0,0.0)).astype(jnp.bfloat16)
        qa[:,:128]=split_query(q_ref[...],head,scale)
        qa[:,128:]=columns_at(lanes,0,three_parts(-lse_ref[:,head:head+1]),0.0).astype(jnp.bfloat16)
        qd[...]=dup_head(q_ref[...],head).astype(jnp.bfloat16)
        dod=dup_head(do_ref[...],head)
        dd[...]=dod.astype(jnp.bfloat16)
        od=dup_head(o32_ref[...],head)
        delta=0.5*jnp.sum(dod*od,axis=1,keepdims=True)
        da[...]=columns_at(lanes,64,three_parts(-delta),jnp.where(lanes<64,dod,0.0)).astype(jnp.bfloat16)
        dk_acc[...]=jnp.zeros_like(dk_acc)
        dv_acc[...]=jnp.zeros_like(dv_acc)
        for qb in range(length//bq):
            qs=slice(qb*bq,(qb+1)*bq)
            def body(kb,dq):
                ks=pl.ds(pl.multiple_of(kb*bk,bk),bk)
                raw=lax.dot_general(ka[ks,:],qa[qs,:],NT,preferred_element_type=jnp.float32)
                start=pl.multiple_of(qb*bq+(length-bk)-kb*bk,128)
                probs=jnp.exp2(raw+strip[:,pl.ds(start,bq)])
                up=lax.dot_general(va[ks,:],da[qs,:],NT,preferred_element_type=jnp.float32)
                score_grad=probs*up
                grads[:,pl.ds(pl.multiple_of(start+bk,128),bq)]+=score_grad
                low=score_grad.astype(jnp.bfloat16)
                dv_acc[ks,:]+=jnp.dot(probs.astype(jnp.bfloat16),dd[qs,:],preferred_element_type=jnp.float32)
                dk_acc[ks,:]+=jnp.dot(low,qd[qs,:],preferred_element_type=jnp.float32)
                return dq+jnp.dot(kt[:,ks],low,preferred_element_type=jnp.float32)
            dq=lax.fori_loop(0,length//bk,body,jnp.zeros((64,bq),jnp.float32))
            dqt_ref[head*64:(head+1)*64,qs]=(dq*0.125).astype(jnp.bfloat16)
        if head==0:
            dk_ref[...]=(dk_acc[...]*0.125).astype(jnp.bfloat16)
            dv_ref[...]=dv_acc[...].astype(jnp.bfloat16)
        else:
            dk_ref[...]=jnp.where(lanes<64,dk_ref[...].astype(jnp.float32),dk_acc[...]*0.125).astype(jnp.bfloat16)
            dv_ref[...]=jnp.where(lanes<64,dv_ref[...].astype(jnp.float32),dv_acc[...]).astype(jnp.bfloat16)
        total=grads[0:8,:]
        for group in range(1,bk//8):
            total=total+pltpu.roll(grads[8*group:8*group+8,:],full_width-8*group,1)
        row=lax.broadcasted_iota(jnp.int32,(8,full_width),0)
        for part in range(1,8):
            total=jnp.where(row==part,pltpu.roll(total,full_width-part,1),total)
        diag_ref[head:head+1,:]=jnp.sum(total,axis=0,keepdims=True)

def attend_back(q,k,v,do,o32,lse,bias_vec,heads,chunk_ids,bq=512,bk=256):
    length=q.shape[0]
    scale=LOG2E/8
    spec=lambda c: pl.BlockSpec((length,128),lambda i,c=c:(0,c))
    full=pl.BlockSpec((length,128),lambda i:(0,0))
    width=2*length-bk
    f32,b16=jnp.float32,jnp.bfloat16
    return pl.pallas_call(
        functools.partial(backward_kernel,heads,length,bq,bk,scale),
        grid=(1,),
        in_specs=[spec(chunk_ids[0]),spec(chunk_ids[1]),spec(chunk_ids[2]),spec(chunk_ids[3]),full,full,pl.BlockSpec(bias_vec.shape,lambda i:(0,0))],
        out_specs=[pl.BlockSpec((128,length),lambda i:(0,0)),full,full,pl.BlockSpec((8,2*length),lambda i:(0,0))],
        out_shape=[jax.ShapeDtypeStruct((128,length),b16),jax.ShapeDtypeStruct((length,128),b16),jax.ShapeDtypeStruct((length,128),b16),jax.ShapeDtypeStruct((8,2*length),f32)],
        scratch_shapes=[pltpu.VMEM((bk,width),f32),pltpu.VMEM((bk,2*length),f32),pltpu.VMEM((length,256),b16),pltpu.VMEM((length,128),b16),pltpu.VMEM((64,length),b16),
            pltpu.VMEM((length,256),b16),pltpu.VMEM((length,128),b16),pltpu.VMEM((length,128),b16),pltpu.VMEM((length,128),b16),pltpu.VMEM((length,128),f32),pltpu.VMEM((length,128),f32)],
        compiler_params=pltpu.CompilerParams(vmem_limit_bytes=56*MIB),
        name="attend_backward",
    )(q,k,v,do,o32,lse,bias_vec)


from jax.sharding import PartitionSpec as P

EPSILON=1e-06
BOTH=("exp","seq")

def inverse_rms(values):
    return lax.rsqrt(jnp.mean(values*values,axis=-1,keepdims=True)+EPSILON)

def matmul(left,right,dims=NN):
    return lax.dot_general(left,right,dims,preferred_element_type=jnp.float32)

TN=(((0,),(0,)),((),()))

def swap_parts(values,axis):
    return lax.all_to_all(values,axis,split_axis=0,concat_axis=0,tiled=True)

def reversed_ids(ids):
    flip=np.eye(128,dtype=np.float32)[::-1]
    rows=ids.shape[0]//128
    flip_rows=np.eye(rows,dtype=np.float32)[::-1]
    grid=ids.astype(jnp.bfloat16).reshape(rows,128)
    grid=matmul(grid,jnp.asarray(flip,jnp.bfloat16)).astype(jnp.bfloat16)
    return matmul(jnp.asarray(flip_rows,jnp.bfloat16),grid).reshape(-1)

def offset_rows(ids,table):
    hot=(ids[None,:].astype(jnp.int32)==jnp.arange(table.shape[0],dtype=jnp.int32)[:,None]).astype(jnp.float32)
    return lax.dot_general(table,hot,(((0,),(0,)),((),())),precision=lax.Precision.HIGHEST)

def shards(tokens,query_weight,key_weight,value_weight,out_weight,router_weight,attn_gain,moe_gain,bias_table,expert_in,expert_out,expert_id,slot_id,bucket_id,cotangent):
    f32,b16=jnp.float32,jnp.bfloat16
    seq_count,stretch,width=tokens.shape
    seq_devs=lax.axis_size("seq")
    experts=lax.axis_size("exp")
    devices=seq_devs*experts
    length=stretch*seq_devs
    count=seq_count*stretch
    capacity=(5*count+4*experts-1)//(4*experts)
    buckets,heads=bias_table.shape
    head_dim=width//heads
    groups=seq_devs//seq_count
    own_heads=heads//groups
    per_chunk=2 if own_heads%2==0 else 1
    chunks=own_heads//per_chunk
    used=per_chunk*head_dim
    span=chunks*128
    row_block=width//devices
    place=lax.axis_index("seq")
    group=place%groups
    def by_group(weight):
        cut=weight.reshape(weight.shape[0],groups,chunks,used)
        cut=jnp.pad(cut,((0,0),(0,0),(0,0),(0,128-used)))
        return cut.reshape(weight.shape[0],groups,span)
    stacked=jnp.stack([by_group(w) for w in (query_weight,key_weight,value_weight)],axis=2).reshape(row_block,groups*3*span)
    stacked_full=lax.all_gather(stacked,BOTH,axis=0,tiled=True)
    gains=jnp.stack([attn_gain,moe_gain],axis=1)
    small=jnp.pad(jnp.concatenate([router_weight,gains],axis=1),((0,0),(0,128-router_weight.shape[1]-2)))
    small_full=lax.all_gather(small,BOTH,axis=0,tiled=True)
    out_full=lax.all_gather(out_weight,BOTH,axis=0,tiled=True)
    first_full=lax.all_gather(expert_in,"seq",axis=2,tiled=True)[0]
    second_full=lax.all_gather(expert_out,"seq",axis=1,tiled=True)[0]
    copies=jnp.broadcast_to(tokens[:,None],(seq_count,groups,stretch,width)).reshape(seq_devs,stretch,width)
    own_sequence=swap_parts(copies,"seq").reshape(length,width).astype(f32)
    weight=lax.dynamic_slice_in_dim(stacked_full,group*3*span,3*span,axis=1)
    router_full=small_full[:,:experts]
    attn_gain_full=small_full[:,experts].astype(f32)
    moe_gain_full=small_full[:,experts+1].astype(f32)
    padded=jnp.concatenate([jnp.zeros((1,),jnp.int32),bucket_id])
    forward_ids=reversed_ids(jnp.concatenate([bucket_id,jnp.zeros((1,),jnp.int32)]))
    own_table=lax.dynamic_slice_in_dim(bias_table,group*own_heads,own_heads,axis=1)*LOG2E
    forward_bias=offset_rows(forward_ids,own_table)
    backward_bias=offset_rows(padded,own_table)
    sequence_inverse=inverse_rms(own_sequence)
    normed=(own_sequence*sequence_inverse*attn_gain_full).astype(b16)
    projected=matmul(normed,weight).astype(b16)
    saved,attended_parts=[],[]
    for chunk in range(chunks):
        bias_rows=slice(chunk*per_chunk,(chunk+1)*per_chunk)
        out,out32,log_total=attend(projected,projected,projected,forward_bias[bias_rows],per_chunk,(chunk,chunks+chunk,2*chunks+chunk))
        saved.append((out32,log_total))
        attended_parts.append(swap_parts(out[:,:used].reshape(seq_devs,stretch,used),"seq"))
    attended=jnp.stack(attended_parts,axis=2).reshape(seq_count,groups,stretch,own_heads*head_dim)
    attended=jnp.swapaxes(attended,1,2).reshape(count,width)
    tokens_f=tokens.astype(f32).reshape(count,width)
    hidden=tokens_f+matmul(attended,out_full)
    moe_inverse=inverse_rms(hidden)
    moe_in=(hidden*moe_inverse*moe_gain_full).astype(b16)
    logits=matmul(moe_in,router_full)
    gates=jax.nn.softmax(logits,axis=-1)
    expert_pick=expert_id.reshape(count)
    slot_pick=slot_id.reshape(count)
    picked=(expert_pick[:,None]==jnp.arange(experts,dtype=jnp.int32)[None,:]).astype(f32)
    gate=jnp.sum(gates*picked,axis=-1)
    slots=experts*capacity
    position=jnp.where(slot_pick<capacity,expert_pick*capacity+slot_pick,slots)
    grad_out=cotangent.astype(f32).reshape(count,width)
    result_grad=(gate[:,None]*grad_out).astype(b16)
    hot=(position[None,:]==jnp.arange(slots,dtype=jnp.int32)[:,None]).astype(b16)
    send_rows=matmul(hot,moe_in).astype(b16).reshape(experts,capacity,width)
    rows=swap_parts(send_rows,"exp").reshape(slots,width)
    back_rows=matmul(hot,result_grad).astype(b16).reshape(experts,capacity,width)
    flat_grad=swap_parts(back_rows,"exp").reshape(slots,width)
    pre=matmul(rows,first_full)
    act_f,gelu_pull=jax.vjp(jax.nn.gelu,pre)
    act=act_f.astype(b16)
    result=matmul(act,second_full).astype(b16).reshape(experts,capacity,width)
    returned=swap_parts(result,"exp").reshape(slots,width)
    act_grad=matmul(flat_grad,second_full,NT).astype(b16)
    (pre_grad_f,)=gelu_pull(act_grad.astype(f32))
    pre_grad=pre_grad_f.astype(b16)
    rows_grad=matmul(pre_grad,first_full,NT).astype(b16).reshape(experts,capacity,width)
    grad_home=swap_parts(rows_grad,"exp").reshape(slots,width)
    out_grad_local=matmul(act,flat_grad,TN)
    in_grad_local=matmul(rows,pre_grad,TN)
    expert_in_grad=lax.psum_scatter(in_grad_local[None].astype(b16),"seq",scatter_dimension=2,tiled=True).astype(f32)
    expert_out_grad=lax.psum_scatter(out_grad_local[None].astype(b16),"seq",scatter_dimension=1,tiled=True).astype(f32)
    result_tok=matmul(hot,returned,TN)
    output=(hidden+gate[:,None]*result_tok).astype(b16).reshape(seq_count,stretch,width)
    gate_grad=jnp.sum(grad_out*result_tok,axis=-1)
    rows_tok=matmul(hot,grad_home,TN)
    logits_grad=(gates*(picked-gate[:,None])*gate_grad[:,None]).astype(b16)
    router_part=matmul(moe_in,logits_grad,TN)
    moe_in_grad=rows_tok+matmul(logits_grad,router_full,NT)
    weighted=moe_in_grad*moe_gain_full
    moe_gain_part=jnp.sum(moe_in_grad*hidden*moe_inverse,axis=0)
    inner=jnp.mean(weighted*hidden,axis=-1,keepdims=True)
    hidden_grad=grad_out+weighted*moe_inverse-hidden*(moe_inverse*moe_inverse*moe_inverse)*inner
    branch_grad=hidden_grad.astype(b16)
    heads_grad=matmul(branch_grad,out_full,NT).astype(b16)
    outgoing=heads_grad.reshape(seq_count,stretch,groups,chunks,used)
    outgoing=jnp.transpose(outgoing,(3,0,2,1,4))
    out_part=matmul(attended,branch_grad,TN)
    extra=jnp.pad(jnp.concatenate([router_part,moe_gain_part[:,None]],axis=1),((0,0),(0,128-experts-1)))
    out_piece=jnp.concatenate([out_part,extra],axis=1).astype(b16).reshape(devices,row_block,width+128)
    out_sum=jnp.sum(swap_parts(out_piece,BOTH).astype(f32),axis=0)
    query_grads,key_grads,value_grads,diagonals=[],[],[],[]
    for chunk in range(chunks):
        arriving=swap_parts(outgoing[chunk].reshape(seq_devs,stretch,used),"seq").reshape(length,used)
        arriving=jnp.pad(arriving,((0,0),(0,128-used)))
        bias_rows=slice(chunk*per_chunk,(chunk+1)*per_chunk)
        out32,log_total=saved[chunk]
        dq,dk,dv,diagonal=attend_back(projected,projected,projected,arriving,out32,log_total,backward_bias[bias_rows],per_chunk,(chunk,chunks+chunk,2*chunks+chunk,0))
        query_grads.append(dq)
        key_grads.append(dk)
        value_grads.append(dv)
        diagonals.append(diagonal[:per_chunk])
    query_grad=jnp.concatenate(query_grads,axis=0)
    rest_grad=jnp.concatenate(key_grads+value_grads,axis=1)
    normed_part=matmul(query_grad,weight[:,:span],(((0,),(1,)),((),())))+matmul(rest_grad,weight[:,span:],NT)
    attn_gain_part=jnp.sum(normed_part*own_sequence*sequence_inverse,axis=0)
    normed_sum=jnp.sum(swap_parts(normed_part.astype(b16).reshape(seq_devs,stretch,width),"seq").reshape(seq_count,groups,stretch,width).astype(f32),axis=1)
    query_part=matmul(normed,query_grad,(((0,),(1,)),((),())))
    rest_part=matmul(normed,rest_grad,TN)
    diagonals=jnp.concatenate(diagonals,axis=0)
    hot_bucket=(padded[None,:]==jnp.arange(buckets,dtype=jnp.int32)[:,None]).astype(f32)
    hot_bucket=hot_bucket*(jnp.arange(length*2)>0)[None,:]
    table_part=lax.dot_general(hot_bucket,diagonals,(((1,),(1,)),((),())),precision=lax.Precision.HIGHEST)
    table_wide=jnp.zeros((buckets,heads),f32)
    table_wide=lax.dynamic_update_slice_in_dim(table_wide,table_part,group*own_heads,axis=1)
    bias_table_grad=lax.psum(table_wide,BOTH)
    piece=jnp.concatenate([query_part,rest_part,jnp.pad(attn_gain_part[:,None],((0,0),(0,127)))],axis=1).astype(b16)
    arrived=swap_parts(piece.reshape(devices,row_block,3*span+128),BOTH).astype(f32)
    arrived=jnp.sum(arrived.reshape(devices//groups,groups,row_block,3*span+128),axis=0)
    attn_gain_grad=jnp.sum(arrived[:,:,3*span],axis=0)
    grads=arrived[:,:,:3*span].reshape(groups,row_block,3,chunks,128)[...,:used]
    grads=jnp.transpose(grads,(2,1,0,3,4)).reshape(3,row_block,width)
    tokens_inverse=inverse_rms(tokens_f)
    normed_sum=normed_sum.reshape(count,width)
    weighted=normed_sum*attn_gain_full
    inner=jnp.mean(weighted*tokens_f,axis=-1,keepdims=True)
    input_grad=hidden_grad+weighted*tokens_inverse-tokens_f*(tokens_inverse*tokens_inverse*tokens_inverse)*inner
    return (
        output,
        input_grad.reshape(seq_count,stretch,width),
        grads[0],grads[1],grads[2],
        out_sum[:,:width],
        out_sum[:,width:width+experts],
        attn_gain_grad,
        out_sum[:,width+experts],
        bias_table_grad,
        expert_in_grad,
        expert_out_grad,
    )

def solution(mesh):
    tokens=P("exp","seq",None)
    rows=P(BOTH,None)
    return jax.shard_map(
        shards,
        mesh=mesh,
        in_specs=(tokens,rows,rows,rows,rows,rows,P(BOTH),P(BOTH),P(),P("exp",None,"seq"),P("exp","seq",None),P("exp","seq"),P("exp","seq"),P(),tokens),
        out_specs=(tokens,tokens,rows,rows,rows,rows,rows,P(BOTH),P(BOTH),P(),P("exp",None,"seq"),P("exp","seq",None)),
        check_vma=False,
    )
```

```python
import functools
import jax
import jax.numpy as jnp
import numpy as np
from jax import lax
from jax.experimental import pallas as pl
from jax.experimental.pallas import tpu as pltpu
from jax.sharding import PartitionSpec as P
NT=(((1,),(1,)),((),()))
NN=(((1,),(0,)),((),()))
LOG2E=1.4426950408889634
MIB=1024*1024
TN=(((0,),(0,)),((),()))
MESH=pl.DeviceIdType.MESH
EPSILON=1e-06
BOTH=("exp","seq")

def lane_iota(rows):
    return lax.broadcasted_iota(jnp.int32,(rows,128),1)

def dup_head(values,head):
    values=values.astype(jnp.float32)
    turned=pltpu.roll(values,64,1)
    low=lane_iota(values.shape[0])<64
    return jnp.where(low,values,turned) if head==0 else jnp.where(low,turned,values)

def three_parts(column):
    first=column.astype(jnp.bfloat16).astype(jnp.float32)
    rest=column-first
    second=rest.astype(jnp.bfloat16).astype(jnp.float32)
    return first,second,rest-second

def columns_at(lanes,start,parts,other):
    out=other
    for place,part in enumerate(parts):
        out=jnp.where(lanes==start+place,part,out)
    return out

def split_query(query,head,scale):
    both=dup_head(query,head)*scale
    high=both.astype(jnp.bfloat16).astype(jnp.float32)
    return jnp.where(lane_iota(query.shape[0])<64,high,both-high).astype(jnp.bfloat16)

def fill_strip(strip,vector,rows,width):
    full=width+rows
    step=8
    spread=jnp.broadcast_to(vector,(rows,full))
    turned=pltpu.roll(spread,0,1,stride=1,stride_axis=0)
    strip[...]=turned[:,rows:]


def forward_kernel(heads,block,srows,scale,q_ref,k_ref,v_ref,bias_ref,out_ref,o32_ref,lse_ref,strip,kd,va,scr):
    length=q_ref.shape[0]
    width=strip.shape[1]
    wide=256
    blocks=length//block
    pieces=length//wide
    lanes=lane_iota(length)
    block_lanes=lane_iota(block)
    for head in range(heads):
        fill_strip(strip,bias_ref[head:head+1,:],srows,width)
        kd[...]=dup_head(k_ref[...],head).astype(jnp.bfloat16)
        va[...]=jnp.where(lanes<64,dup_head(v_ref[...],head),jnp.where(lanes==64,1.0,0.0)).astype(jnp.bfloat16)
        def rows_of(step):
            return pl.ds(pl.multiple_of(step*block,block),block)
        def score_piece(step,qa,c,slot,top):
            raw=lax.dot_general(qa,kd[c*wide:(c+1)*wide,:],NT,preferred_element_type=jnp.float32)
            parts=[]
            for part in range(block//srows):
                start=pl.multiple_of(length-srows-step*block-part*srows+c*wide,128)
                parts.append(raw[part*srows:(part+1)*srows]+strip[:,pl.ds(start,wide)])
            scores=jnp.concatenate(parts,axis=0)
            scr[slot,:,c*wide:(c+1)*wide]=scores
            for j in range(wide//128):
                top=jnp.maximum(top,scores[:,j*128:(j+1)*128])
            return top
        def mix_piece(slot,c,top,total):
            weights=jnp.exp2(scr[slot,:,c*wide:(c+1)*wide]-top).astype(jnp.bfloat16)
            return total+jnp.dot(weights,va[c*wide:(c+1)*wide,:],preferred_element_type=jnp.float32)
        def finish(step,top,mixed):
            rows=rows_of(step)
            total=mixed[:,64:65]
            result=mixed/total
            log_total=top+jnp.log2(total)
            if head==0:
                lse_ref[rows,:]=jnp.broadcast_to(log_total,(block,128))
                o32_ref[rows,:]=result
            else:
                lse_ref[rows,:]=jnp.where(block_lanes==head,log_total,lse_ref[rows,:])
                o32_ref[rows,:]=jnp.where(block_lanes<64,o32_ref[rows,:],pltpu.roll(result,64,1))
        def advance(step,slot,top):
            mixing=top is not None
            qa=split_query(q_ref[rows_of(step),:],head,scale)
            new=jnp.full((block,128),-jnp.inf,jnp.float32)
            mixed=jnp.zeros((block,128),jnp.float32)
            for c in range(pieces):
                new=score_piece(step,qa,c,slot,new)
                if mixing:
                    mixed=mix_piece(1-slot,c,top,mixed)
            if mixing:
                finish(step-1,top,mixed)
            return jnp.max(new,axis=1,keepdims=True)
        def body(i,top):
            top=advance(2*i+1,1,top)
            return advance(2*i+2,0,top)
        top=advance(0,0,None)
        top=lax.fori_loop(0,(blocks-1)//2,body,top)
        last=0
        if blocks%2==0:
            top=advance(blocks-1,1,top)
            last=1
        mixed=jnp.zeros((block,128),jnp.float32)
        for c in range(pieces):
            mixed=mix_piece(last,c,top,mixed)
        finish(blocks-1,top,mixed)
    out_ref[...]=o32_ref[...].astype(jnp.bfloat16)

def attend(projected,chunk,bias_vec,block=512,srows=128):
    length=projected.shape[0]
    heads=bias_vec.shape[0]
    f32,b16=jnp.float32,jnp.bfloat16
    spec=lambda c: pl.BlockSpec((length,128),lambda i,c=c:(0,c))
    full=pl.BlockSpec((length,128),lambda i:(0,0))
    shape=lambda kind: jax.ShapeDtypeStruct((length,128),kind)
    return pl.pallas_call(
        functools.partial(forward_kernel,heads,block,srows,LOG2E/8),
        grid=(1,),
        in_specs=[spec(3*chunk),spec(3*chunk+1),spec(3*chunk+2),pl.BlockSpec(bias_vec.shape,lambda i:(0,0))],
        out_specs=[full]*3,
        out_shape=[shape(b16),shape(f32),shape(f32)],
        scratch_shapes=[pltpu.VMEM((srows,2*length-srows),f32),pltpu.VMEM((length,128),b16),pltpu.VMEM((length,128),b16),pltpu.VMEM((2,block,length),f32)],
        compiler_params=pltpu.CompilerParams(vmem_limit_bytes=40*MIB),
        cost_estimate=pl.CostEstimate(flops=16*heads*length*length*64,bytes_accessed=8*MIB,transcendentals=heads*length*length),
        name="attend_forward",
    )(projected,projected,projected,bias_vec)

def backward_kernel(heads,bq,bk,srows,scale,q_ref,k_ref,v_ref,do_ref,o32_ref,lse_ref,bias_ref,out_ref,diag_ref,strip,grads,ka,va,kt,qa,da,dd,qd,dk_acc,dv_acc):
    length=q_ref.shape[0]
    width=strip.shape[1]
    full_width=2*length
    lanes=lane_iota(length)
    f32,b16=jnp.float32,jnp.bfloat16
    count=length//bk
    for head in range(heads):
        fill_strip(strip,bias_ref[head:head+1,:],srows,width)
        grads[...]=jnp.zeros_like(grads)
        kd=dup_head(k_ref[...],head)
        ka[:,:128]=kd.astype(b16)
        ka[:,128:]=jnp.where(lanes<3,1.0,0.0).astype(b16)
        kt[...]=jnp.transpose(kd).astype(b16)
        va[...]=jnp.where(lanes<64,dup_head(v_ref[...],head),jnp.where(lanes<67,1.0,0.0)).astype(b16)
        qa[:,:128]=split_query(q_ref[...],head,scale)
        qa[:,128:]=columns_at(lanes,0,three_parts(-lse_ref[:,head:head+1]),0.0).astype(b16)
        qd[...]=dup_head(q_ref[...],head).astype(b16)
        upstream=dup_head(do_ref[...],head)
        dd[...]=upstream.astype(b16)
        delta=0.5*jnp.sum(upstream*dup_head(o32_ref[...],head),axis=1,keepdims=True)
        da[...]=columns_at(lanes,64,three_parts(-delta),jnp.where(lanes<64,upstream,0.0)).astype(b16)
        dk_acc[...]=jnp.zeros_like(dk_acc)
        dv_acc[...]=jnp.zeros_like(dv_acc)
        def keep(columns,rows,values):
            held=out_ref[rows,columns].astype(f32)
            out_ref[rows,columns]=(jnp.where(lane_iota(values.shape[0])<64,held,values) if head else values).astype(b16)
        def query_block(qb,carry):
            qs=pl.ds(pl.multiple_of(qb*bq,bq),bq)
            def products(kb):
                ks=slice(kb*bk,(kb+1)*bk)
                raw=lax.dot_general(ka[ks,:],qa[qs,:],NT,preferred_element_type=f32)
                up=lax.dot_general(va[ks,:],da[qs,:],NT,preferred_element_type=f32)
                return raw,up
            def consume(kb,raw,up,dq):
                ks=slice(kb*bk,(kb+1)*bk)
                probs,score_grads=[],[]
                for part in range(bk//srows):
                    start=qb*bq+(length-srows)-kb*bk-part*srows
                    rows=slice(part*srows,(part+1)*srows)
                    prob=jnp.exp2(raw[rows]+strip[:,pl.ds(pl.multiple_of(start,128),bq)])
                    grad=prob*up[rows]
                    grads[:,pl.ds(pl.multiple_of(start+srows,128),bq)]+=grad
                    probs.append(prob.astype(b16))
                    score_grads.append(grad.astype(b16))
                low=jnp.concatenate(score_grads,axis=0)
                dv_acc[ks,:]+=jnp.dot(jnp.concatenate(probs,axis=0),dd[qs,:],preferred_element_type=f32)
                dk_acc[ks,:]+=jnp.dot(low,qd[qs,:],preferred_element_type=f32)
                return dq+jnp.dot(kt[:,ks],low,preferred_element_type=f32)
            dq=jnp.zeros((128,bq),f32)
            ready=products(0)
            for kb in range(count):
                following=products(kb+1) if kb+1<count else None
                dq=consume(kb,*ready,dq)
                ready=following
            keep(slice(0,128),qs,jnp.transpose(dq)*0.125)
            return carry
        lax.fori_loop(0,length//bq,query_block,0)
        every=slice(0,length)
        keep(slice(128,256),every,dk_acc[...]*0.125)
        keep(slice(256,384),every,dv_acc[...])
        total=grads[0:8,:]
        for part in range(1,srows//8):
            total=total+pltpu.roll(grads[8*part:8*part+8,:],full_width-8*part,1)
        row=lax.broadcasted_iota(jnp.int32,(8,full_width),0)
        for part in range(1,8):
            total=jnp.where(row==part,pltpu.roll(total,full_width-part,1),total)
        diag_ref[head:head+1,:]=jnp.sum(total,axis=0,keepdims=True)

def attend_back(projected,chunk,upstream,o32,lse,bias_vec,bq=512,bk=512,srows=128):
    length=projected.shape[0]
    heads=bias_vec.shape[0]
    f32,b16=jnp.float32,jnp.bfloat16
    spec=lambda c: pl.BlockSpec((length,128),lambda i,c=c:(0,c))
    full=pl.BlockSpec((length,128),lambda i:(0,0))
    vm=lambda kind,*shape: pltpu.VMEM(shape,kind)
    return pl.pallas_call(
        functools.partial(backward_kernel,heads,bq,bk,srows,LOG2E/8),
        grid=(1,),
        in_specs=[spec(3*chunk),spec(3*chunk+1),spec(3*chunk+2),full,full,full,pl.BlockSpec(bias_vec.shape,lambda i:(0,0))],
        out_specs=[pl.BlockSpec((length,384),lambda i:(0,0)),pl.BlockSpec((8,2*length),lambda i:(0,0))],
        out_shape=[jax.ShapeDtypeStruct((length,384),b16),jax.ShapeDtypeStruct((8,2*length),f32)],
        scratch_shapes=[vm(f32,srows,2*length-srows),vm(f32,srows,2*length),vm(b16,length,256),vm(b16,length,128),vm(b16,128,length),
            vm(b16,length,256),vm(b16,length,128),vm(b16,length,128),vm(b16,length,128),vm(f32,length,128),vm(f32,length,128)],
        compiler_params=pltpu.CompilerParams(vmem_limit_bytes=48*MIB),
        cost_estimate=pl.CostEstimate(flops=40*heads*length*length*64,bytes_accessed=12*MIB,transcendentals=heads*length*length),
        name="attend_backward",
    )(projected,projected,projected,upstream,o32,lse,bias_vec)

def gelu_pair(u):
    c=0.7978845608028654
    square=u*u
    t=jnp.tanh(c*u*(1.0+0.044715*square))
    half=0.5*(1.0+t)
    return u*half,half+(0.5*c)*u*(1.0-t*t)*(1.0+0.134145*square)

def expert_kernel(experts,cap,width,hidden_width,send_ref,cot_hbm,w1_hbm,w2_hbm,router_ref,home,result_out,dw1,dw2,router_part,
                  rows,cots,grads,results,row_grads,logit_grads,act,slope,w1,w2,rows_t,
                  local_sem,cot_sem,out_sem,s_rows,r_rows,s_home,r_home):
    f32,b16=jnp.float32,jnp.bfloat16
    pairs=experts//2
    me=lax.axis_index("exp")
    seq=lax.axis_index("seq")
    pair,side=me//2,me%2
    other=1-side
    def device(offset,member):
        return lax.rem(pair+offset+pairs,pairs)*2+member
    barrier=pltpu.get_barrier_semaphore()
    for step in range(1,experts):
        pl.semaphore_signal(barrier,inc=1,device_id=(lax.rem(me+step,experts),seq),device_id_type=MESH)
    load1=pltpu.make_async_copy(w1_hbm,w1,local_sem.at[0])
    load2=pltpu.make_async_copy(w2_hbm,w2,local_sem.at[1])
    own_rows=pltpu.make_async_copy(send_ref.at[me],rows.at[side],local_sem.at[2])
    local=[load1,load2,own_rows]
    cot_loads=[pltpu.make_async_copy(cot_hbm.at[device(-j,m)],cots.at[2*j+m],cot_sem.at[2*j+m]) for j in range(pairs) for m in range(2)]
    for copy in local+cot_loads:
        copy.start()
    pl.semaphore_wait(barrier,experts-1)
    def remote(src,dst,s,r,target):
        return pltpu.make_async_remote_copy(src_ref=src,dst_ref=dst,send_sem=s,recv_sem=r,device_id=(target,seq),device_id_type=MESH)
    started=[]
    def launch(copy):
        copy.start()
        started.append(copy)
    visit=[j for step in range(1,pairs//2+1) for j in sorted({step,pairs-step})]
    launch(remote(send_ref.at[device(0,other)],rows.at[side],s_rows.at[1],r_rows.at[side],device(0,other)))
    for j in visit:
        for m in range(2):
            member=side if m==0 else other
            launch(remote(send_ref.at[device(j,member)],rows.at[2*j+side],s_rows.at[2*j+m],r_rows.at[2*j+side],device(j,member)))
    def wait_slot(landing,r,slot):
        remote(landing,landing,s_rows.at[0],r.at[slot],me).wait_recv()
    chunk=512 if hidden_width%512==0 else 128
    steps=hidden_width//chunk
    lanes=lax.broadcasted_iota(jnp.int32,(2*cap,128),1)
    onehot=jnp.where(lanes==me,1.0,0.0)
    outputs=[]
    def process(j):
        x=rows[2*j:2*j+2].reshape(2*cap,width)
        base=2*j*cap
        span=slice(base,base+2*cap)
        logits=jnp.dot(x,router_ref[...],preferred_element_type=f32)
        logits=jnp.where(lanes<experts,logits,-jnp.inf)
        raised=jnp.exp(logits-jnp.max(logits,axis=1,keepdims=True))
        gates=raised/jnp.sum(raised,axis=1,keepdims=True)
        gate=jnp.sum(gates*onehot,axis=1,keepdims=True)
        for m in range(2):
            cot_loads[2*j+m].wait()
        cot=cots[2*j:2*j+2].reshape(2*cap,width).astype(f32)
        grads[span,:]=(gate*cot).astype(b16)
        def forward(step,carry):
            cols=pl.ds(pl.multiple_of(step*chunk,chunk),chunk)
            pre=jnp.dot(x,w1[:,cols],preferred_element_type=f32)
            a,d=gelu_pair(pre)
            act[span,cols]=a.astype(b16)
            slope[span,cols]=d.astype(b16)
            return carry
        lax.fori_loop(0,steps,forward,0)
        result=jnp.dot(act[span,:],w2[...],preferred_element_type=f32).astype(b16)
        results[2*j:2*j+2]=result.reshape(2,cap,width)
        for m in range(2):
            copy=pltpu.make_async_copy(results.at[2*j+m],result_out.at[device(-j,m)],out_sem.at[2*j+m])
            copy.start()
            outputs.append(copy)
        gate_grad=jnp.sum(cots[2*j:2*j+2].reshape(2*cap,width).astype(f32)*result.astype(f32),axis=1,keepdims=True)
        logit_grad=(gates*(onehot-gate)*gate_grad).astype(b16)
        logit_grads[span,:]=logit_grad
        def backward(step,carry):
            cols=pl.ds(pl.multiple_of(step*chunk,chunk),chunk)
            up=lax.dot_general(grads[span,:],w2[cols,:],NT,preferred_element_type=f32)
            up=up.astype(b16).astype(f32)*slope[span,cols].astype(f32)
            slope[span,cols]=up.astype(b16)
            return carry
        lax.fori_loop(0,steps,backward,0)
        back=lax.dot_general(slope[span,:],w1[...],NT,preferred_element_type=f32)
        back=back+lax.dot_general(logit_grad,router_ref[...],NT,preferred_element_type=f32)
        row_grads[2*j:2*j+2]=back.astype(b16).reshape(2,cap,width)
        for m in range(2):
            member=side if m==0 else other
            if j==0 and m==0:
                copy=pltpu.make_async_copy(row_grads.at[side],home.at[me],local_sem.at[3])
                copy.start()
                outputs.append(copy)
            else:
                launch(remote(row_grads.at[2*j+member],home.at[me],s_home.at[2*j+m],r_home.at[2*j+side],device(-j,member)))
    load1.wait()
    load2.wait()
    own_rows.wait()
    wait_slot(rows.at[other],r_rows,other)
    process(0)
    for j in visit:
        for m in range(2):
            wait_slot(rows.at[2*j+m],r_rows,2*j+m)
        process(j)
    rows_t[...]=jnp.transpose(rows[...].reshape(experts*cap,width))
    router_part[...]=jnp.dot(rows_t[...],logit_grads[...],preferred_element_type=f32)
    def weight_grads(step,carry):
        cols=pl.ds(pl.multiple_of(step*chunk,chunk),chunk)
        dw1[:,cols]=jnp.dot(rows_t[...],slope[:,cols],preferred_element_type=f32).astype(b16)
        dw2[cols,:]=lax.dot_general(act[:,cols],grads[...],TN,preferred_element_type=f32).astype(b16)
        return carry
    lax.fori_loop(0,steps,weight_grads,0)
    for j in range(pairs):
        for m in range(2):
            if j:
                wait_slot(home.at[device(j,m)],r_home,2*j+m)
    wait_slot(home.at[device(0,other)],r_home,other)
    for copy in outputs:
        copy.wait()
    for copy in started:
        copy.wait_send()

def expert_layer(send,cot,w1,w2,router,cid=20):
    experts,cap,width=send.shape
    hidden_width=w1.shape[1]
    b16=jnp.bfloat16
    block=jax.ShapeDtypeStruct((experts,cap,width),b16)
    anywhere=pl.BlockSpec(memory_space=pl.ANY)
    vmem=pl.BlockSpec(memory_space=pltpu.VMEM)
    dma=lambda n: pltpu.SemaphoreType.DMA((n,))
    blocks=pltpu.VMEM((experts,cap,width),b16)
    wide=pltpu.VMEM((experts*cap,hidden_width),b16)
    return pl.pallas_call(
        functools.partial(expert_kernel,experts,cap,width,hidden_width),
        in_specs=[anywhere]*4+[vmem],
        out_specs=[anywhere,anywhere,vmem,vmem,vmem],
        out_shape=[block,block,jax.ShapeDtypeStruct(w1.shape,b16),jax.ShapeDtypeStruct(w2.shape,b16),jax.ShapeDtypeStruct((width,128),jnp.float32)],
        scratch_shapes=[blocks,blocks,pltpu.VMEM((experts*cap,width),b16),blocks,blocks,pltpu.VMEM((experts*cap,128),b16),wide,wide,
            pltpu.VMEM(w1.shape,b16),pltpu.VMEM(w2.shape,b16),pltpu.VMEM((width,experts*cap),b16),
            dma(4)]+[dma(experts)]*6,
        compiler_params=pltpu.CompilerParams(collective_id=cid,has_side_effects=True,vmem_limit_bytes=60*MIB),
        cost_estimate=pl.CostEstimate(flops=12*experts*cap*width*hidden_width,bytes_accessed=40*MIB,transcendentals=experts*cap*hidden_width),
        name="expert_layer",
    )(send,cot,w1,w2,router)

def inverse_rms(values):
    return lax.rsqrt(jnp.mean(values*values,axis=-1,keepdims=True)+EPSILON)

def matmul(left,right,dims=NN):
    return lax.dot_general(left,right,dims,preferred_element_type=jnp.float32)

def swap_parts(values,axis):
    return lax.all_to_all(values,axis,split_axis=0,concat_axis=0,tiled=True)

def reversed_ids(ids):
    flip=np.eye(128,dtype=np.float32)[::-1]
    rows=ids.shape[0]//128
    flip_rows=np.eye(rows,dtype=np.float32)[::-1]
    grid=ids.astype(jnp.bfloat16).reshape(rows,128)
    grid=matmul(grid,jnp.asarray(flip,jnp.bfloat16)).astype(jnp.bfloat16)
    return matmul(jnp.asarray(flip_rows,jnp.bfloat16),grid).reshape(-1).astype(jnp.int32)

def offset_rows(ids,table):
    hot=(ids[None,:]==jnp.arange(table.shape[0],dtype=jnp.int32)[:,None]).astype(jnp.float32)
    return lax.dot_general(table,hot,TN,precision=lax.Precision.HIGHEST)

def shards(tokens,query_weight,key_weight,value_weight,out_weight,router_weight,attn_gain,moe_gain,bias_table,expert_in,expert_out,expert_id,slot_id,bucket_id,cotangent):
    f32,b16=jnp.float32,jnp.bfloat16
    seq_count,stretch,width=tokens.shape
    seq_devs=lax.axis_size("seq")
    experts=lax.axis_size("exp")
    devices=seq_devs*experts
    length=stretch*seq_devs
    count=seq_count*stretch
    capacity=(5*count+4*experts-1)//(4*experts)
    padded_cap=(capacity+15)//16*16
    buckets,heads=bias_table.shape
    head_dim=width//heads
    groups=seq_devs//seq_count
    own_heads=heads//groups
    per_chunk=2 if own_heads%2==0 else 1
    chunks=own_heads//per_chunk
    used=per_chunk*head_dim
    span=chunks*384
    row_block=width//devices
    place=lax.axis_index("seq")
    group=place%groups
    def by_group(weight):
        cut=weight.reshape(row_block,groups,chunks,used)
        return jnp.pad(cut,((0,0),(0,0),(0,0),(0,128-used)))
    stacked=jnp.stack([by_group(w) for w in (query_weight,key_weight,value_weight)],axis=3).reshape(row_block,groups*span)
    stacked_full=lax.all_gather(stacked,BOTH,axis=0,tiled=True)
    gains=jnp.stack([attn_gain,moe_gain],axis=1)
    small=jnp.pad(jnp.concatenate([router_weight,gains],axis=1),((0,0),(0,126-experts)))
    small_full=lax.all_gather(small,BOTH,axis=0,tiled=True)
    out_full=lax.all_gather(out_weight,BOTH,axis=0,tiled=True)
    first_full=lax.all_gather(expert_in,"seq",axis=2,tiled=True)[0]
    second_full=lax.all_gather(expert_out,"seq",axis=1,tiled=True)[0]
    copies=jnp.broadcast_to(tokens[:,None],(seq_count,groups,stretch,width)).reshape(seq_devs,stretch,width)
    own_sequence=swap_parts(copies,"seq").reshape(length,width).astype(f32)
    weight=lax.dynamic_slice_in_dim(stacked_full,group*span,span,axis=1)
    router_full=small_full[:,:experts]
    router_wide=jnp.where(jnp.arange(128)[None,:]<experts,small_full,jnp.zeros((),b16))
    attn_gain_full=small_full[:,experts].astype(f32)
    moe_gain_full=small_full[:,experts+1].astype(f32)
    zero_id=jnp.zeros((1,),jnp.int32)
    backward_ids=jnp.concatenate([zero_id,bucket_id])
    forward_ids=reversed_ids(jnp.concatenate([bucket_id,zero_id]))
    own_table=lax.dynamic_slice_in_dim(bias_table,group*own_heads,own_heads,axis=1)*LOG2E
    forward_bias=offset_rows(forward_ids,own_table)
    backward_bias=offset_rows(backward_ids,own_table)
    expert_pick=expert_id.reshape(count)
    slot_pick=slot_id.reshape(count)
    slots=experts*padded_cap
    position=jnp.where(slot_pick<capacity,expert_pick*padded_cap+slot_pick,slots)
    hot=(position[None,:]==jnp.arange(slots,dtype=jnp.int32)[:,None]).astype(b16)
    cot_rows=matmul(hot,cotangent.reshape(count,width)).astype(b16).reshape(experts,padded_cap,width)
    cot_arrived=swap_parts(cot_rows,"exp")
    normed=(own_sequence*inverse_rms(own_sequence)*attn_gain_full).astype(b16)
    projected=matmul(normed,weight).astype(b16)
    saved,attended_parts=[],[]
    for chunk in range(chunks):
        bias_rows=slice(chunk*per_chunk,(chunk+1)*per_chunk)
        out,out32,log_total=attend(projected,chunk,forward_bias[bias_rows])
        saved.append((out32,log_total))
        attended_parts.append(swap_parts(out[:,:used].reshape(seq_devs,stretch,used),"seq"))
    attended=jnp.stack(attended_parts,axis=2).reshape(seq_count,groups,stretch,own_heads*head_dim)
    attended=jnp.swapaxes(attended,1,2).reshape(count,width)
    tokens_f=tokens.astype(f32).reshape(count,width)
    hidden=tokens_f+matmul(attended,out_full)
    moe_inverse=inverse_rms(hidden)
    moe_in=(hidden*moe_inverse*moe_gain_full).astype(b16)
    send_rows=matmul(hot,moe_in).astype(b16).reshape(experts,padded_cap,width)
    home,result,first_grad,second_grad,router_part=expert_layer(send_rows,cot_arrived,first_full,second_full,router_wide)
    returned=swap_parts(result,"exp").reshape(slots,width)
    expert_in_grad=lax.psum_scatter(first_grad[None],"seq",scatter_dimension=2,tiled=True).astype(f32)
    expert_out_grad=lax.psum_scatter(second_grad[None],"seq",scatter_dimension=1,tiled=True).astype(f32)
    grad_out=cotangent.astype(f32).reshape(count,width)
    moe_in_grad=matmul(hot,home.reshape(slots,width),TN)
    weighted=moe_in_grad*moe_gain_full
    moe_gain_part=jnp.sum(moe_in_grad*hidden*moe_inverse,axis=0)
    inner=jnp.mean(weighted*hidden,axis=-1,keepdims=True)
    hidden_grad=grad_out+weighted*moe_inverse-hidden*(moe_inverse*moe_inverse*moe_inverse)*inner
    branch_grad=hidden_grad.astype(b16)
    heads_grad=matmul(branch_grad,out_full,NT).astype(b16)
    outgoing=heads_grad.reshape(seq_count,stretch,groups,chunks,used)
    outgoing=jnp.transpose(outgoing,(3,0,2,1,4))
    arriving=[swap_parts(outgoing[chunk].reshape(seq_devs,stretch,used),"seq").reshape(length,used) for chunk in range(chunks)]
    out_part=matmul(attended,branch_grad,TN)
    extra=jnp.pad(jnp.concatenate([router_part[:,:experts],moe_gain_part[:,None]],axis=1),((0,0),(0,127-experts)))
    out_piece=jnp.concatenate([out_part,extra],axis=1).astype(b16).reshape(devices,row_block,width+128)
    out_sum=jnp.sum(swap_parts(out_piece,BOTH).astype(f32),axis=0)
    logits=matmul(moe_in,router_full)
    gates=jax.nn.softmax(logits,axis=-1)
    picked=(expert_pick[:,None]==jnp.arange(experts,dtype=jnp.int32)[None,:]).astype(f32)
    gate=jnp.sum(gates*picked,axis=-1)
    output=(hidden+gate[:,None]*matmul(hot,returned,TN)).astype(b16).reshape(seq_count,stretch,width)
    diagonals,token_grads,weight_sums=[],[],[]
    hot_bucket=(backward_ids[None,:]==jnp.arange(buckets,dtype=jnp.int32)[:,None]).astype(f32)
    hot_bucket=hot_bucket*(jnp.arange(length*2)>0)[None,:]
    for chunk in range(chunks):
        bias_rows=slice(chunk*per_chunk,(chunk+1)*per_chunk)
        upstream=jnp.pad(arriving[chunk],((0,0),(0,128-used)))
        grads,diagonal=attend_back(projected,chunk,upstream,*saved[chunk],backward_bias[bias_rows])
        diagonals.append(diagonal[:per_chunk])
        token_grads.append(swap_parts(grads.reshape(seq_devs,stretch,384),"seq").reshape(seq_count,groups,stretch,384))
        piece=matmul(normed,grads,TN).astype(b16).reshape(devices,row_block,384)
        if chunk==chunks-1:
            table_part=lax.dot_general(hot_bucket,jnp.concatenate(diagonals,axis=0),NT,precision=lax.Precision.HIGHEST)
            high=table_part.astype(b16)
            low=(table_part-lax.reduce_precision(table_part,8,7)).astype(b16)
            values=jnp.concatenate([high.reshape(-1),low.reshape(-1)])
            values=jnp.pad(values,(0,row_block*128-values.shape[0])).reshape(1,row_block,128)
            piece=jnp.concatenate([piece,jnp.broadcast_to(values,(devices,row_block,128))],axis=2)
        weight_sums.append(swap_parts(piece,BOTH))
    table_values=weight_sums[-1][:,:,384:].astype(f32).reshape(devices//groups,groups,row_block*128)
    table_values=jnp.sum(table_values,axis=0)[:,:2*buckets*own_heads].reshape(groups,2,buckets,own_heads)
    bias_table_grad=jnp.transpose(jnp.sum(table_values,axis=1),(1,0,2)).reshape(buckets,heads)
    normed_grad=jnp.zeros((count,width),f32)
    for chunk in range(chunks):
        for owner in range(groups):
            start=owner*span+chunk*384
            normed_grad=normed_grad+matmul(token_grads[chunk][:,owner].reshape(count,384),stacked_full[:,start:start+384],NT)
    summed=[jnp.sum(part[:,:,:384].astype(f32).reshape(devices//groups,groups,row_block,3,128)[...,:used],axis=0) for part in weight_sums]
    summed=jnp.stack(summed,axis=1)
    weight_grads=jnp.transpose(summed,(3,2,0,1,4)).reshape(3,row_block,width)
    own_weights=jnp.stack([query_weight,key_weight,value_weight]).astype(f32)
    attn_gain_grad=jnp.sum(weight_grads*own_weights,axis=(0,2))/attn_gain.astype(f32)
    tokens_inverse=inverse_rms(tokens_f)
    weighted=normed_grad*attn_gain_full
    inner=jnp.mean(weighted*tokens_f,axis=-1,keepdims=True)
    input_grad=hidden_grad+weighted*tokens_inverse-tokens_f*(tokens_inverse*tokens_inverse*tokens_inverse)*inner
    return (
        output,
        input_grad.reshape(seq_count,stretch,width),
        weight_grads[0],weight_grads[1],weight_grads[2],
        out_sum[:,:width],
        out_sum[:,width:width+experts],
        attn_gain_grad,
        out_sum[:,width+experts],
        bias_table_grad,
        expert_in_grad,
        expert_out_grad,
    )

def solution(mesh):
    tokens=P("exp","seq",None)
    rows=P(BOTH,None)
    return jax.shard_map(
        shards,
        mesh=mesh,
        in_specs=(tokens,rows,rows,rows,rows,rows,P(BOTH),P(BOTH),P(),P("exp",None,"seq"),P("exp","seq",None),P("exp","seq"),P("exp","seq"),P(),tokens),
        out_specs=(tokens,tokens,rows,rows,rows,rows,rows,P(BOTH),P(BOTH),P(),P("exp",None,"seq"),P("exp","seq",None)),
        check_vma=False,
    )
```

```python
import functools
import jax
import jax.numpy as jnp
import numpy as np
from jax import lax
from jax.experimental import pallas as pl
from jax.experimental.pallas import tpu as pltpu
from jax.sharding import PartitionSpec as P
NT=(((1,),(1,)),((),()))
NN=(((1,),(0,)),((),()))
LOG2E=1.4426950408889634
MIB=1024*1024
TN=(((0,),(0,)),((),()))
MESH=pl.DeviceIdType.MESH
EPSILON=1e-06
BOTH=("exp","seq")

def lane_iota(rows):
    return lax.broadcasted_iota(jnp.int32,(rows,128),1)

def dup_head(values,head):
    values=values.astype(jnp.float32)
    turned=pltpu.roll(values,64,1)
    low=lane_iota(values.shape[0])<64
    return jnp.where(low,values,turned) if head==0 else jnp.where(low,turned,values)

def three_parts(column):
    first=column.astype(jnp.bfloat16).astype(jnp.float32)
    rest=column-first
    second=rest.astype(jnp.bfloat16).astype(jnp.float32)
    return first,second,rest-second

def columns_at(lanes,start,parts,other):
    out=other
    for place,part in enumerate(parts):
        out=jnp.where(lanes==start+place,part,out)
    return out

def split_query(query,head,scale):
    both=dup_head(query,head)*scale
    high=both.astype(jnp.bfloat16).astype(jnp.float32)
    return jnp.where(lane_iota(query.shape[0])<64,high,both-high).astype(jnp.bfloat16)

def fill_strip(strip,vector,rows,width):
    full=width+rows
    step=8
    spread=jnp.broadcast_to(vector,(rows,full))
    turned=pltpu.roll(spread,0,1,stride=1,stride_axis=0)
    strip[...]=turned[:,rows:]


def head_column(values,index):
    return jnp.sum(jnp.where(lane_iota(values.shape[0])==index,values,0.0),axis=1,keepdims=True)

def remote(src,dst,sent,received,target):
    return pltpu.make_async_remote_copy(src_ref=src,dst_ref=dst,send_sem=sent,recv_sem=received,device_id=target,device_id_type=MESH)

def loop(first,last,body):
    def step(i,carry):
        body(i)
        return carry
    lax.fori_loop(first,last,step,0)

def forward_kernel(plan,block,srows,scale,proj_ref,bias_ref,cot_ref,att_out,o32_ref,lse_ref,cot_out,strip,kd,va,scr,outs,s_cot,r_cot,s_att,r_att,local_sem):
    experts,seq_devs,seq_count,stretch,heads,chunks=plan
    length=stretch*seq_devs
    groups=seq_devs//seq_count
    f32,b16=jnp.float32,jnp.bfloat16
    me,place=lax.axis_index("exp"),lax.axis_index("seq")
    sequence,group=place//groups,place%groups
    barrier=pltpu.get_barrier_semaphore()
    loop(1,experts,lambda i: pl.semaphore_signal(barrier,inc=1,device_id=(lax.rem(me+i,experts),place),device_id_type=MESH))
    loop(1,seq_devs,lambda i: pl.semaphore_signal(barrier,inc=1,device_id=(me,lax.rem(place+i,seq_devs)),device_id_type=MESH))
    own_cot=pltpu.make_async_copy(cot_ref.at[me],cot_out.at[me],local_sem.at[0])
    own_cot.start()
    pl.semaphore_wait(barrier,experts+seq_devs-2)
    def send_cot(i):
        target=lax.rem(me+i,experts)
        return remote(cot_ref.at[target],cot_out.at[me],s_cot.at[i],r_cot.at[i],(target,place))
    loop(1,experts,lambda i: send_cot(i).start())
    def lanes_of(owner_group,c,size):
        return pl.ds(pl.multiple_of((owner_group*chunks+c)*size,128),size)
    def send_att(c,i):
        target=lax.rem(place+i,seq_devs)
        rows=pl.ds(pl.multiple_of(target*stretch,128),stretch)
        return remote(outs.at[c,rows],att_out.at[sequence,:,lanes_of(group,c,128)],s_att.at[c,i],r_att.at[c,i],(me,target))
    def own_att(c):
        rows=pl.ds(pl.multiple_of(place*stretch,128),stretch)
        return pltpu.make_async_copy(outs.at[c,rows],att_out.at[sequence,:,lanes_of(group,c,128)],local_sem.at[1+c])
    width=strip.shape[1]
    wide=256
    blocks=length//block
    pieces=length//wide
    lanes=lane_iota(length)
    block_lanes=lane_iota(block)
    lse_ref[...]=jnp.zeros_like(lse_ref)
    def attend_head(c,head):
        index=c*heads+head
        base=c*384
        def columns(which):
            return pl.ds(pl.multiple_of(base+which*128,128),128)
        own=pl.ds(pl.multiple_of(c*128,128),128)
        fill_strip(strip,bias_ref[pl.ds(index,1),:],srows,width)
        kd[...]=dup_head(proj_ref[:,columns(1)],head).astype(b16)
        va[...]=jnp.where(lanes<64,dup_head(proj_ref[:,columns(2)],head),jnp.where(lanes==64,1.0,0.0)).astype(b16)
        def rows_of(step):
            return pl.ds(pl.multiple_of(step*block,block),block)
        def score_piece(step,qa,p,slot,top):
            raw=lax.dot_general(qa,kd[p*wide:(p+1)*wide,:],NT,preferred_element_type=f32)
            parts=[]
            for part in range(block//srows):
                start=pl.multiple_of(length-srows-step*block-part*srows+p*wide,128)
                parts.append(raw[part*srows:(part+1)*srows]+strip[:,pl.ds(start,wide)])
            scores=jnp.concatenate(parts,axis=0)
            scr[slot,:,p*wide:(p+1)*wide]=scores
            for j in range(wide//128):
                top=jnp.maximum(top,scores[:,j*128:(j+1)*128])
            return top
        def mix_piece(slot,p,top,total):
            weights=jnp.exp2(scr[slot,:,p*wide:(p+1)*wide]-top).astype(b16)
            return total+jnp.dot(weights,va[p*wide:(p+1)*wide,:],preferred_element_type=f32)
        def finish(step,top,mixed):
            rows=rows_of(step)
            total=mixed[:,64:65]
            result=mixed/total
            lse_ref[rows,:]=jnp.where(block_lanes==index,top+jnp.log2(total),lse_ref[rows,:])
            if head==0:
                o32_ref[rows,own]=result
            else:
                o32_ref[rows,own]=jnp.where(block_lanes<64,o32_ref[rows,own],pltpu.roll(result,64,1))
        def advance(step,slot,top):
            mixing=top is not None
            qa=split_query(proj_ref[rows_of(step),columns(0)],head,scale)
            new=jnp.full((block,128),-jnp.inf,f32)
            mixed=jnp.zeros((block,128),f32)
            for p in range(pieces):
                new=score_piece(step,qa,p,slot,new)
                if mixing:
                    mixed=mix_piece(1-slot,p,top,mixed)
            if mixing:
                finish(step-1,top,mixed)
            return jnp.max(new,axis=1,keepdims=True)
        def body(i,top):
            top=advance(2*i+1,1,top)
            return advance(2*i+2,0,top)
        top=advance(0,0,None)
        top=lax.fori_loop(0,(blocks-1)//2,body,top)
        last=0
        if blocks%2==0:
            top=advance(blocks-1,1,top)
            last=1
        mixed=jnp.zeros((block,128),f32)
        for p in range(pieces):
            mixed=mix_piece(last,p,top,mixed)
        finish(blocks-1,top,mixed)
    def one_chunk(c):
        for head in range(heads):
            attend_head(c,head)
        outs[c]=o32_ref[:,pl.ds(pl.multiple_of(c*128,128),128)].astype(b16)
        loop(1,seq_devs,lambda i: send_att(c,i).start())
        own_att(c).start()
    loop(0,chunks,one_chunk)
    def land_att(c,i):
        source=lax.rem(place-i+seq_devs,seq_devs)
        landing=att_out.at[source//groups,:,lanes_of(source%groups,c,128)]
        remote(landing,landing,s_att.at[c,i],r_att.at[c,i],(me,place)).wait_recv()
    def finish_chunk(c):
        own_att(c).wait()
        loop(1,seq_devs,lambda i: land_att(c,i))
        loop(1,seq_devs,lambda i: send_att(c,i).wait_send())
    loop(0,chunks,finish_chunk)
    def land_cot(i):
        landing=cot_out.at[lax.rem(me-i+experts,experts)]
        remote(landing,landing,s_cot.at[i],r_cot.at[i],(me,place)).wait_recv()
    loop(1,experts,land_cot)
    loop(1,experts,lambda i: send_cot(i).wait_send())
    own_cot.wait()

def attend(plan,projected,bias_vec,cot_rows,block=512,srows=128):
    experts,seq_devs,seq_count,stretch,heads,chunks=plan
    length=stretch*seq_devs
    groups=seq_devs//seq_count
    f32,b16=jnp.float32,jnp.bfloat16
    vmem=pl.BlockSpec(memory_space=pltpu.VMEM)
    anywhere=pl.BlockSpec(memory_space=pl.ANY)
    dma=lambda *shape: pltpu.SemaphoreType.DMA(shape)
    return pl.pallas_call(
        functools.partial(forward_kernel,plan,block,srows,LOG2E/8),
        in_specs=[vmem,vmem,anywhere],
        out_specs=[anywhere,vmem,vmem,anywhere],
        out_shape=[jax.ShapeDtypeStruct((seq_count,stretch,groups*chunks*128),b16),jax.ShapeDtypeStruct((length,chunks*128),f32),jax.ShapeDtypeStruct((length,128),f32),jax.ShapeDtypeStruct(cot_rows.shape,b16)],
        scratch_shapes=[pltpu.VMEM((srows,2*length-srows),f32),pltpu.VMEM((length,128),b16),pltpu.VMEM((length,128),b16),pltpu.VMEM((2,block,length),f32),pltpu.VMEM((chunks,length,128),b16),
            dma(experts),dma(experts),dma(chunks,seq_devs),dma(chunks,seq_devs),dma(1+chunks)],
        compiler_params=pltpu.CompilerParams(collective_id=1,has_side_effects=True,vmem_limit_bytes=48*MIB),
        cost_estimate=pl.CostEstimate(flops=16*heads*chunks*length*length*64,bytes_accessed=16*MIB,transcendentals=heads*chunks*length*length),
        name="attend_forward",
    )(projected,bias_vec,cot_rows)

def backward_kernel(plan,inside,bq,bk,srows,scale,proj_ref,o32_ref,lse_ref,bias_ref,normed_t,bucket_ref,up_ref,res_ref,piece_ref,
                    grad_out,ret_out,piece_out,weight_out,table_out,
                    strip,grads,ka,va,kt,qa,da,dd,qd,dk_acc,dv_acc,ups,outs,weight_parts,diag,table,
                    s_up,r_up,s_res,r_res,s_piece,r_piece,s_grad,r_grad,s_weight,r_weight,s_table,r_table,local_sem,own_sem):
    experts,seq_devs,seq_count,stretch,heads,chunks=plan
    length=stretch*seq_devs
    groups=seq_devs//seq_count
    devices=experts*seq_devs
    f32,b16=jnp.float32,jnp.bfloat16
    me,place=lax.axis_index("exp"),lax.axis_index("seq")
    sequence,group=place//groups,place%groups
    rank=me*seq_devs+place
    def other(i):
        target=lax.rem(rank+i,devices)
        return target,(target//seq_devs,target%seq_devs)
    barrier=pltpu.get_barrier_semaphore()
    loop(1,devices,lambda i: pl.semaphore_signal(barrier,inc=1,device_id=other(i)[1],device_id_type=MESH))
    def lanes_of(owner_group,c,size):
        return pl.ds(pl.multiple_of((owner_group*chunks+c)*size,128),size)
    def rows_of(owner):
        return pl.ds(pl.multiple_of(owner*stretch,128),stretch)
    def send_up(c,i):
        target=lax.rem(place+i,seq_devs)
        return remote(up_ref.at[target//groups,:,lanes_of(target%groups,c,128)],ups.at[c,rows_of(place)],s_up.at[c,i],r_up.at[c,i],(me,target))
    def own_up(c):
        return pltpu.make_async_copy(up_ref.at[sequence,:,lanes_of(group,c,128)],ups.at[c,rows_of(place)],local_sem.at[0,c])
    def send_res(i):
        target=lax.rem(me+i,experts)
        return remote(res_ref.at[target],ret_out.at[me],s_res.at[i],r_res.at[i],(target,place))
    def send_piece(i):
        target,where=other(i)
        return remote(piece_ref.at[target],piece_out.at[rank],s_piece.at[i],r_piece.at[i],where)
    def send_grad(c,i):
        target=lax.rem(place+i,seq_devs)
        return remote(outs.at[c,rows_of(target)],grad_out.at[sequence,:,lanes_of(group,c,384)],s_grad.at[c,i],r_grad.at[c,i],(me,target))
    def own_grad(c):
        return pltpu.make_async_copy(outs.at[c,rows_of(place)],grad_out.at[sequence,:,lanes_of(group,c,384)],local_sem.at[1,c])
    def send_weight(c,i):
        target,where=other(i)
        return remote(weight_parts.at[c,target],weight_out.at[c,rank],s_weight.at[c,i],r_weight.at[c,i],where)
    def own_weight(c):
        return pltpu.make_async_copy(weight_parts.at[c,rank],weight_out.at[c,rank],local_sem.at[2,c])
    def send_table(i):
        return remote(table,table_out.at[rank],s_table.at[i],r_table.at[i],other(i)[1])
    own_table=pltpu.make_async_copy(table,table_out.at[rank],own_sem.at[0])
    own_res=pltpu.make_async_copy(res_ref.at[me],ret_out.at[me],own_sem.at[1])
    own_piece=pltpu.make_async_copy(piece_ref.at[rank],piece_out.at[rank],own_sem.at[2])
    def landed(landing,received):
        remote(landing,landing,own_sem.at[3],received,(me,place)).wait_recv()
    own_res.start()
    own_piece.start()
    loop(0,chunks,lambda c: own_up(c).start())
    pl.semaphore_wait(barrier,devices-1)
    loop(0,chunks,lambda c: loop(1,seq_devs,lambda i: send_up(c,i).start()))
    width=strip.shape[1]
    full_width=2*length
    lanes=lane_iota(length)
    count=length//bk
    if inside:
        weight_parts[...]=jnp.zeros_like(weight_parts)
    diag[...]=jnp.zeros_like(diag)
    def head_back(c,head):
        index=c*heads+head
        def columns(which):
            return pl.ds(pl.multiple_of(c*384+which*128,128),128)
        query,key,value=[proj_ref[:,columns(which)] for which in range(3)]
        fill_strip(strip,bias_ref[pl.ds(index,1),:],srows,width)
        grads[...]=jnp.zeros_like(grads)
        kd=dup_head(key,head)
        ka[:,:128]=kd.astype(b16)
        ka[:,128:]=jnp.where(lanes<3,1.0,0.0).astype(b16)
        kt[...]=jnp.transpose(kd).astype(b16)
        va[...]=jnp.where(lanes<64,dup_head(value,head),jnp.where(lanes<67,1.0,0.0)).astype(b16)
        qa[:,:128]=split_query(query,head,scale)
        qa[:,128:]=columns_at(lanes,0,three_parts(-head_column(lse_ref[...],index)),0.0).astype(b16)
        qd[...]=dup_head(query,head).astype(b16)
        upstream=dup_head(ups[c],head)
        dd[...]=upstream.astype(b16)
        delta=0.5*jnp.sum(upstream*dup_head(o32_ref[:,pl.ds(pl.multiple_of(c*128,128),128)],head),axis=1,keepdims=True)
        da[...]=columns_at(lanes,64,three_parts(-delta),jnp.where(lanes<64,upstream,0.0)).astype(b16)
        dk_acc[...]=jnp.zeros_like(dk_acc)
        dv_acc[...]=jnp.zeros_like(dv_acc)
        def keep(part,rows,values):
            if head:
                values=jnp.where(lane_iota(values.shape[0])<64,outs[c,rows,part].astype(f32),values)
            outs[c,rows,part]=values.astype(b16)
        def query_block(qb):
            qs=pl.ds(pl.multiple_of(qb*bq,bq),bq)
            def products(kb):
                ks=slice(kb*bk,(kb+1)*bk)
                raw=lax.dot_general(ka[ks,:],qa[qs,:],NT,preferred_element_type=f32)
                up=lax.dot_general(va[ks,:],da[qs,:],NT,preferred_element_type=f32)
                return raw,up
            def consume(kb,raw,up,dq):
                ks=slice(kb*bk,(kb+1)*bk)
                probs,score_grads=[],[]
                for part in range(bk//srows):
                    start=qb*bq+(length-srows)-kb*bk-part*srows
                    rows=slice(part*srows,(part+1)*srows)
                    prob=jnp.exp2(raw[rows]+strip[:,pl.ds(pl.multiple_of(start,128),bq)])
                    grad=prob*up[rows]
                    grads[:,pl.ds(pl.multiple_of(start+srows,128),bq)]+=grad
                    probs.append(prob.astype(b16))
                    score_grads.append(grad.astype(b16))
                low=jnp.concatenate(score_grads,axis=0)
                dv_acc[ks,:]+=jnp.dot(jnp.concatenate(probs,axis=0),dd[qs,:],preferred_element_type=f32)
                dk_acc[ks,:]+=jnp.dot(low,qd[qs,:],preferred_element_type=f32)
                return dq+jnp.dot(kt[:,ks],low,preferred_element_type=f32)
            dq=jnp.zeros((128,bq),f32)
            ready=products(0)
            for kb in range(count):
                following=products(kb+1) if kb+1<count else None
                dq=consume(kb,*ready,dq)
                ready=following
            keep(slice(0,128),qs,jnp.transpose(dq)*0.125)
        loop(0,length//bq,query_block)
        every=slice(0,length)
        keep(slice(128,256),every,dk_acc[...]*0.125)
        keep(slice(256,384),every,dv_acc[...])
        total=grads[0:8,:]
        for part in range(1,srows//8):
            total=total+pltpu.roll(grads[8*part:8*part+8,:],full_width-8*part,1)
        row=lax.broadcasted_iota(jnp.int32,(8,full_width),0)
        for part in range(1,8):
            total=jnp.where(row==part,pltpu.roll(total,full_width-part,1),total)
        diag[pl.ds(index,1),:]=jnp.sum(total,axis=0,keepdims=True)
    def one_chunk(c):
        loop(1,seq_devs,lambda i: landed(ups.at[c,rows_of(lax.rem(place-i+seq_devs,seq_devs))],r_up.at[c,i]))
        own_up(c).wait()
        @pl.when(c==0)
        def _():
            loop(1,experts,lambda i: send_res(i).start())
            loop(1,devices,lambda i: send_piece(i).start())
        for head in range(heads):
            head_back(c,head)
        loop(1,seq_devs,lambda i: send_grad(c,i).start())
        own_grad(c).start()
        if inside:
            part=jnp.dot(normed_t[...],outs[c],preferred_element_type=f32)
            block=normed_t.shape[0]//devices
            weight_parts[c,:,:block,:]=part.reshape(devices,block,384).astype(b16)
            loop(1,devices,lambda i: send_weight(c,i).start())
            own_weight(c).start()
    loop(0,chunks,one_chunk)
    table[...]=lax.dot_general(bucket_ref[...],diag[...],NT,precision=lax.Precision.HIGHEST,preferred_element_type=f32)
    loop(1,devices,lambda i: send_table(i).start())
    own_table.start()
    def back(i,total):
        return lax.rem(i[0]-i[1]+total,total)
    def finish_chunk(c):
        def grad_landed(i):
            source=lax.rem(place-i+seq_devs,seq_devs)
            landed(grad_out.at[source//groups,:,lanes_of(source%groups,c,384)],r_grad.at[c,i])
            send_grad(c,i).wait_send()
            send_up(c,i).wait_send()
        loop(1,seq_devs,grad_landed)
        own_grad(c).wait()
        if inside:
            def weight_landed(i):
                landed(weight_out.at[c,lax.rem(rank-i+devices,devices)],r_weight.at[c,i])
                send_weight(c,i).wait_send()
            loop(1,devices,weight_landed)
            own_weight(c).wait()
    loop(0,chunks,finish_chunk)
    def res_landed(i):
        landed(ret_out.at[lax.rem(me-i+experts,experts)],r_res.at[i])
        send_res(i).wait_send()
    loop(1,experts,res_landed)
    def piece_landed(i):
        source=lax.rem(rank-i+devices,devices)
        landed(piece_out.at[source],r_piece.at[i])
        send_piece(i).wait_send()
        landed(table_out.at[source],r_table.at[i])
        send_table(i).wait_send()
    loop(1,devices,piece_landed)
    own_res.wait()
    own_piece.wait()
    own_table.wait()

def attend_back(plan,projected,o32,lse,bias_vec,normed_t,buckets,upstream,result,piece,bq=512,bk=512,srows=128):
    experts,seq_devs,seq_count,stretch,heads,chunks=plan
    length=stretch*seq_devs
    groups=seq_devs//seq_count
    devices=experts*seq_devs
    block=normed_t.shape[0]//devices
    inside=block%8==0
    rows=(block+15)//16*16
    f32,b16=jnp.float32,jnp.bfloat16
    vm=lambda kind,*shape: pltpu.VMEM(shape,kind)
    vmem=pl.BlockSpec(memory_space=pltpu.VMEM)
    anywhere=pl.BlockSpec(memory_space=pl.ANY)
    dma=lambda *shape: pltpu.SemaphoreType.DMA(shape)
    shape=lambda kind,*dims: jax.ShapeDtypeStruct(dims,kind)
    weight_shape=(chunks,devices,rows,384) if inside else (1,1,16,128)
    return pl.pallas_call(
        functools.partial(backward_kernel,plan,inside,bq,bk,srows,LOG2E/8),
        in_specs=[vmem]*6+[anywhere]*3,
        out_specs=[anywhere]*5,
        out_shape=[shape(b16,seq_count,stretch,groups*chunks*384),shape(b16,*result.shape),shape(b16,*piece.shape),shape(b16,*weight_shape),shape(f32,devices,buckets.shape[0],diag_rows(plan))],
        scratch_shapes=[vm(f32,srows,2*length-srows),vm(f32,srows,2*length),vm(b16,length,256),vm(b16,length,128),vm(b16,128,length),
            vm(b16,length,256),vm(b16,length,128),vm(b16,length,128),vm(b16,length,128),vm(f32,length,128),vm(f32,length,128),
            vm(b16,chunks,length,128),vm(b16,chunks,length,384),vm(b16,*weight_shape),vm(f32,diag_rows(plan),2*length),vm(f32,buckets.shape[0],diag_rows(plan)),
            dma(chunks,seq_devs),dma(chunks,seq_devs),dma(experts),dma(experts),dma(devices),dma(devices),dma(chunks,seq_devs),dma(chunks,seq_devs),
            dma(chunks,devices),dma(chunks,devices),dma(devices),dma(devices),dma(3,chunks),dma(4)],
        compiler_params=pltpu.CompilerParams(collective_id=2,has_side_effects=True,vmem_limit_bytes=58*MIB),
        cost_estimate=pl.CostEstimate(flops=40*heads*chunks*length*length*64,bytes_accessed=24*MIB,transcendentals=heads*chunks*length*length),
        name="attend_backward",
    )(projected,o32,lse,bias_vec,normed_t,buckets,upstream,result,piece)

def diag_rows(plan):
    return 128

def gelu_pair(u):
    c=0.7978845608028654
    square=u*u
    t=jnp.tanh(c*u*(1.0+0.044715*square))
    half=0.5*(1.0+t)
    return u*half,half+(0.5*c)*u*(1.0-t*t)*(1.0+0.134145*square)

def expert_kernel(experts,cap,width,hidden_width,send_ref,cot_hbm,w1_hbm,w2_hbm,router_ref,home,result_out,dw1,dw2,router_part,
                  rows,cots,grads,results,row_grads,logit_grads,act,slope,w1,w2,rows_t,
                  local_sem,cot_sem,out_sem,s_rows,r_rows,s_home,r_home):
    f32,b16=jnp.float32,jnp.bfloat16
    pairs=experts//2
    me=lax.axis_index("exp")
    seq=lax.axis_index("seq")
    pair,side=me//2,me%2
    other=1-side
    def device(offset,member):
        return lax.rem(pair+offset+pairs,pairs)*2+member
    barrier=pltpu.get_barrier_semaphore()
    for step in range(1,experts):
        pl.semaphore_signal(barrier,inc=1,device_id=(lax.rem(me+step,experts),seq),device_id_type=MESH)
    load1=pltpu.make_async_copy(w1_hbm,w1,local_sem.at[0])
    load2=pltpu.make_async_copy(w2_hbm,w2,local_sem.at[1])
    own_rows=pltpu.make_async_copy(send_ref.at[me],rows.at[side],local_sem.at[2])
    local=[load1,load2,own_rows]
    cot_loads=[pltpu.make_async_copy(cot_hbm.at[device(-j,m)],cots.at[2*j+m],cot_sem.at[2*j+m]) for j in range(pairs) for m in range(2)]
    for copy in local+cot_loads:
        copy.start()
    pl.semaphore_wait(barrier,experts-1)
    def remote(src,dst,s,r,target):
        return pltpu.make_async_remote_copy(src_ref=src,dst_ref=dst,send_sem=s,recv_sem=r,device_id=(target,seq),device_id_type=MESH)
    started=[]
    def launch(copy):
        copy.start()
        started.append(copy)
    visit=[j for step in range(1,pairs//2+1) for j in sorted({step,pairs-step})]
    launch(remote(send_ref.at[device(0,other)],rows.at[side],s_rows.at[1],r_rows.at[side],device(0,other)))
    for j in visit:
        for m in range(2):
            member=side if m==0 else other
            launch(remote(send_ref.at[device(j,member)],rows.at[2*j+side],s_rows.at[2*j+m],r_rows.at[2*j+side],device(j,member)))
    def wait_slot(landing,r,slot):
        remote(landing,landing,s_rows.at[0],r.at[slot],me).wait_recv()
    chunk=512 if hidden_width%512==0 else 128
    steps=hidden_width//chunk
    lanes=lax.broadcasted_iota(jnp.int32,(2*cap,128),1)
    onehot=jnp.where(lanes==me,1.0,0.0)
    outputs=[]
    def process(j):
        x=rows[2*j:2*j+2].reshape(2*cap,width)
        base=2*j*cap
        span=slice(base,base+2*cap)
        logits=jnp.dot(x,router_ref[...],preferred_element_type=f32)
        logits=jnp.where(lanes<experts,logits,-jnp.inf)
        raised=jnp.exp(logits-jnp.max(logits,axis=1,keepdims=True))
        gates=raised/jnp.sum(raised,axis=1,keepdims=True)
        gate=jnp.sum(gates*onehot,axis=1,keepdims=True)
        for m in range(2):
            cot_loads[2*j+m].wait()
        cot=cots[2*j:2*j+2].reshape(2*cap,width).astype(f32)
        grads[span,:]=(gate*cot).astype(b16)
        def forward(step,carry):
            cols=pl.ds(pl.multiple_of(step*chunk,chunk),chunk)
            pre=jnp.dot(x,w1[:,cols],preferred_element_type=f32)
            a,d=gelu_pair(pre)
            act[span,cols]=a.astype(b16)
            slope[span,cols]=d.astype(b16)
            return carry
        lax.fori_loop(0,steps,forward,0)
        result=jnp.dot(act[span,:],w2[...],preferred_element_type=f32).astype(b16)
        results[2*j:2*j+2]=result.reshape(2,cap,width)
        for m in range(2):
            copy=pltpu.make_async_copy(results.at[2*j+m],result_out.at[device(-j,m)],out_sem.at[2*j+m])
            copy.start()
            outputs.append(copy)
        gate_grad=jnp.sum(cots[2*j:2*j+2].reshape(2*cap,width).astype(f32)*result.astype(f32),axis=1,keepdims=True)
        logit_grad=(gates*(onehot-gate)*gate_grad).astype(b16)
        logit_grads[span,:]=logit_grad
        def backward(step,carry):
            cols=pl.ds(pl.multiple_of(step*chunk,chunk),chunk)
            up=lax.dot_general(grads[span,:],w2[cols,:],NT,preferred_element_type=f32)
            up=up.astype(b16).astype(f32)*slope[span,cols].astype(f32)
            slope[span,cols]=up.astype(b16)
            return carry
        lax.fori_loop(0,steps,backward,0)
        back=lax.dot_general(slope[span,:],w1[...],NT,preferred_element_type=f32)
        back=back+lax.dot_general(logit_grad,router_ref[...],NT,preferred_element_type=f32)
        row_grads[2*j:2*j+2]=back.astype(b16).reshape(2,cap,width)
        for m in range(2):
            member=side if m==0 else other
            if j==0 and m==0:
                copy=pltpu.make_async_copy(row_grads.at[side],home.at[me],local_sem.at[3])
                copy.start()
                outputs.append(copy)
            else:
                launch(remote(row_grads.at[2*j+member],home.at[me],s_home.at[2*j+m],r_home.at[2*j+side],device(-j,member)))
    load1.wait()
    load2.wait()
    own_rows.wait()
    wait_slot(rows.at[other],r_rows,other)
    process(0)
    for j in visit:
        for m in range(2):
            wait_slot(rows.at[2*j+m],r_rows,2*j+m)
        process(j)
    rows_t[...]=jnp.transpose(rows[...].reshape(experts*cap,width))
    router_part[...]=jnp.dot(rows_t[...],logit_grads[...],preferred_element_type=f32)
    def weight_grads(step,carry):
        cols=pl.ds(pl.multiple_of(step*chunk,chunk),chunk)
        dw1[:,cols]=jnp.dot(rows_t[...],slope[:,cols],preferred_element_type=f32).astype(b16)
        dw2[cols,:]=lax.dot_general(act[:,cols],grads[...],TN,preferred_element_type=f32).astype(b16)
        return carry
    lax.fori_loop(0,steps,weight_grads,0)
    for j in range(pairs):
        for m in range(2):
            if j:
                wait_slot(home.at[device(j,m)],r_home,2*j+m)
    wait_slot(home.at[device(0,other)],r_home,other)
    for copy in outputs:
        copy.wait()
    for copy in started:
        copy.wait_send()

def expert_layer(send,cot,w1,w2,router,cid=20):
    experts,cap,width=send.shape
    hidden_width=w1.shape[1]
    b16=jnp.bfloat16
    block=jax.ShapeDtypeStruct((experts,cap,width),b16)
    anywhere=pl.BlockSpec(memory_space=pl.ANY)
    vmem=pl.BlockSpec(memory_space=pltpu.VMEM)
    dma=lambda n: pltpu.SemaphoreType.DMA((n,))
    blocks=pltpu.VMEM((experts,cap,width),b16)
    wide=pltpu.VMEM((experts*cap,hidden_width),b16)
    return pl.pallas_call(
        functools.partial(expert_kernel,experts,cap,width,hidden_width),
        in_specs=[anywhere]*4+[vmem],
        out_specs=[anywhere,anywhere,vmem,vmem,vmem],
        out_shape=[block,block,jax.ShapeDtypeStruct(w1.shape,b16),jax.ShapeDtypeStruct(w2.shape,b16),jax.ShapeDtypeStruct((width,128),jnp.float32)],
        scratch_shapes=[blocks,blocks,pltpu.VMEM((experts*cap,width),b16),blocks,blocks,pltpu.VMEM((experts*cap,128),b16),wide,wide,
            pltpu.VMEM(w1.shape,b16),pltpu.VMEM(w2.shape,b16),pltpu.VMEM((width,experts*cap),b16),
            dma(4)]+[dma(experts)]*6,
        compiler_params=pltpu.CompilerParams(collective_id=cid,has_side_effects=True,vmem_limit_bytes=60*MIB),
        cost_estimate=pl.CostEstimate(flops=12*experts*cap*width*hidden_width,bytes_accessed=40*MIB,transcendentals=experts*cap*hidden_width),
        name="expert_layer",
    )(send,cot,w1,w2,router)

def inverse_rms(values):
    return lax.rsqrt(jnp.mean(values*values,axis=-1,keepdims=True)+EPSILON)

def matmul(left,right,dims=NN):
    return lax.dot_general(left,right,dims,preferred_element_type=jnp.float32)

def swap_parts(values,axis):
    return lax.all_to_all(values,axis,split_axis=0,concat_axis=0,tiled=True)

def reversed_ids(ids):
    flip=np.eye(128,dtype=np.float32)[::-1]
    rows=ids.shape[0]//128
    flip_rows=np.eye(rows,dtype=np.float32)[::-1]
    grid=ids.astype(jnp.bfloat16).reshape(rows,128)
    grid=matmul(grid,jnp.asarray(flip,jnp.bfloat16)).astype(jnp.bfloat16)
    return matmul(jnp.asarray(flip_rows,jnp.bfloat16),grid).reshape(-1).astype(jnp.int32)

def offset_rows(ids,table):
    hot=(ids[None,:]==jnp.arange(table.shape[0],dtype=jnp.int32)[:,None]).astype(jnp.float32)
    return lax.dot_general(table,hot,TN,precision=lax.Precision.HIGHEST)

def shards(tokens,query_weight,key_weight,value_weight,out_weight,router_weight,attn_gain,moe_gain,bias_table,expert_in,expert_out,expert_id,slot_id,bucket_id,cotangent):
    f32,b16=jnp.float32,jnp.bfloat16
    seq_count,stretch,width=tokens.shape
    seq_devs=lax.axis_size("seq")
    experts=lax.axis_size("exp")
    devices=seq_devs*experts
    length=stretch*seq_devs
    count=seq_count*stretch
    capacity=(5*count+4*experts-1)//(4*experts)
    padded_cap=(capacity+15)//16*16
    buckets,heads=bias_table.shape
    head_dim=width//heads
    groups=seq_devs//seq_count
    own_heads=heads//groups
    per_chunk=2 if own_heads%2==0 else 1
    chunks=own_heads//per_chunk
    used=per_chunk*head_dim
    span=chunks*384
    heads_width=groups*chunks*128
    row_block=width//devices
    place=lax.axis_index("seq")
    group=place%groups
    def by_group(weight):
        cut=weight.reshape(row_block,groups,chunks,used)
        return jnp.pad(cut,((0,0),(0,0),(0,0),(0,128-used)))
    stacked=jnp.stack([by_group(w) for w in (query_weight,key_weight,value_weight)],axis=3).reshape(row_block,groups*span)
    stacked_full=lax.all_gather(stacked,BOTH,axis=0,tiled=True)
    gains=jnp.stack([attn_gain,moe_gain],axis=1)
    small=jnp.pad(jnp.concatenate([router_weight,gains],axis=1),((0,0),(0,126-experts)))
    small_full=lax.all_gather(small,BOTH,axis=0,tiled=True)
    out_full=lax.all_gather(out_weight,BOTH,axis=0,tiled=True)
    out_full=jnp.pad(out_full.reshape(groups*chunks,used,width),((0,0),(0,128-used),(0,0))).reshape(heads_width,width)
    first_full=lax.all_gather(expert_in,"seq",axis=2,tiled=True)[0]
    second_full=lax.all_gather(expert_out,"seq",axis=1,tiled=True)[0]
    copies=jnp.broadcast_to(tokens[:,None],(seq_count,groups,stretch,width)).reshape(seq_devs,stretch,width)
    own_sequence=swap_parts(copies,"seq").reshape(length,width).astype(f32)
    weight=lax.dynamic_slice_in_dim(stacked_full,group*span,span,axis=1)
    router_full=small_full[:,:experts]
    router_wide=jnp.where(jnp.arange(128)[None,:]<experts,small_full,jnp.zeros((),b16))
    attn_gain_full=small_full[:,experts].astype(f32)
    moe_gain_full=small_full[:,experts+1].astype(f32)
    zero_id=jnp.zeros((1,),jnp.int32)
    backward_ids=jnp.concatenate([zero_id,bucket_id])
    forward_ids=reversed_ids(jnp.concatenate([bucket_id,zero_id]))
    own_table=lax.dynamic_slice_in_dim(bias_table,group*own_heads,own_heads,axis=1)*LOG2E
    forward_bias=offset_rows(forward_ids,own_table)
    backward_bias=offset_rows(backward_ids,own_table)
    expert_pick=expert_id.reshape(count)
    slot_pick=slot_id.reshape(count)
    slots=experts*padded_cap
    position=jnp.where(slot_pick<capacity,expert_pick*padded_cap+slot_pick,slots)
    hot=(position[None,:]==jnp.arange(slots,dtype=jnp.int32)[:,None]).astype(b16)
    cot_rows=matmul(hot,cotangent.reshape(count,width)).astype(b16).reshape(experts,padded_cap,width)
    plan=(experts,seq_devs,seq_count,stretch,per_chunk,chunks)
    normed=(own_sequence*inverse_rms(own_sequence)*attn_gain_full).astype(b16)
    projected=matmul(normed,weight).astype(b16)
    attended,out32,log_total,cot_arrived=attend(plan,projected,forward_bias,cot_rows)
    attended=attended.reshape(count,heads_width)
    tokens_f=tokens.astype(f32).reshape(count,width)
    hidden=tokens_f+matmul(attended,out_full)
    moe_inverse=inverse_rms(hidden)
    moe_in=(hidden*moe_inverse*moe_gain_full).astype(b16)
    send_rows=matmul(hot,moe_in).astype(b16).reshape(experts,padded_cap,width)
    home,result,first_grad,second_grad,router_part=expert_layer(send_rows,cot_arrived,first_full,second_full,router_wide)
    expert_in_grad=lax.psum_scatter(first_grad[None],"seq",scatter_dimension=2,tiled=True).astype(f32)
    expert_out_grad=lax.psum_scatter(second_grad[None],"seq",scatter_dimension=1,tiled=True).astype(f32)
    grad_out=cotangent.astype(f32).reshape(count,width)
    moe_in_grad=matmul(hot,home.reshape(slots,width),TN)
    weighted=moe_in_grad*moe_gain_full
    moe_gain_part=jnp.sum(moe_in_grad*hidden*moe_inverse,axis=0)
    inner=jnp.mean(weighted*hidden,axis=-1,keepdims=True)
    hidden_grad=grad_out+weighted*moe_inverse-hidden*(moe_inverse*moe_inverse*moe_inverse)*inner
    branch_grad=hidden_grad.astype(b16)
    heads_grad=matmul(branch_grad,out_full,NT).astype(b16)
    out_part=matmul(attended,branch_grad,TN).reshape(groups*chunks,128,width)[:,:used].reshape(width,width)
    extra=jnp.pad(jnp.concatenate([router_part[:,:experts],moe_gain_part[:,None]],axis=1),((0,0),(0,127-experts)))
    out_piece=jnp.concatenate([out_part,extra],axis=1).astype(b16).reshape(devices,row_block,width+128)
    out_piece=jnp.pad(out_piece,((0,0),(0,-row_block%16),(0,0)))
    hot_bucket=(backward_ids[None,:]==jnp.arange(buckets,dtype=jnp.int32)[:,None]).astype(f32)
    hot_bucket=hot_bucket*(jnp.arange(length*2)>0)[None,:]
    normed_t=jnp.transpose(normed)
    token_grads,returned,out_pieces,weight_pieces,tables=attend_back(plan,projected,out32,log_total,backward_bias,normed_t,hot_bucket,heads_grad.reshape(seq_count,stretch,heads_width),result,out_piece)
    out_sum=jnp.sum(out_pieces[:,:row_block].astype(f32),axis=0)
    logits=matmul(moe_in,router_full)
    gates=jax.nn.softmax(logits,axis=-1)
    picked=(expert_pick[:,None]==jnp.arange(experts,dtype=jnp.int32)[None,:]).astype(f32)
    gate=jnp.sum(gates*picked,axis=-1)
    output=(hidden+gate[:,None]*matmul(hot,returned.reshape(slots,width),TN)).astype(b16).reshape(seq_count,stretch,width)
    tables=jnp.sum(tables.reshape(devices//groups,groups,buckets,-1),axis=0)[:,:,:own_heads]
    bias_table_grad=jnp.transpose(tables,(1,0,2)).reshape(buckets,heads)
    token_grads=token_grads.reshape(count,groups*span)
    normed_grad=matmul(token_grads,stacked_full,NT)
    if row_block%8:
        normed_own=(tokens_f*inverse_rms(tokens_f)*attn_gain_full).astype(b16)
        parts=matmul(normed_own,token_grads,TN).astype(b16).reshape(devices,row_block,groups,chunks,3,128)
        summed=jnp.sum(swap_parts(parts,BOTH).astype(f32),axis=0)
    else:
        parts=weight_pieces[:,:,:row_block].astype(f32).reshape(chunks,devices//groups,groups,row_block,3,128)
        summed=jnp.transpose(jnp.sum(parts,axis=1),(2,1,0,3,4))
    weight_grads=jnp.transpose(summed[...,:used],(3,0,1,2,4)).reshape(3,row_block,width)
    own_weights=jnp.stack([query_weight,key_weight,value_weight]).astype(f32)
    attn_gain_grad=jnp.sum(weight_grads*own_weights,axis=(0,2))/attn_gain.astype(f32)
    tokens_inverse=inverse_rms(tokens_f)
    weighted=normed_grad*attn_gain_full
    inner=jnp.mean(weighted*tokens_f,axis=-1,keepdims=True)
    input_grad=hidden_grad+weighted*tokens_inverse-tokens_f*(tokens_inverse*tokens_inverse*tokens_inverse)*inner
    return (
        output,
        input_grad.reshape(seq_count,stretch,width),
        weight_grads[0],weight_grads[1],weight_grads[2],
        out_sum[:,:width],
        out_sum[:,width:width+experts],
        attn_gain_grad,
        out_sum[:,width+experts],
        bias_table_grad,
        expert_in_grad,
        expert_out_grad,
    )

def solution(mesh):
    tokens=P("exp","seq",None)
    rows=P(BOTH,None)
    return jax.shard_map(
        shards,
        mesh=mesh,
        in_specs=(tokens,rows,rows,rows,rows,rows,P(BOTH),P(BOTH),P(),P("exp",None,"seq"),P("exp","seq",None),P("exp","seq"),P("exp","seq"),P(),tokens),
        out_specs=(tokens,tokens,rows,rows,rows,rows,rows,P(BOTH),P(BOTH),P(),P("exp",None,"seq"),P("exp","seq",None)),
        check_vma=False,
    )
```

```python
import functools
import jax
import jax.numpy as jnp
import numpy as np
from jax import lax
from jax.experimental import pallas as pl
from jax.experimental.pallas import tpu as pltpu
from jax.sharding import PartitionSpec as P
NT=(((1,),(1,)),((),()))
NN=(((1,),(0,)),((),()))
LOG2E=1.4426950408889634
MIB=1024*1024
TN=(((0,),(0,)),((),()))
MESH=pl.DeviceIdType.MESH
EPSILON=1e-06
BOTH=("exp","seq")

def lane_iota(rows):
    return lax.broadcasted_iota(jnp.int32,(rows,128),1)

def dup_head(values,head):
    values=values.astype(jnp.float32)
    turned=pltpu.roll(values,64,1)
    low=lane_iota(values.shape[0])<64
    return jnp.where(low,values,turned) if head==0 else jnp.where(low,turned,values)

def three_parts(column):
    first=column.astype(jnp.bfloat16).astype(jnp.float32)
    rest=column-first
    second=rest.astype(jnp.bfloat16).astype(jnp.float32)
    return first,second,rest-second

def columns_at(lanes,start,parts,other):
    out=other
    for place,part in enumerate(parts):
        out=jnp.where(lanes==start+place,part,out)
    return out

def split_query(query,head,scale):
    both=dup_head(query,head)*scale
    high=both.astype(jnp.bfloat16).astype(jnp.float32)
    return jnp.where(lane_iota(query.shape[0])<64,high,both-high).astype(jnp.bfloat16)

def fill_strip(strip,vector,rows,width):
    full=width+rows
    step=8
    spread=jnp.broadcast_to(vector,(rows,full))
    turned=pltpu.roll(spread,0,1,stride=1,stride_axis=0)
    strip[...]=turned[:,rows:]


def head_column(values,index):
    return jnp.sum(jnp.where(lane_iota(values.shape[0])==index,values,0.0),axis=1,keepdims=True)

def remote(src,dst,sent,received,target):
    return pltpu.make_async_remote_copy(src_ref=src,dst_ref=dst,send_sem=sent,recv_sem=received,device_id=target,device_id_type=MESH)

def loop(first,last,body):
    def step(i,carry):
        body(i)
        return carry
    lax.fori_loop(first,last,step,0)

class Spread:
    def __init__(self,axes,seq_count,groups,source,slot,direct,passed,received,own):
        self.me,self.place=axes
        self.counts=(seq_count,groups)
        self.source,self.slot=source,slot
        self.direct,self.passed,self.received,self.own=direct,passed,received,own
        self.sequence,self.group=self.place//groups,self.place%groups
    def at(self,sequence_step,group_step):
        seq_count,groups=self.counts
        return lax.rem(self.sequence+sequence_step,seq_count)*groups+lax.rem(self.group+group_step,groups)
    def copies(self):
        seq_count,groups=self.counts
        targets=[self.at(i,0) for i in range(1,seq_count)]+[self.at(0,i) for i in range(1,groups)]
        return [remote(self.source(target//groups),self.slot(self.place),self.direct.at[i],self.received.at[self.place],(self.me,target)) for i,target in enumerate(targets)]
    def local(self):
        return pltpu.make_async_copy(self.source(self.sequence),self.slot(self.place),self.own)
    def landed(self,place):
        landing=self.slot(place)
        remote(landing,landing,self.own,self.received.at[place],(self.me,self.place)).wait_recv()
    def relays(self):
        seq_count,groups=self.counts
        out=[]
        for i in range(1,seq_count):
            part=self.at(i,0)
            for j in range(1,groups):
                index=(i-1)*(groups-1)+j-1
                out.append(remote(self.slot(part),self.slot(part),self.passed.at[index],self.received.at[part],(self.me,self.at(0,j))))
        return out
    def start(self):
        self.local().start()
        for copy in self.copies():
            copy.start()
    def relay(self):
        seq_count,groups=self.counts
        for i in range(1,seq_count):
            self.landed(self.at(i,0))
        for copy in self.relays():
            copy.start()
    def finish(self):
        seq_count,groups=self.counts
        for j in range(1,groups):
            for i in range(seq_count):
                self.landed(self.at(i,j))
        for copy in self.copies()+self.relays():
            copy.wait_send()
        self.local().wait()

def spread_semaphores(seq_count,groups):
    dma=lambda n: pltpu.SemaphoreType.DMA((n,))
    return [dma(seq_count+groups-2),dma(max((seq_count-1)*(groups-1),1)),dma(seq_count*groups),pltpu.SemaphoreType.DMA]

def start_kernel(plan,rows,span,token_ref,unit_ref,w1_ref,proj_ref,normed_ref,own_out,w1_out,
                 tok,scaled,units,land,s_unit,r_unit,s_block,r_block,s_pass,own_sem,*spread_sems):
    experts,seq_devs,seq_count,stretch,heads,chunks=plan
    groups=seq_devs//seq_count
    length=stretch*seq_devs
    f32,b16=jnp.float32,jnp.bfloat16
    me,place=lax.axis_index("exp"),lax.axis_index("seq")
    pairs=experts//2
    pair,side=me//2,me%2
    other=1-side
    block=seq_devs*rows
    quarter=w1_ref.shape[2]
    def device(offset,member):
        return lax.rem(pair+offset+pairs,pairs)*2+member
    barrier=pltpu.get_barrier_semaphore()
    for i in range(1,experts):
        pl.semaphore_signal(barrier,inc=1,device_id=(lax.rem(me+i,experts),place),device_id_type=MESH)
    for i in range(1,seq_devs):
        pl.semaphore_signal(barrier,inc=1,device_id=(me,lax.rem(place+i,seq_devs)),device_id_type=MESH)
    def stretch_of(owner):
        return tok.at[pl.ds(pl.multiple_of(owner*stretch,128),stretch)]
    def part_of(owner):
        return w1_out.at[:,pl.ds(pl.multiple_of(owner*quarter,128),quarter)]
    tokens=Spread((me,place),seq_count,groups,lambda n: token_ref.at[n],stretch_of,*spread_sems[:4])
    firsts=Spread((me,place),seq_count,groups,lambda n: w1_ref.at[0],part_of,*spread_sems[4:])
    own_unit=pltpu.make_async_copy(unit_ref.at[place%groups],units.at[place],own_sem.at[0])
    own_unit.start()
    pl.semaphore_wait(barrier,experts+seq_devs-2)
    def send_unit(i):
        target=lax.rem(place+i,seq_devs)
        return remote(unit_ref.at[target%groups],units.at[place],s_unit.at[i],r_unit.at[place],(me,target))
    for i in range(1,seq_devs):
        send_unit(i).start()
    tokens.start()
    firsts.start()
    def landed(landing,received):
        remote(landing,landing,own_sem.at[1],received,(me,place)).wait_recv()
    own_unit.wait()
    for i in range(1,seq_devs):
        source=lax.rem(place+i,seq_devs)
        landed(units.at[source],r_unit.at[source])
    def block_of(owner):
        return land.at[pl.ds(pl.multiple_of(owner*block,16),block)]
    joined=jnp.concatenate([units[i].astype(f32)[:rows] for i in range(seq_devs)],axis=0)
    land[pl.ds(pl.multiple_of(me*block,16),block),:]=joined.astype(b16)
    visit=[j for step in range(1,pairs//2+1) for j in sorted({step,pairs-step})]
    def send_block(j,member,index):
        return remote(block_of(me),block_of(me),s_block.at[index],r_block.at[me],(device(j,member),place))
    sends=[send_block(0,other,0)]+[send_block(j,side,j) for j in visit]
    for copy in sends:
        copy.start()
    passes=[remote(block_of(device(j,side)),block_of(device(j,side)),s_pass.at[j],r_block.at[device(j,side)],(device(0,other),place)) for j in visit]
    for j,copy in zip(visit,passes):
        landed(block_of(device(j,side)),r_block.at[device(j,side)])
        copy.start()
    piece=512 if length%512==0 else 128
    tokens.relay()
    tokens.finish()
    def scale_rows(step):
        part=pl.ds(pl.multiple_of(step*piece,piece),piece)
        x=tok[part,:].astype(f32)
        scaled[part,:]=x*lax.rsqrt(jnp.mean(x*x,axis=-1,keepdims=True)+EPSILON)
    loop(0,length//piece,scale_rows)
    for j in [0]+visit:
        landed(block_of(device(j,other)),r_block.at[device(j,other)])
    own_copy=pltpu.make_async_copy(land,own_out,own_sem.at[2])
    own_copy.start()
    gain=jnp.transpose(land[:,span:].astype(f32))[experts:experts+1,:]
    def project(step):
        part=pl.ds(pl.multiple_of(step*piece,piece),piece)
        normed=(scaled[part,:]*gain).astype(b16)
        normed_ref[part,:]=normed
        proj_ref[part,:]=jnp.dot(normed,land[:,:span],preferred_element_type=f32).astype(b16)
    loop(0,length//piece,project)
    firsts.relay()
    own_copy.wait()
    firsts.finish()
    for copy in sends+passes:
        copy.wait_send()
    for i in range(1,seq_devs):
        send_unit(i).wait_send()

def gather_start(plan,rows,tokens,units,expert_in):
    experts,seq_devs,seq_count,stretch,heads,chunks=plan
    groups=seq_devs//seq_count
    length=stretch*seq_devs
    width=tokens.shape[2]
    span=chunk_span(heads)*chunks
    b16=jnp.bfloat16
    vmem=pl.BlockSpec(memory_space=pltpu.VMEM)
    anywhere=pl.BlockSpec(memory_space=pl.ANY)
    dma=lambda n: pltpu.SemaphoreType.DMA((n,))
    shape=lambda *dims: jax.ShapeDtypeStruct(dims,b16)
    return pl.pallas_call(
        functools.partial(start_kernel,plan,rows,span),
        in_specs=[anywhere,anywhere,vmem],
        out_specs=[vmem,vmem,anywhere,anywhere],
        out_shape=[shape(length,span),shape(length,width),shape(width,span+128),shape(width,expert_in.shape[2]*seq_devs)],
        scratch_shapes=[pltpu.VMEM((length,width),b16),pltpu.VMEM((length,width),jnp.float32),pltpu.VMEM((seq_devs,)+units.shape[1:],b16),pltpu.VMEM((width,span+128),b16),
            dma(seq_devs),dma(seq_devs),dma(experts),dma(experts),dma(experts),dma(3)]+spread_semaphores(seq_count,groups)*2,
        compiler_params=pltpu.CompilerParams(collective_id=3,has_side_effects=True,vmem_limit_bytes=40*MIB),
        cost_estimate=pl.CostEstimate(flops=2*length*width*span,bytes_accessed=24*MIB,transcendentals=0),
        name="gather_start",
    )(tokens,units,expert_in)

def chunk_span(heads):
    return 128*(1+heads)

def forward_kernel(plan,block,srows,scale,proj_ref,bias_ref,cot_ref,own_ref,w2_ref,att_out,o32_ref,lse_ref,cot_out,all_out,w2_out,strip,kd,va,scr,outs,s_cot,r_cot,s_att,r_att,s_all,r_all,local_sem,*spread_sems):
    experts,seq_devs,seq_count,stretch,heads,chunks=plan
    length=stretch*seq_devs
    groups=seq_devs//seq_count
    f32,b16=jnp.float32,jnp.bfloat16
    me,place=lax.axis_index("exp"),lax.axis_index("seq")
    sequence,group=place//groups,place%groups
    barrier=pltpu.get_barrier_semaphore()
    loop(1,experts,lambda i: pl.semaphore_signal(barrier,inc=1,device_id=(lax.rem(me+i,experts),place),device_id_type=MESH))
    loop(1,seq_devs,lambda i: pl.semaphore_signal(barrier,inc=1,device_id=(me,lax.rem(place+i,seq_devs)),device_id_type=MESH))
    own_cot=pltpu.make_async_copy(cot_ref.at[me],cot_out.at[me],local_sem.at[0])
    own_cot.start()
    own_all=pltpu.make_async_copy(own_ref,all_out.at[group],local_sem.at[1+chunks])
    own_all.start()
    deep=w2_ref.shape[1]
    seconds=Spread((me,place),seq_count,groups,lambda n: w2_ref.at[0],lambda owner: w2_out.at[pl.ds(pl.multiple_of(owner*deep,128),deep)],*spread_sems)
    pl.semaphore_wait(barrier,experts+seq_devs-2)
    seconds.start()
    def send_all(i):
        return remote(own_ref,all_out.at[group],s_all.at[i],r_all.at[i],(me,sequence*groups+lax.rem(group+i,groups)))
    loop(1,groups,lambda i: send_all(i).start())
    def send_cot(i):
        target=lax.rem(me+i,experts)
        return remote(cot_ref.at[target],cot_out.at[me],s_cot.at[i],r_cot.at[i],(target,place))
    loop(1,experts,lambda i: send_cot(i).start())
    def lanes_of(owner_group,c,size):
        return pl.ds(pl.multiple_of((owner_group*chunks+c)*size,128),size)
    def send_att(c,i):
        target=lax.rem(place+i,seq_devs)
        rows=pl.ds(pl.multiple_of(target*stretch,128),stretch)
        return remote(outs.at[c,rows],att_out.at[sequence,:,lanes_of(group,c,128)],s_att.at[c,i],r_att.at[c,i],(me,target))
    def own_att(c):
        rows=pl.ds(pl.multiple_of(place*stretch,128),stretch)
        return pltpu.make_async_copy(outs.at[c,rows],att_out.at[sequence,:,lanes_of(group,c,128)],local_sem.at[1+c])
    width=strip.shape[1]
    wide=256
    blocks=length//block
    pieces=length//wide
    lanes=lane_iota(length)
    block_lanes=lane_iota(block)
    lse_ref[...]=jnp.zeros_like(lse_ref)
    def attend_head(c,head):
        index=c*heads+head
        def columns(which):
            return slice(c*chunk_span(heads)+which*128,c*chunk_span(heads)+(which+1)*128)
        own=slice(c*128,(c+1)*128)
        fill_strip(strip,bias_ref[index:index+1,:],srows,width)
        kd[...]=dup_head(proj_ref[:,columns(1+head)],0).astype(b16)
        va[...]=jnp.where(lanes<64,dup_head(proj_ref[:,columns(1+head)],1),jnp.where(lanes==64,1.0,0.0)).astype(b16)
        def rows_of(step):
            return slice(step*block,(step+1)*block)
        def score_piece(step,qa,p,slot,top):
            raw=lax.dot_general(qa,kd[p*wide:(p+1)*wide,:],NT,preferred_element_type=f32)
            parts=[]
            for part in range(block//srows):
                start=length-srows-step*block-part*srows+p*wide
                parts.append(raw[part*srows:(part+1)*srows]+strip[:,pl.ds(start,wide)])
            scores=jnp.concatenate(parts,axis=0)
            scr[slot,:,p*wide:(p+1)*wide]=scores
            for j in range(wide//128):
                top=jnp.maximum(top,scores[:,j*128:(j+1)*128])
            return top
        def mix_piece(slot,p,top,total):
            weights=jnp.exp2(scr[slot,:,p*wide:(p+1)*wide]-top).astype(b16)
            return total+jnp.dot(weights,va[p*wide:(p+1)*wide,:],preferred_element_type=f32)
        def finish(step,top,mixed):
            rows=rows_of(step)
            total=mixed[:,64:65]
            result=mixed/total
            lse_ref[rows,:]=jnp.where(block_lanes==index,top+jnp.log2(total),lse_ref[rows,:])
            if head:
                result=jnp.where(block_lanes<64,o32_ref[rows,own],pltpu.roll(result,64,1))
            o32_ref[rows,own]=result
            if head==heads-1:
                outs[c,rows]=result.astype(b16)
        def send_steps(first,last):
            for part in range(first*block//stretch,last*block//stretch):
                distance=lax.rem(part-place+seq_devs,seq_devs)
                @pl.when(distance==0)
                def _():
                    own_att(c).start()
                @pl.when(distance!=0)
                def _():
                    send_att(c,distance).start()
        def advance(step,slot,top):
            mixing=top is not None
            qa=split_query(proj_ref[rows_of(step),columns(0)],head,scale)
            new=jnp.full((block,128),-jnp.inf,f32)
            mixed=jnp.zeros((block,128),f32)
            for p in range(pieces):
                new=score_piece(step,qa,p,slot,new)
                if mixing:
                    mixed=mix_piece(1-slot,p,top,mixed)
            if mixing:
                finish(step-1,top,mixed)
            return jnp.max(new,axis=1,keepdims=True)
        top=None
        for step in range(blocks):
            top=advance(step,step%2,top)
        if head==heads-1:
            send_steps(0,blocks-1)
        mixed=jnp.zeros((block,128),f32)
        for p in range(pieces):
            mixed=mix_piece((blocks-1)%2,p,top,mixed)
        finish(blocks-1,top,mixed)
        if head==heads-1:
            send_steps(blocks-1,blocks)
    for c in range(chunks):
        for head in range(heads):
            attend_head(c,head)
    seconds.relay()
    def land_att(c,i):
        source=lax.rem(place-i+seq_devs,seq_devs)
        landing=att_out.at[source//groups,:,lanes_of(source%groups,c,128)]
        remote(landing,landing,s_att.at[c,i],r_att.at[c,i],(me,place)).wait_recv()
    def finish_chunk(c):
        own_att(c).wait()
        loop(1,seq_devs,lambda i: land_att(c,i))
        loop(1,seq_devs,lambda i: send_att(c,i).wait_send())
    loop(0,chunks,finish_chunk)
    def land_cot(i):
        landing=cot_out.at[lax.rem(me-i+experts,experts)]
        remote(landing,landing,s_cot.at[i],r_cot.at[i],(me,place)).wait_recv()
    loop(1,experts,land_cot)
    loop(1,experts,lambda i: send_cot(i).wait_send())
    def land_all(i):
        landing=all_out.at[lax.rem(group-i+groups,groups)]
        remote(landing,landing,s_all.at[i],r_all.at[i],(me,place)).wait_recv()
        send_all(i).wait_send()
    loop(1,groups,land_all)
    own_all.wait()
    own_cot.wait()
    seconds.finish()

def attend(plan,projected,bias_vec,cot_rows,own_weight,expert_out,block=512,srows=128):
    experts,seq_devs,seq_count,stretch,heads,chunks=plan
    length=stretch*seq_devs
    groups=seq_devs//seq_count
    f32,b16=jnp.float32,jnp.bfloat16
    vmem=pl.BlockSpec(memory_space=pltpu.VMEM)
    anywhere=pl.BlockSpec(memory_space=pl.ANY)
    dma=lambda *shape: pltpu.SemaphoreType.DMA(shape)
    return pl.pallas_call(
        functools.partial(forward_kernel,plan,block,srows,LOG2E/8),
        in_specs=[vmem,vmem,anywhere,vmem,vmem],
        out_specs=[anywhere,vmem,vmem]+[anywhere]*3,
        out_shape=[jax.ShapeDtypeStruct((seq_count,stretch,groups*chunks*128),b16),jax.ShapeDtypeStruct((length,chunks*128),f32),jax.ShapeDtypeStruct((length,128),f32),jax.ShapeDtypeStruct(cot_rows.shape,b16),jax.ShapeDtypeStruct((groups,)+own_weight.shape,b16),jax.ShapeDtypeStruct((expert_out.shape[1]*seq_devs,expert_out.shape[2]),b16)],
        scratch_shapes=[pltpu.VMEM((srows,2*length-srows),f32),pltpu.VMEM((length,128),b16),pltpu.VMEM((length,128),b16),pltpu.VMEM((2,block,length),f32),pltpu.VMEM((chunks,length,128),b16),
            dma(experts),dma(experts),dma(chunks,seq_devs),dma(chunks,seq_devs),dma(groups),dma(groups),dma(2+chunks)]+spread_semaphores(seq_count,groups),
        compiler_params=pltpu.CompilerParams(collective_id=1,has_side_effects=True,vmem_limit_bytes=48*MIB),
        cost_estimate=pl.CostEstimate(flops=16*heads*chunks*length*length*64,bytes_accessed=16*MIB,transcendentals=heads*chunks*length*length),
        name="attend_forward",
    )(projected,bias_vec,cot_rows,own_weight,expert_out)

def backward_kernel(plan,inside,bq,bk,srows,scale,proj_ref,o32_ref,lse_ref,bias_ref,normed_ref,bucket_ref,up_ref,res_ref,piece_ref,
                    grad_out,ret_out,piece_out,weight_out,table_out,
                    strip,grads,ka,va,kt,qa,da,dd,qd,dk_acc,dv_acc,ups,outs,weight_parts,diag,table,normed_t,
                    s_up,r_up,s_res,r_res,s_piece,r_piece,s_grad,r_grad,s_weight,r_weight,s_table,r_table,local_sem,own_sem):
    experts,seq_devs,seq_count,stretch,heads,chunks=plan
    length=stretch*seq_devs
    groups=seq_devs//seq_count
    devices=experts*seq_devs
    f32,b16=jnp.float32,jnp.bfloat16
    me,place=lax.axis_index("exp"),lax.axis_index("seq")
    sequence,group=place//groups,place%groups
    rank=me*seq_devs+place
    def other(i):
        target=lax.rem(rank+i,devices)
        return target,(target//seq_devs,target%seq_devs)
    barrier=pltpu.get_barrier_semaphore()
    loop(1,devices,lambda i: pl.semaphore_signal(barrier,inc=1,device_id=other(i)[1],device_id_type=MESH))
    def lanes_of(owner_group,c,size):
        return pl.ds(pl.multiple_of((owner_group*chunks+c)*size,128),size)
    def rows_of(owner):
        return pl.ds(pl.multiple_of(owner*stretch,128),stretch)
    def send_up(c,i):
        target=lax.rem(place+i,seq_devs)
        return remote(up_ref.at[target//groups,:,lanes_of(target%groups,c,128)],ups.at[c,rows_of(place)],s_up.at[c,i],r_up.at[c,i],(me,target))
    def own_up(c):
        return pltpu.make_async_copy(up_ref.at[sequence,:,lanes_of(group,c,128)],ups.at[c,rows_of(place)],local_sem.at[0,c])
    def send_res(i):
        target=lax.rem(me+i,experts)
        return remote(res_ref.at[target],ret_out.at[me],s_res.at[i],r_res.at[i],(target,place))
    def send_piece(i):
        target,where=other(i)
        return remote(piece_ref.at[target],piece_out.at[rank],s_piece.at[i],r_piece.at[i],where)
    def grad_lanes(owner_group,c,part):
        return pl.ds(pl.multiple_of((owner_group*chunks+c)*chunk_span(heads)+part*128,128),128)
    def send_grad(c,part,i):
        target=lax.rem(place+i,seq_devs)
        return remote(outs.at[c,rows_of(target),part*128:(part+1)*128],grad_out.at[sequence,:,grad_lanes(group,c,part)],s_grad.at[c,part,i],r_grad.at[c,part,i],(me,target))
    def own_grad(c,part):
        return pltpu.make_async_copy(outs.at[c,rows_of(place),part*128:(part+1)*128],grad_out.at[sequence,:,grad_lanes(group,c,part)],local_sem.at[2+part,c])
    def send_weight(c,i):
        target,where=other(i)
        return remote(weight_parts.at[c,target],weight_out.at[c,rank],s_weight.at[c,i],r_weight.at[c,i],where)
    def own_weight(c):
        return pltpu.make_async_copy(weight_parts.at[c,rank],weight_out.at[c,rank],local_sem.at[1,c])
    def send_table(i):
        return remote(table,table_out.at[rank],s_table.at[i],r_table.at[i],other(i)[1])
    own_table=pltpu.make_async_copy(table,table_out.at[rank],own_sem.at[0])
    own_res=pltpu.make_async_copy(res_ref.at[me],ret_out.at[me],own_sem.at[1])
    own_piece=pltpu.make_async_copy(piece_ref.at[rank],piece_out.at[rank],own_sem.at[2])
    def landed(landing,received):
        remote(landing,landing,own_sem.at[3],received,(me,place)).wait_recv()
    own_res.start()
    own_piece.start()
    loop(0,chunks,lambda c: own_up(c).start())
    pl.semaphore_wait(barrier,devices-1)
    loop(1,seq_devs,lambda i: send_up(0,i).start())
    width=strip.shape[1]
    full_width=2*length
    lanes=lane_iota(length)
    count=length//bk
    if inside:
        weight_parts[...]=jnp.zeros_like(weight_parts)
        normed_t[...]=jnp.transpose(normed_ref[...])
    diag[...]=jnp.zeros_like(diag)
    def head_back(c,head):
        index=c*heads+head
        def columns(which):
            return slice(c*chunk_span(heads)+which*128,c*chunk_span(heads)+(which+1)*128)
        query,both=proj_ref[:,columns(0)],proj_ref[:,columns(1+head)]
        fill_strip(strip,bias_ref[index:index+1,:],srows,width)
        grads[...]=jnp.zeros_like(grads)
        kd=dup_head(both,0)
        ka[:,:128]=kd.astype(b16)
        ka[:,128:]=jnp.where(lanes<3,1.0,0.0).astype(b16)
        kt[...]=jnp.transpose(kd).astype(b16)
        va[...]=jnp.where(lanes<64,dup_head(both,1),jnp.where(lanes<67,1.0,0.0)).astype(b16)
        qa[:,:128]=split_query(query,head,scale)
        qa[:,128:]=columns_at(lanes,0,three_parts(-head_column(lse_ref[...],index)),0.0).astype(b16)
        qd[...]=dup_head(query,head).astype(b16)
        if head==0:
            take_up(c)
        upstream=dup_head(ups[c],head)
        dd[...]=upstream.astype(b16)
        delta=0.5*jnp.sum(upstream*dup_head(o32_ref[:,c*128:(c+1)*128],head),axis=1,keepdims=True)
        da[...]=columns_at(lanes,64,three_parts(-delta),jnp.where(lanes<64,upstream,0.0)).astype(b16)
        dk_acc[...]=jnp.zeros_like(dk_acc)
        dv_acc[...]=jnp.zeros_like(dv_acc)
        def query_block(qb):
            qs=pl.ds(pl.multiple_of(qb*bq,bq),bq)
            def products(kb):
                ks=slice(kb*bk,(kb+1)*bk)
                raw=lax.dot_general(ka[ks,:],qa[qs,:],NT,preferred_element_type=f32)
                up=lax.dot_general(va[ks,:],da[qs,:],NT,preferred_element_type=f32)
                return raw,up
            def consume(kb,raw,up,dq):
                ks=slice(kb*bk,(kb+1)*bk)
                probs,score_grads=[],[]
                for part in range(bk//srows):
                    start=qb*bq+(length-srows)-kb*bk-part*srows
                    rows=slice(part*srows,(part+1)*srows)
                    prob=jnp.exp2(raw[rows]+strip[:,pl.ds(pl.multiple_of(start,128),bq)])
                    grad=prob*up[rows]
                    grads[:,pl.ds(pl.multiple_of(start+srows,128),bq)]+=grad
                    probs.append(prob.astype(b16))
                    score_grads.append(grad.astype(b16))
                low=jnp.concatenate(score_grads,axis=0)
                dv_acc[ks,:]+=jnp.dot(jnp.concatenate(probs,axis=0),dd[qs,:],preferred_element_type=f32)
                dk_acc[ks,:]+=jnp.dot(low,qd[qs,:],preferred_element_type=f32)
                return dq+jnp.dot(kt[:,ks],low,preferred_element_type=f32)
            dq=jnp.zeros((128,bq),f32)
            ready=products(0)
            for kb in range(count):
                following=products(kb+1) if kb+1<count else None
                dq=consume(kb,*ready,dq)
                ready=following
            dq=jnp.transpose(dq)*0.125
            if head:
                dq=jnp.where(lane_iota(bq)<64,outs[c,qs,0:128].astype(f32),dq)
            outs[c,qs,0:128]=dq.astype(b16)
            if head==heads-1:
                for part in range(bq//stretch):
                    distance=lax.rem(qb*(bq//stretch)+part-place+seq_devs,seq_devs)
                    @pl.when(distance==0)
                    def _():
                        own_grad(c,0).start()
                    @pl.when(distance!=0)
                    def _():
                        send_grad(c,0,distance).start()
        loop(0,length//bq,query_block)
        outs[c,:,128*(1+head):128*(2+head)]=jnp.where(lanes<64,dk_acc[...]*0.125,dv_acc[...]).astype(b16)
        loop(1,seq_devs,lambda i: send_grad(c,1+head,i).start())
        own_grad(c,1+head).start()
        total=grads[0:8,:]
        for part in range(1,srows//8):
            total=total+pltpu.roll(grads[8*part:8*part+8,:],full_width-8*part,1)
        row=lax.broadcasted_iota(jnp.int32,(8,full_width),0)
        for part in range(1,8):
            total=jnp.where(row==part,pltpu.roll(total,full_width-part,1),total)
        diag[index:index+1,:]=jnp.sum(total,axis=0,keepdims=True)
    def take_up(c):
        loop(1,seq_devs,lambda i: landed(ups.at[c,rows_of(lax.rem(place-i+seq_devs,seq_devs))],r_up.at[c,i]))
        own_up(c).wait()
        if c==0:
            loop(1,chunks,lambda later: loop(1,seq_devs,lambda i: send_up(later,i).start()))
            loop(1,experts,lambda i: send_res(i).start())
            loop(1,devices,lambda i: send_piece(i).start())
    def one_chunk(c):
        for head in range(heads):
            head_back(c,head)
        if inside:
            part=jnp.dot(normed_t[...],outs[c],preferred_element_type=f32)
            block=normed_t.shape[0]//devices
            weight_parts[c,:,:block,:]=part.reshape(devices,block,chunk_span(heads)).astype(b16)
            loop(1,devices,lambda i: send_weight(c,i).start())
            own_weight(c).start()
    for c in range(chunks):
        one_chunk(c)
    table[...]=lax.dot_general(bucket_ref[...],diag[...],NT,precision=lax.Precision.HIGHEST,preferred_element_type=f32)
    loop(1,devices,lambda i: send_table(i).start())
    own_table.start()
    def finish_chunk(c):
        def grad_landed(i):
            source=lax.rem(place-i+seq_devs,seq_devs)
            for part in range(1+heads):
                landed(grad_out.at[source//groups,:,grad_lanes(source%groups,c,part)],r_grad.at[c,part,i])
                send_grad(c,part,i).wait_send()
            send_up(c,i).wait_send()
        loop(1,seq_devs,grad_landed)
        for part in range(1+heads):
            own_grad(c,part).wait()
        if inside:
            def weight_landed(i):
                landed(weight_out.at[c,lax.rem(rank-i+devices,devices)],r_weight.at[c,i])
                send_weight(c,i).wait_send()
            loop(1,devices,weight_landed)
            own_weight(c).wait()
    loop(0,chunks,finish_chunk)
    def res_landed(i):
        landed(ret_out.at[lax.rem(me-i+experts,experts)],r_res.at[i])
        send_res(i).wait_send()
    loop(1,experts,res_landed)
    def piece_landed(i):
        source=lax.rem(rank-i+devices,devices)
        landed(piece_out.at[source],r_piece.at[i])
        send_piece(i).wait_send()
        landed(table_out.at[source],r_table.at[i])
        send_table(i).wait_send()
    loop(1,devices,piece_landed)
    own_res.wait()
    own_piece.wait()
    own_table.wait()

def attend_back(plan,projected,o32,lse,bias_vec,normed,buckets,upstream,result,piece,bq=512,bk=512,srows=128):
    experts,seq_devs,seq_count,stretch,heads,chunks=plan
    length=stretch*seq_devs
    groups=seq_devs//seq_count
    devices=experts*seq_devs
    block=normed.shape[1]//devices
    inside=block%8==0
    rows=(block+15)//16*16
    f32,b16=jnp.float32,jnp.bfloat16
    vm=lambda kind,*shape: pltpu.VMEM(shape,kind)
    vmem=pl.BlockSpec(memory_space=pltpu.VMEM)
    anywhere=pl.BlockSpec(memory_space=pl.ANY)
    dma=lambda *shape: pltpu.SemaphoreType.DMA(shape)
    shape=lambda kind,*dims: jax.ShapeDtypeStruct(dims,kind)
    weight_shape=(chunks,devices,rows,chunk_span(heads)) if inside else (1,1,16,128)
    return pl.pallas_call(
        functools.partial(backward_kernel,plan,inside,bq,bk,srows,LOG2E/8),
        in_specs=[vmem]*6+[anywhere]*3,
        out_specs=[anywhere]*5,
        out_shape=[shape(b16,seq_count,stretch,groups*chunks*chunk_span(heads)),shape(b16,*result.shape),shape(b16,*piece.shape),shape(b16,*weight_shape),shape(f32,devices,buckets.shape[0],diag_rows(plan))],
        scratch_shapes=[vm(f32,srows,2*length-srows),vm(f32,srows,2*length),vm(b16,length,256),vm(b16,length,128),vm(b16,128,length),
            vm(b16,length,256),vm(b16,length,128),vm(b16,length,128),vm(b16,length,128),vm(f32,length,128),vm(f32,length,128),
            vm(b16,chunks,length,128),vm(b16,chunks,length,chunk_span(heads)),vm(b16,*weight_shape),vm(f32,diag_rows(plan),2*length),vm(f32,buckets.shape[0],diag_rows(plan)),vm(b16,normed.shape[1],length),
            dma(chunks,seq_devs),dma(chunks,seq_devs),dma(experts),dma(experts),dma(devices),dma(devices),dma(chunks,1+heads,seq_devs),dma(chunks,1+heads,seq_devs),
            dma(chunks,devices),dma(chunks,devices),dma(devices),dma(devices),dma(3+heads,chunks),dma(4)],
        compiler_params=pltpu.CompilerParams(collective_id=2,has_side_effects=True,vmem_limit_bytes=58*MIB),
        cost_estimate=pl.CostEstimate(flops=40*heads*chunks*length*length*64,bytes_accessed=24*MIB,transcendentals=heads*chunks*length*length),
        name="attend_backward",
    )(projected,o32,lse,bias_vec,normed,buckets,upstream,result,piece)

def diag_rows(plan):
    return 128

def combine_kernel(experts,pos_ref,home_ref,hidden_ref,cot_ref,att_ref,out_w_ref,gain_ref,router_ref,grad_ref,heads_ref,part_ref,total,gain_total):
    f32,b16=jnp.float32,jnp.bfloat16
    step=pl.program_id(0)
    rows=hidden_ref.shape[0]
    slots=home_ref.shape[0]
    width=hidden_ref.shape[1]
    hot=(pos_ref[...]==lax.broadcasted_iota(jnp.int32,(rows,slots),1)).astype(f32).astype(b16)
    moe_in_grad=jnp.dot(hot,home_ref[...],preferred_element_type=f32)
    hidden=hidden_ref[...]
    inverse=lax.rsqrt(jnp.mean(hidden*hidden,axis=-1,keepdims=True)+EPSILON)
    weighted=moe_in_grad*gain_ref[...]
    inner=jnp.mean(weighted*hidden,axis=-1,keepdims=True)
    hidden_grad=cot_ref[...].astype(f32)+weighted*inverse-hidden*(inverse*inverse*inverse)*inner
    grad_ref[...]=hidden_grad
    branch=hidden_grad.astype(b16)
    heads_ref[...]=lax.dot_general(branch,out_w_ref[...],NT,preferred_element_type=f32).astype(b16)
    part=lax.dot_general(att_ref[...],branch,TN,preferred_element_type=f32)
    gain_part=jnp.sum(moe_in_grad*hidden*inverse,axis=0,keepdims=True)
    @pl.when(step==0)
    def _():
        total[...]=part
        gain_total[...]=jnp.broadcast_to(gain_part,gain_total.shape)
    @pl.when(step>0)
    def _():
        total[...]+=part
        gain_total[...]+=gain_part
    @pl.when(step==pl.num_programs(0)-1)
    def _():
        heads_width=total.shape[0]
        part_ref[:,:width]=total[...].astype(b16)
        column=jnp.transpose(jnp.broadcast_to(gain_total[0:1,:],(128,width)))
        lanes=lax.broadcasted_iota(jnp.int32,(width,128),1)
        part_ref[:width,width:]=jnp.where(lanes==experts,column,router_ref[...]).astype(b16)

def combine(experts,position,home,hidden,cotangent,attended,out_full,gain,router_part,block=256):
    count,width=hidden.shape
    heads_width=attended.shape[1]
    f32,b16=jnp.float32,jnp.bfloat16
    block=min(block,count)
    by_rows=lambda columns: pl.BlockSpec((block,columns),lambda i:(i,0))
    whole=lambda value: pl.BlockSpec(value.shape,lambda i:(0,0))
    return pl.pallas_call(
        functools.partial(combine_kernel,experts),
        grid=(count//block,),
        in_specs=[by_rows(1),whole(home),by_rows(width),by_rows(width),by_rows(heads_width),whole(out_full),whole(gain),whole(router_part)],
        out_specs=[by_rows(width),by_rows(heads_width),pl.BlockSpec((heads_width,width+128),lambda i:(0,0))],
        out_shape=[jax.ShapeDtypeStruct((count,width),f32),jax.ShapeDtypeStruct((count,heads_width),b16),jax.ShapeDtypeStruct((heads_width,width+128),b16)],
        scratch_shapes=[pltpu.VMEM((heads_width,width),f32),pltpu.VMEM((8,width),f32)],
        compiler_params=pltpu.CompilerParams(vmem_limit_bytes=40*MIB),
        cost_estimate=pl.CostEstimate(flops=6*count*width*width,bytes_accessed=16*MIB,transcendentals=0),
        name="combine",
    )(position,home,hidden,cotangent,attended,out_full,gain,router_part)

def finish_kernel(experts,groups,heads,chunks,inside,pos_ref,pick_ref,returned_ref,hidden_ref,grad_ref,token_ref,token_grad_ref,every_ref,gains_ref,router_ref,piece_ref,weight_ref,table_ref,
                  output_ref,input_ref,piece_sum,query_sum,key_sum,value_sum,table_sum):
    f32,b16=jnp.float32,jnp.bfloat16
    step=pl.program_id(0)
    rows,width=hidden_ref.shape
    slots=returned_ref.shape[0]
    cw=chunk_span(heads)
    span=chunks*cw
    hidden=hidden_ref[...]
    moe_in=(hidden*lax.rsqrt(jnp.mean(hidden*hidden,axis=-1,keepdims=True)+EPSILON)*gains_ref[1:2,:]).astype(b16)
    lanes=lax.broadcasted_iota(jnp.int32,(rows,128),1)
    logits=jnp.where(lanes<experts,jnp.dot(moe_in,router_ref[...],preferred_element_type=f32),-jnp.inf)
    raised=jnp.exp(logits-jnp.max(logits,axis=1,keepdims=True))
    gate=jnp.sum(jnp.where(lanes==pick_ref[...],raised,0.0),axis=1,keepdims=True)/jnp.sum(raised,axis=1,keepdims=True)
    hot=(pos_ref[...]==lax.broadcasted_iota(jnp.int32,(rows,slots),1)).astype(f32).astype(b16)
    output_ref[...]=(hidden+gate*jnp.dot(hot,returned_ref[...],preferred_element_type=f32)).astype(b16)
    normed_grad=jnp.zeros((rows,width),f32)
    for owner in range(groups):
        normed_grad=normed_grad+lax.dot_general(token_grad_ref[:,owner*span:(owner+1)*span],every_ref[owner,:,:span],NT,preferred_element_type=f32)
    x=token_ref[...].astype(f32)
    inverse=lax.rsqrt(jnp.mean(x*x,axis=-1,keepdims=True)+EPSILON)
    weighted=normed_grad*gains_ref[0:1,:]
    inner=jnp.mean(weighted*x,axis=-1,keepdims=True)
    input_ref[...]=grad_ref[...]+weighted*inverse-x*(inverse*inverse*inverse)*inner
    @pl.when(step==0)
    def _():
        devices=piece_ref.shape[0]
        def add_piece(i,total):
            return total+piece_ref[i].astype(f32)
        piece_sum[...]=lax.fori_loop(1,devices,add_piece,piece_ref[0].astype(f32))
        for owner in range(groups):
            def add_table(i,total):
                return total+table_ref[i*groups+owner]
            table_sum[owner]=lax.fori_loop(1,devices//groups,add_table,table_ref[owner])
            if inside:
                for c in range(chunks):
                    def add_weight(i,total):
                        return total+weight_ref[c,i*groups+owner].astype(f32)
                    summed=lax.fori_loop(1,devices//groups,add_weight,weight_ref[c,owner].astype(f32))
                    place=slice((owner*chunks+c)*128,(owner*chunks+c+1)*128)
                    query_sum[:,place]=summed[:,0:128]
                    first=summed[:,128:256]
                    second=summed[:,128*heads:128*(heads+1)]
                    low=lane_iota(summed.shape[0])<64
                    key_sum[:,place]=jnp.where(low,first,pltpu.roll(second,64,1))
                    value_sum[:,place]=jnp.where(low,pltpu.roll(first,64,1),second)

def finish(experts,groups,heads,chunks,inside,position,pick,returned,hidden,hidden_grad,tokens,token_grads,every_weight,gains,router,pieces,weights,tables,block=256):
    count,width=hidden.shape
    f32,b16=jnp.float32,jnp.bfloat16
    block=min(block,count)
    by_rows=lambda columns: pl.BlockSpec((block,columns),lambda i:(i,0))
    def whole(shape):
        return pl.BlockSpec(shape,lambda i:(0,)*len(shape))
    sums=jax.ShapeDtypeStruct((pieces.shape[1],groups*chunks*128),f32)
    table_shape=jax.ShapeDtypeStruct((groups,)+tables.shape[1:],f32)
    piece_shape=jax.ShapeDtypeStruct(pieces.shape[1:],f32)
    return pl.pallas_call(
        functools.partial(finish_kernel,experts,groups,heads,chunks,inside),
        grid=(count//block,),
        in_specs=[by_rows(1),by_rows(1),whole(returned.shape),by_rows(width),by_rows(width),by_rows(width),by_rows(token_grads.shape[1]),whole(every_weight.shape),whole(gains.shape),whole(router.shape),whole(pieces.shape),whole(weights.shape),whole(tables.shape)],
        out_specs=[by_rows(width),by_rows(width),whole(piece_shape.shape)]+[whole(sums.shape)]*3+[whole(table_shape.shape)],
        out_shape=[jax.ShapeDtypeStruct((count,width),b16),jax.ShapeDtypeStruct((count,width),f32),piece_shape,sums,sums,sums,table_shape],
        compiler_params=pltpu.CompilerParams(vmem_limit_bytes=56*MIB),
        cost_estimate=pl.CostEstimate(flops=8*count*width*width,bytes_accessed=24*MIB,transcendentals=0),
        name="finish",
    )(position,pick,returned,hidden,hidden_grad,tokens,token_grads,every_weight,gains,router,pieces,weights,tables)

def gelu_pair(u):
    c=0.7978845608028654
    square=u*u
    t=jnp.tanh(c*u*(1.0+0.044715*square))
    half=0.5*(1.0+t)
    return u*half,half+(0.5*c)*u*(1.0-t*t)*(1.0+0.134145*square)

def expert_kernel(experts,cap,width,hidden_width,send_ref,cot_hbm,w1_hbm,w2_hbm,router_ref,home,result_out,dw1,dw2,router_part,
                  rows,cots,grads,results,row_grads,logit_grads,act,slope,w1,w2,rows_t,
                  local_sem,cot_sem,out_sem,s_rows,r_rows,s_home,r_home):
    f32,b16=jnp.float32,jnp.bfloat16
    pairs=experts//2
    me=lax.axis_index("exp")
    seq=lax.axis_index("seq")
    pair,side=me//2,me%2
    other=1-side
    def device(offset,member):
        return lax.rem(pair+offset+pairs,pairs)*2+member
    barrier=pltpu.get_barrier_semaphore()
    for step in range(1,experts):
        pl.semaphore_signal(barrier,inc=1,device_id=(lax.rem(me+step,experts),seq),device_id_type=MESH)
    load1=pltpu.make_async_copy(w1_hbm,w1,local_sem.at[0])
    load2=pltpu.make_async_copy(w2_hbm,w2,local_sem.at[1])
    own_rows=pltpu.make_async_copy(send_ref.at[me],rows.at[side],local_sem.at[2])
    local=[own_rows,load1,load2]
    cot_loads=[pltpu.make_async_copy(cot_hbm.at[device(-j,m)],cots.at[2*j+m],cot_sem.at[2*j+m]) for j in range(pairs) for m in range(2)]
    for copy in local+cot_loads:
        copy.start()
    pl.semaphore_wait(barrier,experts-1)
    def remote(src,dst,s,r,target):
        return pltpu.make_async_remote_copy(src_ref=src,dst_ref=dst,send_sem=s,recv_sem=r,device_id=(target,seq),device_id_type=MESH)
    started=[]
    def launch(copy):
        copy.start()
        started.append(copy)
    visit=[j for step in range(1,pairs//2+1) for j in sorted({step,pairs-step})]
    launch(remote(send_ref.at[device(0,other)],rows.at[side],s_rows.at[1],r_rows.at[side],device(0,other)))
    for j in visit:
        for m in range(2):
            member=side if m==0 else other
            launch(remote(send_ref.at[device(j,member)],rows.at[2*j+side],s_rows.at[2*j+m],r_rows.at[2*j+side],device(j,member)))
    def wait_slot(landing,r,slot):
        remote(landing,landing,s_rows.at[0],r.at[slot],me).wait_recv()
    chunk=512 if hidden_width%512==0 else 128
    steps=hidden_width//chunk
    lanes=lax.broadcasted_iota(jnp.int32,(2*cap,128),1)
    onehot=jnp.where(lanes==me,1.0,0.0)
    outputs=[]
    def process(j):
        x=rows[2*j:2*j+2].reshape(2*cap,width)
        base=2*j*cap
        span=slice(base,base+2*cap)
        logits=jnp.dot(x,router_ref[...],preferred_element_type=f32)
        logits=jnp.where(lanes<experts,logits,-jnp.inf)
        raised=jnp.exp(logits-jnp.max(logits,axis=1,keepdims=True))
        gates=raised/jnp.sum(raised,axis=1,keepdims=True)
        gate=jnp.sum(gates*onehot,axis=1,keepdims=True)
        for m in range(2):
            cot_loads[2*j+m].wait()
        cot=cots[2*j:2*j+2].reshape(2*cap,width).astype(f32)
        grads[span,:]=(gate*cot).astype(b16)
        def forward(step,carry):
            cols=pl.ds(pl.multiple_of(step*chunk,chunk),chunk)
            pre=jnp.dot(x,w1[:,cols],preferred_element_type=f32)
            a,d=gelu_pair(pre)
            act[span,cols]=a.astype(b16)
            slope[span,cols]=d.astype(b16)
            return carry
        lax.fori_loop(0,steps,forward,0)
        result=jnp.dot(act[span,:],w2[...],preferred_element_type=f32).astype(b16)
        results[2*j:2*j+2]=result.reshape(2,cap,width)
        for m in range(2):
            copy=pltpu.make_async_copy(results.at[2*j+m],result_out.at[device(-j,m)],out_sem.at[2*j+m])
            copy.start()
            outputs.append(copy)
        gate_grad=jnp.sum(cots[2*j:2*j+2].reshape(2*cap,width).astype(f32)*result.astype(f32),axis=1,keepdims=True)
        logit_grad=(gates*(onehot-gate)*gate_grad).astype(b16)
        logit_grads[span,:]=logit_grad
        def backward(step,carry):
            cols=pl.ds(pl.multiple_of(step*chunk,chunk),chunk)
            up=lax.dot_general(grads[span,:],w2[cols,:],NT,preferred_element_type=f32)
            up=up.astype(b16).astype(f32)*slope[span,cols].astype(f32)
            slope[span,cols]=up.astype(b16)
            return carry
        lax.fori_loop(0,steps,backward,0)
        back=lax.dot_general(slope[span,:],w1[...],NT,preferred_element_type=f32)
        back=back+lax.dot_general(logit_grad,router_ref[...],NT,preferred_element_type=f32)
        row_grads[2*j:2*j+2]=back.astype(b16).reshape(2,cap,width)
        for m in range(2):
            member=side if m==0 else other
            if j==0 and m==0:
                copy=pltpu.make_async_copy(row_grads.at[side],home.at[me],local_sem.at[3])
                copy.start()
                outputs.append(copy)
            else:
                launch(remote(row_grads.at[2*j+member],home.at[me],s_home.at[2*j+m],r_home.at[2*j+side],device(-j,member)))
    load1.wait()
    load2.wait()
    own_rows.wait()
    wait_slot(rows.at[other],r_rows,other)
    process(0)
    for j in visit:
        for m in range(2):
            wait_slot(rows.at[2*j+m],r_rows,2*j+m)
        process(j)
    rows_t[...]=jnp.transpose(rows[...].reshape(experts*cap,width))
    router_part[...]=jnp.dot(rows_t[...],logit_grads[...],preferred_element_type=f32)
    def weight_grads(step,carry):
        cols=pl.ds(pl.multiple_of(step*chunk,chunk),chunk)
        dw1[:,cols]=jnp.dot(rows_t[...],slope[:,cols],preferred_element_type=f32).astype(b16)
        dw2[cols,:]=lax.dot_general(act[:,cols],grads[...],TN,preferred_element_type=f32).astype(b16)
        return carry
    lax.fori_loop(0,steps,weight_grads,0)
    for j in range(pairs):
        for m in range(2):
            if j:
                wait_slot(home.at[device(j,m)],r_home,2*j+m)
    wait_slot(home.at[device(0,other)],r_home,other)
    for copy in outputs:
        copy.wait()
    for copy in started:
        copy.wait_send()

def expert_layer(send,cot,w1,w2,router,cid=4):
    experts,cap,width=send.shape
    hidden_width=w1.shape[1]
    b16=jnp.bfloat16
    block=jax.ShapeDtypeStruct((experts,cap,width),b16)
    anywhere=pl.BlockSpec(memory_space=pl.ANY)
    vmem=pl.BlockSpec(memory_space=pltpu.VMEM)
    dma=lambda n: pltpu.SemaphoreType.DMA((n,))
    blocks=pltpu.VMEM((experts,cap,width),b16)
    wide=pltpu.VMEM((experts*cap,hidden_width),b16)
    return pl.pallas_call(
        functools.partial(expert_kernel,experts,cap,width,hidden_width),
        in_specs=[anywhere]*4+[vmem],
        out_specs=[anywhere,anywhere,vmem,vmem,vmem],
        out_shape=[block,block,jax.ShapeDtypeStruct(w1.shape,b16),jax.ShapeDtypeStruct(w2.shape,b16),jax.ShapeDtypeStruct((width,128),jnp.float32)],
        scratch_shapes=[blocks,blocks,pltpu.VMEM((experts*cap,width),b16),blocks,blocks,pltpu.VMEM((experts*cap,128),b16),wide,wide,
            pltpu.VMEM(w1.shape,b16),pltpu.VMEM(w2.shape,b16),pltpu.VMEM((width,experts*cap),b16),
            dma(4)]+[dma(experts)]*6,
        compiler_params=pltpu.CompilerParams(collective_id=cid,has_side_effects=True,vmem_limit_bytes=60*MIB),
        cost_estimate=pl.CostEstimate(flops=12*experts*cap*width*hidden_width,bytes_accessed=40*MIB,transcendentals=experts*cap*hidden_width),
        name="expert_layer",
    )(send,cot,w1,w2,router)

def inverse_rms(values):
    return lax.rsqrt(jnp.mean(values*values,axis=-1,keepdims=True)+EPSILON)

def matmul(left,right,dims=NN):
    return lax.dot_general(left,right,dims,preferred_element_type=jnp.float32)

def swap_parts(values,axis):
    return lax.all_to_all(values,axis,split_axis=0,concat_axis=0,tiled=True)

def reversed_ids(ids):
    flip=np.eye(128,dtype=np.float32)[::-1]
    rows=ids.shape[0]//128
    flip_rows=np.eye(rows,dtype=np.float32)[::-1]
    grid=ids.astype(jnp.bfloat16).reshape(rows,128)
    grid=matmul(grid,jnp.asarray(flip,jnp.bfloat16)).astype(jnp.bfloat16)
    return matmul(jnp.asarray(flip_rows,jnp.bfloat16),grid).reshape(-1).astype(jnp.int32)

def offset_rows(ids,table):
    hot=(ids[None,:]==jnp.arange(table.shape[0],dtype=jnp.int32)[:,None]).astype(jnp.float32)
    return lax.dot_general(table,hot,TN,precision=lax.Precision.HIGHEST)

def shards(tokens,query_weight,key_weight,value_weight,out_weight,router_weight,attn_gain,moe_gain,bias_table,expert_in,expert_out,expert_id,slot_id,bucket_id,cotangent):
    f32,b16=jnp.float32,jnp.bfloat16
    seq_count,stretch,width=tokens.shape
    seq_devs=lax.axis_size("seq")
    experts=lax.axis_size("exp")
    devices=seq_devs*experts
    length=stretch*seq_devs
    count=seq_count*stretch
    capacity=(5*count+4*experts-1)//(4*experts)
    padded_cap=(capacity+15)//16*16
    buckets,heads=bias_table.shape
    head_dim=width//heads
    groups=seq_devs//seq_count
    own_heads=heads//groups
    per_chunk=2 if own_heads%2==0 else 1
    chunks=own_heads//per_chunk
    used=per_chunk*head_dim
    span=chunks*chunk_span(per_chunk)
    heads_width=groups*chunks*128
    row_block=width//devices
    place=lax.axis_index("seq")
    group=place%groups
    def by_group(weight):
        return weight.reshape(row_block,groups,chunks,per_chunk,head_dim)
    query_part=jnp.pad(by_group(query_weight).reshape(row_block,groups,chunks,used),((0,0),(0,0),(0,0),(0,128-used)))
    both_part=jnp.concatenate([by_group(key_weight),by_group(value_weight)],axis=4).reshape(row_block,groups,chunks,per_chunk*128)
    stacked=jnp.concatenate([query_part,both_part],axis=3).reshape(row_block,groups,span)
    gains=jnp.stack([attn_gain,moe_gain],axis=1)
    small=jnp.pad(jnp.concatenate([router_weight,gains],axis=1),((0,0),(0,126-experts)))
    units=jnp.concatenate([stacked,jnp.broadcast_to(small[:,None],(row_block,groups,128))],axis=2)
    out_full=lax.all_gather(out_weight,BOTH,axis=0,tiled=True)
    out_full=jnp.pad(out_full.reshape(groups*chunks,used,width),((0,0),(0,128-used),(0,0))).reshape(heads_width,width)
    plan=(experts,seq_devs,seq_count,stretch,per_chunk,chunks)
    if row_block%8==0 and row_block*seq_devs%16==0:
        units=jnp.pad(jnp.swapaxes(units,0,1),((0,0),(0,-row_block%16),(0,0)))
        projected,normed,own_weight,first_full=gather_start(plan,row_block,tokens,units,expert_in)
    else:
        copies=jnp.broadcast_to(tokens[:,None],(seq_count,groups,stretch,width)).reshape(seq_devs,stretch,width)
        own_sequence=swap_parts(copies,"seq").reshape(length,width).astype(f32)
        every=lax.all_gather(units,BOTH,axis=0,tiled=True)
        own_weight=lax.dynamic_index_in_dim(every,group,axis=1,keepdims=False)
        normed=(own_sequence*inverse_rms(own_sequence)*own_weight[:,span+experts].astype(f32)).astype(b16)
        projected=matmul(normed,own_weight[:,:span]).astype(b16)
        first_full=lax.all_gather(expert_in[0],"seq",axis=1,tiled=True)
    small_full=own_weight[:,span:]
    router_full=small_full[:,:experts]
    router_wide=jnp.where(jnp.arange(128)[None,:]<experts,small_full,jnp.zeros((),b16))
    attn_gain_full=small_full[:,experts].astype(f32)
    moe_gain_full=small_full[:,experts+1].astype(f32)
    zero_id=jnp.zeros((1,),jnp.int32)
    backward_ids=jnp.concatenate([zero_id,bucket_id])
    forward_ids=reversed_ids(jnp.concatenate([bucket_id,zero_id]))
    own_table=lax.dynamic_slice_in_dim(bias_table,group*own_heads,own_heads,axis=1)*LOG2E
    forward_bias=offset_rows(forward_ids,own_table)
    backward_bias=offset_rows(backward_ids,own_table)
    expert_pick=expert_id.reshape(count)
    slot_pick=slot_id.reshape(count)
    slots=experts*padded_cap
    position=jnp.where(slot_pick<capacity,expert_pick*padded_cap+slot_pick,slots)
    hot=(position[None,:]==jnp.arange(slots,dtype=jnp.int32)[:,None]).astype(b16)
    cot_rows=matmul(hot,cotangent.reshape(count,width)).astype(b16).reshape(experts,padded_cap,width)
    attended,out32,log_total,cot_arrived,every_weight,second_full=attend(plan,projected,forward_bias,cot_rows,own_weight,expert_out)
    attended=attended.reshape(count,heads_width)
    tokens_f=tokens.astype(f32).reshape(count,width)
    hidden=tokens_f+matmul(attended,out_full)
    moe_inverse=inverse_rms(hidden)
    moe_in=(hidden*moe_inverse*moe_gain_full).astype(b16)
    send_rows=matmul(hot,moe_in).astype(b16).reshape(experts,padded_cap,width)
    home,result,first_grad,second_grad,router_part=expert_layer(send_rows,cot_arrived,first_full,second_full,router_wide)
    expert_in_grad=lax.psum_scatter(first_grad[None],"seq",scatter_dimension=2,tiled=True).astype(f32)
    expert_out_grad=lax.psum_scatter(second_grad[None],"seq",scatter_dimension=1,tiled=True).astype(f32)
    gain_rows=jnp.transpose(small_full[:,experts:experts+2].astype(f32))
    home=home.reshape(slots,width)
    positions=position[:,None]
    hidden_grad,heads_grad,out_part=combine(experts,positions,home,hidden,cotangent.reshape(count,width),attended,out_full,gain_rows[1:2],router_part)
    out_part=jnp.concatenate([out_part[:,:width].reshape(groups*chunks,128,width)[:,:used].reshape(width,width),out_part[:width,width:]],axis=1) if used<128 else out_part
    out_piece=jnp.pad(out_part.reshape(devices,row_block,width+128),((0,0),(0,-row_block%16),(0,0)))
    hot_bucket=(backward_ids[None,:]==jnp.arange(buckets,dtype=jnp.int32)[:,None]).astype(f32)
    hot_bucket=hot_bucket*(jnp.arange(length*2)>0)[None,:]
    token_grads,returned,out_pieces,weight_pieces,tables=attend_back(plan,projected,out32,log_total,backward_bias,normed,hot_bucket,heads_grad.reshape(seq_count,stretch,heads_width),result,out_piece)
    inside=row_block%8==0
    token_grads=token_grads.reshape(count,groups*span)
    output,input_grad,out_sum,*weight_grads,tables=finish(experts,groups,per_chunk,chunks,inside,positions,expert_pick[:,None],returned.reshape(slots,width),hidden,hidden_grad,tokens.reshape(count,width),token_grads,every_weight,gain_rows,router_wide,out_pieces,weight_pieces,tables)
    out_sum=out_sum[:row_block]
    output=output.reshape(seq_count,stretch,width)
    bias_table_grad=jnp.transpose(tables[:,:,:own_heads],(1,0,2)).reshape(buckets,heads)
    if inside:
        weight_grads=jnp.stack([part[:row_block] for part in weight_grads])
    else:
        tokens_f=tokens.astype(f32).reshape(count,width)
        normed_own=(tokens_f*inverse_rms(tokens_f)*attn_gain_full).astype(b16)
        parts=matmul(normed_own,token_grads,TN).astype(b16).reshape(devices,row_block,groups*chunks,1+per_chunk,128)
        summed=jnp.sum(swap_parts(parts,BOTH).astype(f32),axis=0)
        both_sum=summed[:,:,1:].reshape(row_block,groups*chunks,per_chunk,2,head_dim)
        weight_grads=jnp.stack([summed[:,:,0,:used].reshape(row_block,width)]+[both_sum[:,:,:,i].reshape(row_block,width) for i in range(2)])
    own_weights=jnp.stack([query_weight,key_weight,value_weight]).astype(f32)
    attn_gain_grad=jnp.sum(weight_grads*own_weights,axis=(0,2))/attn_gain.astype(f32)
    return (
        output,
        input_grad.reshape(seq_count,stretch,width),
        weight_grads[0],weight_grads[1],weight_grads[2],
        out_sum[:,:width],
        out_sum[:,width:width+experts],
        attn_gain_grad,
        out_sum[:,width+experts],
        bias_table_grad,
        expert_in_grad,
        expert_out_grad,
    )

def solution(mesh):
    tokens=P("exp","seq",None)
    rows=P(BOTH,None)
    return jax.shard_map(
        shards,
        mesh=mesh,
        in_specs=(tokens,rows,rows,rows,rows,rows,P(BOTH),P(BOTH),P(),P("exp",None,"seq"),P("exp","seq",None),P("exp","seq"),P("exp","seq"),P(),tokens),
        out_specs=(tokens,tokens,rows,rows,rows,rows,rows,P(BOTH),P(BOTH),P(),P("exp",None,"seq"),P("exp","seq",None)),
        check_vma=False,
    )
```

```python
import functools
import jax
import jax.numpy as jnp
import numpy as np
from jax import lax
from jax.experimental import pallas as pl
from jax.experimental.pallas import tpu as pltpu
from jax.sharding import PartitionSpec as P
NT=(((1,),(1,)),((),()))
NN=(((1,),(0,)),((),()))
LOG2E=1.4426950408889634
MIB=1024*1024
TN=(((0,),(0,)),((),()))
MESH=pl.DeviceIdType.MESH
EPSILON=1e-06
BOTH=("exp","seq")

def lane_iota(rows):
    return lax.broadcasted_iota(jnp.int32,(rows,128),1)

def dup_head(values,head):
    values=values.astype(jnp.float32)
    turned=pltpu.roll(values,64,1)
    low=lane_iota(values.shape[0])<64
    return jnp.where(low,values,turned) if head==0 else jnp.where(low,turned,values)

def three_parts(column):
    first=column.astype(jnp.bfloat16).astype(jnp.float32)
    rest=column-first
    second=rest.astype(jnp.bfloat16).astype(jnp.float32)
    return first,second,rest-second

def columns_at(lanes,start,parts,other):
    out=other
    for place,part in enumerate(parts):
        out=jnp.where(lanes==start+place,part,out)
    return out

def split_query(query,head,scale):
    both=dup_head(query,head)*scale
    high=both.astype(jnp.bfloat16).astype(jnp.float32)
    return jnp.where(lane_iota(query.shape[0])<64,high,both-high).astype(jnp.bfloat16)

def fill_strip(strip,vector,rows,width):
    full=width+rows
    step=8
    spread=jnp.broadcast_to(vector,(rows,full))
    turned=pltpu.roll(spread,0,1,stride=1,stride_axis=0)
    strip[...]=turned[:,rows:]


def head_column(values,index):
    return jnp.sum(jnp.where(lane_iota(values.shape[0])==index,values,0.0),axis=1,keepdims=True)

def remote(src,dst,sent,received,target):
    return pltpu.make_async_remote_copy(src_ref=src,dst_ref=dst,send_sem=sent,recv_sem=received,device_id=target,device_id_type=MESH)

def loop(first,last,body):
    def step(i,carry):
        body(i)
        return carry
    lax.fori_loop(first,last,step,0)

class Spread:
    def __init__(self,axes,seq_count,groups,source,slot,direct,passed,received,own):
        self.me,self.place=axes
        self.counts=(seq_count,groups)
        self.source,self.slot=source,slot
        self.direct,self.passed,self.received,self.own=direct,passed,received,own
        self.sequence,self.group=self.place//groups,self.place%groups
    def at(self,sequence_step,group_step):
        seq_count,groups=self.counts
        return lax.rem(self.sequence+sequence_step,seq_count)*groups+lax.rem(self.group+group_step,groups)
    def copies(self):
        seq_count,groups=self.counts
        targets=[self.at(i,0) for i in range(1,seq_count)]+[self.at(0,i) for i in range(1,groups)]
        return [remote(self.source(target//groups),self.slot(self.place),self.direct.at[i],self.received.at[self.place],(self.me,target)) for i,target in enumerate(targets)]
    def local(self):
        return pltpu.make_async_copy(self.source(self.sequence),self.slot(self.place),self.own)
    def landed(self,place):
        landing=self.slot(place)
        remote(landing,landing,self.own,self.received.at[place],(self.me,self.place)).wait_recv()
    def relays(self):
        seq_count,groups=self.counts
        out=[]
        for i in range(1,seq_count):
            part=self.at(i,0)
            for j in range(1,groups):
                index=(i-1)*(groups-1)+j-1
                out.append(remote(self.slot(part),self.slot(part),self.passed.at[index],self.received.at[part],(self.me,self.at(0,j))))
        return out
    def start(self):
        self.local().start()
        for copy in self.copies():
            copy.start()
    def relay(self):
        seq_count,groups=self.counts
        for i in range(1,seq_count):
            self.landed(self.at(i,0))
        for copy in self.relays():
            copy.start()
    def finish(self):
        seq_count,groups=self.counts
        for j in range(1,groups):
            for i in range(seq_count):
                self.landed(self.at(i,j))
        for copy in self.copies()+self.relays():
            copy.wait_send()
        self.local().wait()

def spread_semaphores(seq_count,groups):
    dma=lambda n: pltpu.SemaphoreType.DMA((n,))
    return [dma(seq_count+groups-2),dma(max((seq_count-1)*(groups-1),1)),dma(seq_count*groups),pltpu.SemaphoreType.DMA]

def start_kernel(plan,rows,span,token_ref,unit_ref,w1_ref,pos_ref,cot_ref,proj_ref,normed_ref,cot_rows_ref,own_out,w1_out,
                 tok,scaled,units,land,s_unit,r_unit,s_block,r_block,s_pass,own_sem,*spread_sems):
    experts,seq_devs,seq_count,stretch,heads,chunks=plan
    groups=seq_devs//seq_count
    length=stretch*seq_devs
    f32,b16=jnp.float32,jnp.bfloat16
    me,place=lax.axis_index("exp"),lax.axis_index("seq")
    pairs=experts//2
    pair,side=me//2,me%2
    other=1-side
    block=seq_devs*rows
    quarter=w1_ref.shape[2]
    def device(offset,member):
        return lax.rem(pair+offset+pairs,pairs)*2+member
    barrier=pltpu.get_barrier_semaphore()
    for i in range(1,experts):
        pl.semaphore_signal(barrier,inc=1,device_id=(lax.rem(me+i,experts),place),device_id_type=MESH)
    for i in range(1,seq_devs):
        pl.semaphore_signal(barrier,inc=1,device_id=(me,lax.rem(place+i,seq_devs)),device_id_type=MESH)
    def stretch_of(owner):
        return tok.at[pl.ds(pl.multiple_of(owner*stretch,128),stretch)]
    def part_of(owner):
        return w1_out.at[:,pl.ds(pl.multiple_of(owner*quarter,128),quarter)]
    tokens=Spread((me,place),seq_count,groups,lambda n: token_ref.at[n],stretch_of,*spread_sems[:4])
    firsts=Spread((me,place),seq_count,groups,lambda n: w1_ref.at[0],part_of,*spread_sems[4:])
    own_unit=pltpu.make_async_copy(unit_ref.at[place%groups],units.at[place],own_sem.at[0])
    own_unit.start()
    pl.semaphore_wait(barrier,experts+seq_devs-2)
    def send_unit(i):
        target=lax.rem(place+i,seq_devs)
        return remote(unit_ref.at[target%groups],units.at[place],s_unit.at[i],r_unit.at[place],(me,target))
    for i in range(1,seq_devs):
        send_unit(i).start()
    tokens.start()
    firsts.start()
    def landed(landing,received):
        remote(landing,landing,own_sem.at[1],received,(me,place)).wait_recv()
    own_unit.wait()
    for i in range(1,seq_devs):
        source=lax.rem(place+i,seq_devs)
        landed(units.at[source],r_unit.at[source])
    def block_of(owner):
        return land.at[pl.ds(pl.multiple_of(owner*block,16),block)]
    joined=jnp.concatenate([units[i].astype(f32)[:rows] for i in range(seq_devs)],axis=0)
    land[pl.ds(pl.multiple_of(me*block,16),block),:]=joined.astype(b16)
    visit=[j for step in range(1,pairs//2+1) for j in sorted({step,pairs-step})]
    def send_block(j,member,index):
        return remote(block_of(me),block_of(me),s_block.at[index],r_block.at[me],(device(j,member),place))
    sends=[send_block(0,other,0)]+[send_block(j,side,j) for j in visit]
    for copy in sends:
        copy.start()
    passes=[remote(block_of(device(j,side)),block_of(device(j,side)),s_pass.at[j],r_block.at[device(j,side)],(device(0,other),place)) for j in visit]
    for j,copy in zip(visit,passes):
        landed(block_of(device(j,side)),r_block.at[device(j,side)])
        copy.start()
    cap=cot_rows_ref.shape[1]
    def place_rows(expert):
        slots=lax.broadcasted_iota(jnp.int32,(cap,pos_ref.shape[1]),0)+expert*cap
        hot=(slots==pos_ref[...]).astype(f32).astype(b16)
        cot_rows_ref[expert]=jnp.dot(hot,cot_ref[...],preferred_element_type=f32).astype(b16)
    loop(0,experts,place_rows)
    piece=512 if length%512==0 else 128
    tokens.relay()
    tokens.finish()
    def scale_rows(step):
        part=pl.ds(pl.multiple_of(step*piece,piece),piece)
        x=tok[part,:].astype(f32)
        scaled[part,:]=x*lax.rsqrt(jnp.mean(x*x,axis=-1,keepdims=True)+EPSILON)
    loop(0,length//piece,scale_rows)
    for j in [0]+visit:
        landed(block_of(device(j,other)),r_block.at[device(j,other)])
    own_copy=pltpu.make_async_copy(land,own_out,own_sem.at[2])
    own_copy.start()
    gain=jnp.transpose(land[:,span:].astype(f32))[experts:experts+1,:]
    def project(step):
        part=pl.ds(pl.multiple_of(step*piece,piece),piece)
        normed=(scaled[part,:]*gain).astype(b16)
        normed_ref[part,:]=normed
        proj_ref[part,:]=jnp.dot(normed,land[:,:span],preferred_element_type=f32).astype(b16)
    loop(0,length//piece,project)
    firsts.relay()
    own_copy.wait()
    firsts.finish()
    for copy in sends+passes:
        copy.wait_send()
    for i in range(1,seq_devs):
        send_unit(i).wait_send()

def gather_start(plan,rows,tokens,units,expert_in,position,cotangent,cap):
    experts,seq_devs,seq_count,stretch,heads,chunks=plan
    groups=seq_devs//seq_count
    length=stretch*seq_devs
    width=tokens.shape[2]
    span=chunk_span(heads)*chunks
    b16=jnp.bfloat16
    vmem=pl.BlockSpec(memory_space=pltpu.VMEM)
    anywhere=pl.BlockSpec(memory_space=pl.ANY)
    dma=lambda n: pltpu.SemaphoreType.DMA((n,))
    shape=lambda *dims: jax.ShapeDtypeStruct(dims,b16)
    return pl.pallas_call(
        functools.partial(start_kernel,plan,rows,span),
        in_specs=[anywhere,anywhere,vmem,vmem,vmem],
        out_specs=[vmem,vmem,vmem,anywhere,anywhere],
        out_shape=[shape(length,span),shape(length,width),shape(experts,cap,width),shape(width,span+128),shape(width,expert_in.shape[2]*seq_devs)],
        scratch_shapes=[pltpu.VMEM((length,width),b16),pltpu.VMEM((length,width),jnp.float32),pltpu.VMEM((seq_devs,)+units.shape[1:],b16),pltpu.VMEM((width,span+128),b16),
            dma(seq_devs),dma(seq_devs),dma(experts),dma(experts),dma(experts),dma(3)]+spread_semaphores(seq_count,groups)*2,
        compiler_params=pltpu.CompilerParams(collective_id=3,has_side_effects=True,vmem_limit_bytes=40*MIB),
        cost_estimate=pl.CostEstimate(flops=2*length*width*span,bytes_accessed=24*MIB,transcendentals=0),
        name="gather_start",
    )(tokens,units,expert_in,position,cotangent)

def one_hot_rows(ids):
    return (lax.broadcasted_iota(jnp.int32,(128,ids.shape[1]),0)==ids).astype(jnp.float32).astype(jnp.bfloat16)

def stack_parts(values):
    return jnp.concatenate(three_parts(values),axis=0).astype(jnp.bfloat16)

def join_parts(product):
    rows=product.shape[0]//3
    return product[:rows]+product[rows:2*rows]+product[2*rows:]

def table_rows(table,hot):
    return join_parts(jnp.dot(stack_parts(table),hot,preferred_element_type=jnp.float32))

def chunk_span(heads):
    return 128*(1+heads)

def forward_kernel(plan,block,srows,scale,proj_ref,ids_ref,rows_ref,cot_ref,own_ref,w2_ref,att_out,o32_ref,lse_ref,cot_out,all_out,w2_out,strip,bias_ref,kd,va,scr,outs,s_cot,r_cot,s_att,r_att,s_all,r_all,local_sem,*spread_sems):
    experts,seq_devs,seq_count,stretch,heads,chunks=plan
    length=stretch*seq_devs
    groups=seq_devs//seq_count
    f32,b16=jnp.float32,jnp.bfloat16
    me,place=lax.axis_index("exp"),lax.axis_index("seq")
    sequence,group=place//groups,place%groups
    barrier=pltpu.get_barrier_semaphore()
    loop(1,experts,lambda i: pl.semaphore_signal(barrier,inc=1,device_id=(lax.rem(me+i,experts),place),device_id_type=MESH))
    loop(1,seq_devs,lambda i: pl.semaphore_signal(barrier,inc=1,device_id=(me,lax.rem(place+i,seq_devs)),device_id_type=MESH))
    own_cot=pltpu.make_async_copy(cot_ref.at[me],cot_out.at[me],local_sem.at[0])
    own_cot.start()
    own_all=pltpu.make_async_copy(own_ref,all_out.at[group],local_sem.at[1+chunks])
    own_all.start()
    deep=w2_ref.shape[1]
    seconds=Spread((me,place),seq_count,groups,lambda n: w2_ref.at[0],lambda owner: w2_out.at[pl.ds(pl.multiple_of(owner*deep,128),deep)],*spread_sems)
    pl.semaphore_wait(barrier,experts+seq_devs-2)
    seconds.start()
    def send_all(i):
        return remote(own_ref,all_out.at[group],s_all.at[i],r_all.at[i],(me,sequence*groups+lax.rem(group+i,groups)))
    loop(1,groups,lambda i: send_all(i).start())
    def send_cot(i):
        target=lax.rem(me+i,experts)
        return remote(cot_ref.at[target],cot_out.at[me],s_cot.at[i],r_cot.at[i],(target,place))
    loop(1,experts,lambda i: send_cot(i).start())
    def lanes_of(owner_group,c,size):
        return pl.ds(pl.multiple_of((owner_group*chunks+c)*size,128),size)
    def send_att(c,i):
        target=lax.rem(place+i,seq_devs)
        rows=pl.ds(pl.multiple_of(target*stretch,128),stretch)
        return remote(outs.at[c,rows],att_out.at[sequence,:,lanes_of(group,c,128)],s_att.at[c,i],r_att.at[c,i],(me,target))
    def own_att(c):
        rows=pl.ds(pl.multiple_of(place*stretch,128),stretch)
        return pltpu.make_async_copy(outs.at[c,rows],att_out.at[sequence,:,lanes_of(group,c,128)],local_sem.at[1+c])
    width=strip.shape[1]
    wide=256
    blocks=length//block
    pieces=length//wide
    lanes=lane_iota(length)
    block_lanes=lane_iota(block)
    lse_ref[...]=jnp.zeros_like(lse_ref)
    bias_ref[...]=table_rows(rows_ref[...],one_hot_rows(ids_ref[...]))
    def attend_head(c,head):
        index=c*heads+head
        def columns(which):
            return slice(c*chunk_span(heads)+which*128,c*chunk_span(heads)+(which+1)*128)
        own=slice(c*128,(c+1)*128)
        fill_strip(strip,bias_ref[index:index+1,:],srows,width)
        kd[...]=dup_head(proj_ref[:,columns(1+head)],0).astype(b16)
        va[...]=jnp.where(lanes<64,dup_head(proj_ref[:,columns(1+head)],1),jnp.where(lanes==64,1.0,0.0)).astype(b16)
        def rows_of(step):
            return slice(step*block,(step+1)*block)
        def score_piece(step,qa,p,slot,top):
            raw=lax.dot_general(qa,kd[p*wide:(p+1)*wide,:],NT,preferred_element_type=f32)
            parts=[]
            for part in range(block//srows):
                start=length-srows-step*block-part*srows+p*wide
                parts.append(raw[part*srows:(part+1)*srows]+strip[:,pl.ds(start,wide)])
            scores=jnp.concatenate(parts,axis=0)
            scr[slot,:,p*wide:(p+1)*wide]=scores
            for j in range(wide//128):
                top=jnp.maximum(top,scores[:,j*128:(j+1)*128])
            return top
        def mix_piece(slot,p,top,total):
            weights=jnp.exp2(scr[slot,:,p*wide:(p+1)*wide]-top).astype(b16)
            return total+jnp.dot(weights,va[p*wide:(p+1)*wide,:],preferred_element_type=f32)
        def finish(step,top,mixed):
            rows=rows_of(step)
            total=mixed[:,64:65]
            result=mixed/total
            lse_ref[rows,:]=jnp.where(block_lanes==index,top+jnp.log2(total),lse_ref[rows,:])
            if head:
                result=jnp.where(block_lanes<64,o32_ref[rows,own],pltpu.roll(result,64,1))
            o32_ref[rows,own]=result
            if head==heads-1:
                outs[c,rows]=result.astype(b16)
        def send_steps(first,last):
            for part in range(first*block//stretch,last*block//stretch):
                distance=lax.rem(part-place+seq_devs,seq_devs)
                @pl.when(distance==0)
                def _():
                    own_att(c).start()
                @pl.when(distance!=0)
                def _():
                    send_att(c,distance).start()
        def advance(step,slot,top):
            mixing=top is not None
            qa=split_query(proj_ref[rows_of(step),columns(0)],head,scale)
            new=jnp.full((block,128),-jnp.inf,f32)
            mixed=jnp.zeros((block,128),f32)
            for p in range(pieces):
                new=score_piece(step,qa,p,slot,new)
                if mixing:
                    mixed=mix_piece(1-slot,p,top,mixed)
            if mixing:
                finish(step-1,top,mixed)
            return jnp.max(new,axis=1,keepdims=True)
        top=None
        for step in range(blocks):
            top=advance(step,step%2,top)
        if head==heads-1:
            send_steps(0,blocks-1)
        mixed=jnp.zeros((block,128),f32)
        for p in range(pieces):
            mixed=mix_piece((blocks-1)%2,p,top,mixed)
        finish(blocks-1,top,mixed)
        if head==heads-1:
            send_steps(blocks-1,blocks)
    for c in range(chunks):
        for head in range(heads):
            attend_head(c,head)
    seconds.relay()
    def land_att(c,i):
        source=lax.rem(place-i+seq_devs,seq_devs)
        landing=att_out.at[source//groups,:,lanes_of(source%groups,c,128)]
        remote(landing,landing,s_att.at[c,i],r_att.at[c,i],(me,place)).wait_recv()
    def finish_chunk(c):
        own_att(c).wait()
        loop(1,seq_devs,lambda i: land_att(c,i))
        loop(1,seq_devs,lambda i: send_att(c,i).wait_send())
    loop(0,chunks,finish_chunk)
    def land_cot(i):
        landing=cot_out.at[lax.rem(me-i+experts,experts)]
        remote(landing,landing,s_cot.at[i],r_cot.at[i],(me,place)).wait_recv()
    loop(1,experts,land_cot)
    loop(1,experts,lambda i: send_cot(i).wait_send())
    def land_all(i):
        landing=all_out.at[lax.rem(group-i+groups,groups)]
        remote(landing,landing,s_all.at[i],r_all.at[i],(me,place)).wait_recv()
        send_all(i).wait_send()
    loop(1,groups,land_all)
    own_all.wait()
    own_cot.wait()
    seconds.finish()

def attend(plan,projected,ids,table,cot_rows,own_weight,expert_out,block=512,srows=128):
    experts,seq_devs,seq_count,stretch,heads,chunks=plan
    length=stretch*seq_devs
    groups=seq_devs//seq_count
    f32,b16=jnp.float32,jnp.bfloat16
    vmem=pl.BlockSpec(memory_space=pltpu.VMEM)
    anywhere=pl.BlockSpec(memory_space=pl.ANY)
    dma=lambda *shape: pltpu.SemaphoreType.DMA(shape)
    return pl.pallas_call(
        functools.partial(forward_kernel,plan,block,srows,LOG2E/8),
        in_specs=[vmem,vmem,vmem,anywhere,vmem,vmem],
        out_specs=[anywhere,vmem,vmem]+[anywhere]*3,
        out_shape=[jax.ShapeDtypeStruct((seq_count,stretch,groups*chunks*128),b16),jax.ShapeDtypeStruct((length,chunks*128),f32),jax.ShapeDtypeStruct((length,128),f32),jax.ShapeDtypeStruct(cot_rows.shape,b16),jax.ShapeDtypeStruct((groups,)+own_weight.shape,b16),jax.ShapeDtypeStruct((expert_out.shape[1]*seq_devs,expert_out.shape[2]),b16)],
        scratch_shapes=[pltpu.VMEM((srows,2*length-srows),f32),pltpu.VMEM((table.shape[0],2*length),f32),pltpu.VMEM((length,128),b16),pltpu.VMEM((length,128),b16),pltpu.VMEM((2,block,length),f32),pltpu.VMEM((chunks,length,128),b16),
            dma(experts),dma(experts),dma(chunks,seq_devs),dma(chunks,seq_devs),dma(groups),dma(groups),dma(2+chunks)]+spread_semaphores(seq_count,groups),
        compiler_params=pltpu.CompilerParams(collective_id=1,has_side_effects=True,vmem_limit_bytes=48*MIB),
        cost_estimate=pl.CostEstimate(flops=16*heads*chunks*length*length*64,bytes_accessed=16*MIB,transcendentals=heads*chunks*length*length),
        name="attend_forward",
    )(projected,ids,table,cot_rows,own_weight,expert_out)

def backward_kernel(plan,inside,bq,bk,srows,scale,proj_ref,o32_ref,lse_ref,ids_ref,rows_ref,normed_ref,up_ref,res_ref,piece_ref,
                    grad_out,ret_out,piece_out,weight_out,table_out,
                    strip,grads,kk,kt,qa,da,qd,dkv_acc,lse_t,delta,ups,outs,weight_parts,piece_parts,piece_land,diag,table,normed_t,hot,bias_ref,
                    s_up,r_up,s_res,r_res,s_piece,r_piece,s_grad,r_grad,s_weight,r_weight,s_half,r_half,s_table,r_table,local_sem,own_sem):
    experts,seq_devs,seq_count,stretch,heads,chunks=plan
    length=stretch*seq_devs
    groups=seq_devs//seq_count
    devices=experts*seq_devs
    f32,b16=jnp.float32,jnp.bfloat16
    me,place=lax.axis_index("exp"),lax.axis_index("seq")
    sequence,group=place//groups,place%groups
    rank=me*seq_devs+place
    def other(i):
        target=lax.rem(rank+i,devices)
        return target,(target//seq_devs,target%seq_devs)
    barrier=pltpu.get_barrier_semaphore()
    loop(1,devices,lambda i: pl.semaphore_signal(barrier,inc=1,device_id=other(i)[1],device_id_type=MESH))
    def lanes_of(owner_group,c,size):
        return pl.ds(pl.multiple_of((owner_group*chunks+c)*size,128),size)
    def rows_of(owner):
        return pl.ds(pl.multiple_of(owner*stretch,128),stretch)
    def send_up(c,i):
        target=lax.rem(place+i,seq_devs)
        return remote(up_ref.at[target//groups,:,lanes_of(target%groups,c,128)],ups.at[c,rows_of(place)],s_up.at[c,i],r_up.at[c,i],(me,target))
    def own_up(c):
        return pltpu.make_async_copy(up_ref.at[sequence,:,lanes_of(group,c,128)],ups.at[c,rows_of(place)],local_sem.at[0,c])
    def send_res(i):
        target=lax.rem(me+i,experts)
        return remote(res_ref.at[target],ret_out.at[me],s_res.at[i],r_res.at[i],(target,place))
    half=experts*seq_count
    spot=me*seq_count+sequence
    def fellow(i):
        target=lax.rem(spot+i,half)
        return target,(target//seq_count,(target%seq_count)*groups+group)
    def half_piece(i):
        target=lax.rem(group+i,groups)
        return remote(piece_ref.at[target],piece_land.at[i-1],s_half.at[i],r_half.at[i],(me,sequence*groups+target))
    own_piece=pltpu.make_async_copy(piece_ref.at[group],piece_parts,own_sem.at[2])
    def send_piece(i):
        target,where=fellow(i)
        return remote(piece_parts.at[target],piece_out.at[spot],s_piece.at[i],r_piece.at[i],where)
    keep_piece=pltpu.make_async_copy(piece_parts.at[spot],piece_out.at[spot],own_sem.at[4])
    def meet_pieces():
        own_piece.wait()
        for j in range(1,groups):
            landed(piece_land.at[j-1],r_half.at[j])
        def add(i):
            total=piece_parts[i].astype(f32)
            for j in range(1,groups):
                total=total+piece_land[j-1,i].astype(f32)
            piece_parts[i]=total.astype(b16)
        loop(0,half,add)
        loop(1,half,lambda i: send_piece(i).start())
        keep_piece.start()
    def grad_lanes(owner_group,c,part):
        return pl.ds(pl.multiple_of((owner_group*chunks+c)*chunk_span(heads)+part*128,128),128)
    def send_grad(c,part,i):
        target=lax.rem(place+i,seq_devs)
        return remote(outs.at[c,rows_of(target),part*128:(part+1)*128],grad_out.at[sequence,:,grad_lanes(group,c,part)],s_grad.at[c,part,i],r_grad.at[c,part,i],(me,target))
    def own_grad(c,part):
        return pltpu.make_async_copy(outs.at[c,rows_of(place),part*128:(part+1)*128],grad_out.at[sequence,:,grad_lanes(group,c,part)],local_sem.at[2+part,c])
    def send_weight(c,i):
        target,where=other(i)
        return remote(weight_parts.at[c,target],weight_out.at[c,rank],s_weight.at[c,i],r_weight.at[c,i],where)
    def own_weight(c):
        return pltpu.make_async_copy(weight_parts.at[c,rank],weight_out.at[c,rank],local_sem.at[1,c])
    def send_table(i):
        return remote(table,table_out.at[rank],s_table.at[i],r_table.at[i],other(i)[1])
    own_table=pltpu.make_async_copy(table,table_out.at[rank],own_sem.at[0])
    own_res=pltpu.make_async_copy(res_ref.at[me],ret_out.at[me],own_sem.at[1])
    def landed(landing,received):
        remote(landing,landing,own_sem.at[3],received,(me,place)).wait_recv()
    own_res.start()
    own_piece.start()
    loop(0,chunks,lambda c: own_up(c).start())
    pl.semaphore_wait(barrier,devices-1)
    loop(1,seq_devs,lambda i: send_up(0,i).start())
    width=strip.shape[1]
    full_width=2*length
    lanes=lane_iota(length)
    count=length//bk
    if inside:
        weight_parts[...]=jnp.zeros_like(weight_parts)
        normed_t[...]=jnp.transpose(normed_ref[...])
    diag[...]=jnp.zeros_like(diag)
    lse_t[...]=jnp.transpose(lse_ref[...])
    hot[...]=one_hot_rows(ids_ref[...])
    bias_ref[...]=table_rows(rows_ref[...],hot[...])
    def head_back(c,head):
        index=c*heads+head
        def columns(which):
            return pl.ds(pl.multiple_of(c*chunk_span(heads)+which*128,128),128)
        query,both=proj_ref[:,columns(0)],proj_ref[:,columns(1+head)]
        fill_strip(strip,bias_ref[pl.ds(index,1),:],srows,width)
        grads[...]=jnp.zeros_like(grads)
        low_lanes=lanes<64
        kk[:,:128]=both
        kk[:,128:]=both
        kt[...]=jnp.transpose(both)
        query=query.astype(f32)
        query=jnp.where(low_lanes,pltpu.roll(query,64,1) if head else query,0.0)
        scaled=query*scale
        high=scaled.astype(b16).astype(f32)
        qa[:,:128]=high.astype(b16)
        qa[:,128:]=(scaled-high).astype(b16)
        qd[...]=(query*0.125).astype(b16)
        if head==0:
            take_up(c)
            products_sum=ups[c].astype(f32)*o32_ref[:,pl.ds(pl.multiple_of(c*128,128),128)]
            halves=lax.broadcasted_iota(jnp.int32,(8,128),0)==lax.broadcasted_iota(jnp.int32,(8,128),1)//64
            halves=halves.astype(f32).astype(b16)
            delta[...]=sum(lax.dot_general(halves,part.astype(b16),NT,preferred_element_type=f32) for part in three_parts(products_sum))
        upstream=ups[c].astype(f32)
        da[...]=jnp.where(low_lanes,0.0,upstream if head else pltpu.roll(upstream,64,1)).astype(b16)
        dkv_acc[...]=jnp.zeros_like(dkv_acc)
        def query_block(qb):
            qs=pl.ds(pl.multiple_of(qb*bq,bq),bq)
            def products(kb):
                ks=slice(kb*bk,(kb+1)*bk)
                raw=lax.dot_general(kk[ks,:],qa[qs,:],NT,preferred_element_type=f32)
                up=lax.dot_general(kk[ks,:128],da[qs,:],NT,preferred_element_type=f32)
                return raw,up
            log_row=lse_t[pl.ds(index,1),qs]
            delta_row=delta[head:head+1,qs]
            def consume(kb,raw,up,dq):
                ks=slice(kb*bk,(kb+1)*bk)
                probs,score_grads=[],[]
                for part in range(bk//srows):
                    start=qb*bq+(length-srows)-kb*bk-part*srows
                    rows=slice(part*srows,(part+1)*srows)
                    prob=jnp.exp2(raw[rows]+strip[:,pl.ds(pl.multiple_of(start,128),bq)]-log_row)
                    grad=prob*(up[rows]-delta_row)
                    grads[:,pl.ds(pl.multiple_of(start+srows,128),bq)]+=grad
                    probs.append(prob.astype(b16))
                    score_grads.append(grad.astype(b16))
                low=jnp.concatenate(score_grads,axis=0)
                dkv_acc[ks,:]+=jnp.dot(jnp.concatenate(probs,axis=0),da[qs,:],preferred_element_type=f32)+jnp.dot(low,qd[qs,:],preferred_element_type=f32)
                return dq+jnp.dot(kt[:,ks],low,preferred_element_type=f32)
            dq=jnp.zeros((128,bq),f32)
            ready=products(0)
            for kb in range(count):
                following=products(kb+1) if kb+1<count else None
                dq=consume(kb,*ready,dq)
                ready=following
            dq=jnp.transpose(dq)*0.125
            if head:
                dq=jnp.where(lane_iota(bq)<64,outs[c,qs,0:128].astype(f32),pltpu.roll(dq,64,1))
            outs[c,qs,0:128]=dq.astype(b16)
            if head==heads-1:
                for part in range(bq//stretch):
                    distance=lax.rem(qb*(bq//stretch)+part-place+seq_devs,seq_devs)
                    @pl.when(distance==0)
                    def _():
                        own_grad(c,0).start()
                    @pl.when(distance!=0)
                    def _():
                        send_grad(c,0,distance).start()
        loop(0,length//bq,query_block)
        outs[c,:,128*(1+head):128*(2+head)]=dkv_acc[...].astype(b16)
        loop(1,seq_devs,lambda i: send_grad(c,1+head,i).start())
        own_grad(c,1+head).start()
        total=grads[0:8,:]
        for part in range(1,srows//8):
            total=total+pltpu.roll(grads[8*part:8*part+8,:],full_width-8*part,1)
        row=lax.broadcasted_iota(jnp.int32,(8,full_width),0)
        for part in range(1,8):
            total=jnp.where(row==part,pltpu.roll(total,full_width-part,1),total)
        diag[pl.ds(index,1),:]=jnp.sum(total,axis=0,keepdims=True)
    def take_up(c):
        loop(1,seq_devs,lambda i: landed(ups.at[c,rows_of(lax.rem(place-i+seq_devs,seq_devs))],r_up.at[c,i]))
        own_up(c).wait()
        @pl.when(c==0)
        def _():
            loop(1,chunks,lambda later: loop(1,seq_devs,lambda i: send_up(later,i).start()))
            loop(1,groups,lambda i: half_piece(i).start())
            loop(1,experts,lambda i: send_res(i).start())
    def one_chunk(c):
        for head in range(heads):
            head_back(c,head)
            if head==0:
                @pl.when(c==0)
                def _():
                    meet_pieces()
        if inside:
            part=jnp.dot(normed_t[...],outs[c],preferred_element_type=f32)
            block=normed_t.shape[0]//devices
            weight_parts[c,:,:block,:]=part.reshape(devices,block,chunk_span(heads)).astype(b16)
            loop(1,devices,lambda i: send_weight(c,i).start())
            own_weight(c).start()
    loop(0,chunks,one_chunk)
    table[...]=join_parts(lax.dot_general(stack_parts(diag[...]),hot[...],NT,preferred_element_type=f32))
    loop(1,devices,lambda i: send_table(i).start())
    own_table.start()
    def finish_chunk(c):
        def grad_landed(i):
            source=lax.rem(place-i+seq_devs,seq_devs)
            for part in range(1+heads):
                landed(grad_out.at[source//groups,:,grad_lanes(source%groups,c,part)],r_grad.at[c,part,i])
                send_grad(c,part,i).wait_send()
            send_up(c,i).wait_send()
        loop(1,seq_devs,grad_landed)
        for part in range(1+heads):
            own_grad(c,part).wait()
        if inside:
            def weight_landed(i):
                landed(weight_out.at[c,lax.rem(rank-i+devices,devices)],r_weight.at[c,i])
                send_weight(c,i).wait_send()
            loop(1,devices,weight_landed)
            own_weight(c).wait()
    loop(0,chunks,finish_chunk)
    def res_landed(i):
        landed(ret_out.at[lax.rem(me-i+experts,experts)],r_res.at[i])
        send_res(i).wait_send()
    loop(1,experts,res_landed)
    def piece_landed(i):
        landed(piece_out.at[lax.rem(spot-i+half,half)],r_piece.at[i])
        send_piece(i).wait_send()
    loop(1,half,piece_landed)
    def table_landed(i):
        landed(table_out.at[lax.rem(rank-i+devices,devices)],r_table.at[i])
        send_table(i).wait_send()
    loop(1,devices,table_landed)
    own_res.wait()
    loop(1,groups,lambda i: half_piece(i).wait_send())
    keep_piece.wait()
    own_table.wait()

def attend_back(plan,projected,o32,lse,ids,table,normed,upstream,result,piece,bq=512,bk=512,srows=128):
    experts,seq_devs,seq_count,stretch,heads,chunks=plan
    length=stretch*seq_devs
    groups=seq_devs//seq_count
    devices=experts*seq_devs
    block=normed.shape[1]//devices
    inside=block%8==0
    rows=(block+15)//16*16
    f32,b16=jnp.float32,jnp.bfloat16
    vm=lambda kind,*shape: pltpu.VMEM(shape,kind)
    vmem=pl.BlockSpec(memory_space=pltpu.VMEM)
    anywhere=pl.BlockSpec(memory_space=pl.ANY)
    dma=lambda *shape: pltpu.SemaphoreType.DMA(shape)
    shape=lambda kind,*dims: jax.ShapeDtypeStruct(dims,kind)
    weight_shape=(chunks,devices,rows,chunk_span(heads)) if inside else (1,1,16,128)
    return pl.pallas_call(
        functools.partial(backward_kernel,plan,inside,bq,bk,srows,LOG2E/8),
        in_specs=[vmem]*6+[anywhere]*3,
        out_specs=[anywhere]*5,
        out_shape=[shape(b16,seq_count,stretch,groups*chunks*chunk_span(heads)),shape(b16,*result.shape),shape(b16,*piece.shape[1:]),shape(b16,*weight_shape),shape(f32,devices,table.shape[0],128)],
        scratch_shapes=[vm(f32,srows,2*length-srows),vm(f32,srows,2*length),vm(b16,length,256),vm(b16,128,length),vm(b16,length,256),vm(b16,length,128),
            vm(b16,length,128),vm(f32,length,128),vm(f32,128,length),vm(f32,8,length),
            vm(b16,chunks,length,128),vm(b16,chunks,length,chunk_span(heads)),vm(b16,*weight_shape),vm(b16,*piece.shape[1:]),vm(b16,max(groups-1,1),*piece.shape[1:]),vm(f32,table.shape[0],2*length),vm(f32,table.shape[0],128),vm(b16,normed.shape[1],length),vm(b16,128,2*length),vm(f32,table.shape[0],2*length),
            dma(chunks,seq_devs),dma(chunks,seq_devs),dma(experts),dma(experts),dma(experts*seq_count),dma(experts*seq_count),dma(chunks,1+heads,seq_devs),dma(chunks,1+heads,seq_devs),
            dma(chunks,devices),dma(chunks,devices),dma(groups),dma(groups),dma(devices),dma(devices),dma(3+heads,chunks),dma(5)],
        compiler_params=pltpu.CompilerParams(collective_id=2,has_side_effects=True,vmem_limit_bytes=58*MIB),
        cost_estimate=pl.CostEstimate(flops=40*heads*chunks*length*length*64,bytes_accessed=24*MIB,transcendentals=heads*chunks*length*length),
        name="attend_backward",
    )(projected,o32,lse,ids,table,normed,upstream,result,piece)


def combine_kernel(experts,pos_ref,home_ref,hidden_ref,cot_ref,att_ref,out_w_ref,gain_ref,router_ref,grad_ref,heads_ref,part_ref,total,gain_total):
    f32,b16=jnp.float32,jnp.bfloat16
    step=pl.program_id(0)
    rows=hidden_ref.shape[0]
    slots=home_ref.shape[0]
    width=hidden_ref.shape[1]
    hot=(pos_ref[...]==lax.broadcasted_iota(jnp.int32,(rows,slots),1)).astype(f32).astype(b16)
    moe_in_grad=jnp.dot(hot,home_ref[...],preferred_element_type=f32)
    hidden=hidden_ref[...]
    inverse=lax.rsqrt(jnp.mean(hidden*hidden,axis=-1,keepdims=True)+EPSILON)
    weighted=moe_in_grad*gain_ref[...]
    inner=jnp.mean(weighted*hidden,axis=-1,keepdims=True)
    hidden_grad=cot_ref[...].astype(f32)+weighted*inverse-hidden*(inverse*inverse*inverse)*inner
    grad_ref[...]=hidden_grad
    branch=hidden_grad.astype(b16)
    heads_ref[...]=lax.dot_general(branch,out_w_ref[...],NT,preferred_element_type=f32).astype(b16)
    part=lax.dot_general(att_ref[...],branch,TN,preferred_element_type=f32)
    gain_part=jnp.sum(moe_in_grad*hidden*inverse,axis=0,keepdims=True)
    @pl.when(step==0)
    def _():
        total[...]=part
        gain_total[...]=jnp.broadcast_to(gain_part,gain_total.shape)
    @pl.when(step>0)
    def _():
        total[...]+=part
        gain_total[...]+=gain_part
    @pl.when(step==pl.num_programs(0)-1)
    def _():
        heads_width=total.shape[0]
        part_ref[:,:width]=total[...].astype(b16)
        column=jnp.transpose(jnp.broadcast_to(gain_total[0:1,:],(128,width)))
        lanes=lax.broadcasted_iota(jnp.int32,(width,128),1)
        part_ref[:width,width:]=jnp.where(lanes==experts,column,router_ref[...]).astype(b16)

def combine(experts,position,home,hidden,cotangent,attended,out_full,gain,router_part,block=256):
    count,width=hidden.shape
    heads_width=attended.shape[1]
    f32,b16=jnp.float32,jnp.bfloat16
    block=min(block,count)
    by_rows=lambda columns: pl.BlockSpec((block,columns),lambda i:(i,0))
    whole=lambda value: pl.BlockSpec(value.shape,lambda i:(0,0))
    return pl.pallas_call(
        functools.partial(combine_kernel,experts),
        grid=(count//block,),
        in_specs=[by_rows(1),whole(home),by_rows(width),by_rows(width),by_rows(heads_width),whole(out_full),whole(gain),whole(router_part)],
        out_specs=[by_rows(width),by_rows(heads_width),pl.BlockSpec((heads_width,width+128),lambda i:(0,0))],
        out_shape=[jax.ShapeDtypeStruct((count,width),f32),jax.ShapeDtypeStruct((count,heads_width),b16),jax.ShapeDtypeStruct((heads_width,width+128),b16)],
        scratch_shapes=[pltpu.VMEM((heads_width,width),f32),pltpu.VMEM((8,width),f32)],
        compiler_params=pltpu.CompilerParams(vmem_limit_bytes=40*MIB),
        cost_estimate=pl.CostEstimate(flops=6*count*width*width,bytes_accessed=16*MIB,transcendentals=0),
        name="combine",
    )(position,home,hidden,cotangent,attended,out_full,gain,router_part)

def finish_kernel(experts,groups,heads,chunks,inside,pos_ref,pick_ref,returned_ref,hidden_ref,grad_ref,token_ref,token_grad_ref,every_ref,gains_ref,router_ref,piece_ref,weight_ref,table_ref,first_ref,second_ref,own_ref,own_gain_ref,
                  output_ref,input_ref,first_out,second_out,out_sum,small_sum,query_sum,key_sum,value_sum,gain_sum,table_sum):
    f32,b16=jnp.float32,jnp.bfloat16
    step=pl.program_id(0)
    rows,width=hidden_ref.shape
    row_block=out_sum.shape[0]
    first_out[...]=first_ref[...].astype(f32)
    second_out[...]=second_ref[...].astype(f32)
    slots=returned_ref.shape[0]
    cw=chunk_span(heads)
    span=chunks*cw
    hidden=hidden_ref[...]
    moe_in=(hidden*lax.rsqrt(jnp.mean(hidden*hidden,axis=-1,keepdims=True)+EPSILON)*gains_ref[1:2,:]).astype(b16)
    lanes=lax.broadcasted_iota(jnp.int32,(rows,128),1)
    logits=jnp.where(lanes<experts,jnp.dot(moe_in,router_ref[...],preferred_element_type=f32),-jnp.inf)
    raised=jnp.exp(logits-jnp.max(logits,axis=1,keepdims=True))
    gate=jnp.sum(jnp.where(lanes==pick_ref[...],raised,0.0),axis=1,keepdims=True)/jnp.sum(raised,axis=1,keepdims=True)
    hot=(pos_ref[...]==lax.broadcasted_iota(jnp.int32,(rows,slots),1)).astype(f32).astype(b16)
    output_ref[...]=(hidden+gate*jnp.dot(hot,returned_ref[...],preferred_element_type=f32)).astype(b16)
    normed_grad=jnp.zeros((rows,width),f32)
    for owner in range(groups):
        normed_grad=normed_grad+lax.dot_general(token_grad_ref[:,owner*span:(owner+1)*span],every_ref[owner,:,:span],NT,preferred_element_type=f32)
    x=token_ref[...].astype(f32)
    inverse=lax.rsqrt(jnp.mean(x*x,axis=-1,keepdims=True)+EPSILON)
    weighted=normed_grad*gains_ref[0:1,:]
    inner=jnp.mean(weighted*x,axis=-1,keepdims=True)
    input_ref[...]=grad_ref[...]+weighted*inverse-x*(inverse*inverse*inverse)*inner
    @pl.when(step==0)
    def _():
        devices=piece_ref.shape[0]
        def add_piece(i,total):
            return total+piece_ref[i].astype(f32)
        total=lax.fori_loop(1,devices,add_piece,piece_ref[0].astype(f32))[:row_block]
        out_sum[...]=total[:,:width]
        small_sum[...]=total[:,width:]
        for owner in range(groups):
            def add_table(i,total):
                return total+table_ref[i*groups+owner]
            table_sum[owner]=lax.fori_loop(1,table_ref.shape[0]//groups,add_table,table_ref[owner])
            if inside:
                for c in range(chunks):
                    def add_weight(i,total):
                        return total+weight_ref[c,i*groups+owner].astype(f32)
                    summed=lax.fori_loop(1,weight_ref.shape[1]//groups,add_weight,weight_ref[c,owner].astype(f32))[:row_block]
                    place=slice((owner*chunks+c)*128,(owner*chunks+c+1)*128)
                    query_sum[:,place]=summed[:,0:128]
                    first=summed[:,128:256]
                    second=summed[:,128*heads:128*(heads+1)]
                    low=lane_iota(summed.shape[0])<64
                    key_sum[:,place]=jnp.where(low,first,pltpu.roll(second,64,1))
                    value_sum[:,place]=jnp.where(low,pltpu.roll(first,64,1),second)
        if inside:
            products=query_sum[...]*own_ref[0].astype(f32)+key_sum[...]*own_ref[1].astype(f32)+value_sum[...]*own_ref[2].astype(f32)
            gain_sum[...]=jnp.broadcast_to(jnp.sum(products,axis=1,keepdims=True),gain_sum.shape)/own_gain_ref[...]

def finish(experts,groups,heads,chunks,inside,position,pick,returned,hidden,hidden_grad,tokens,token_grads,every_weight,gains,router,pieces,weights,tables,first,second,own_weights,own_gain,block=256):
    count,width=hidden.shape
    f32,b16=jnp.float32,jnp.bfloat16
    block=min(block,count)
    by_rows=lambda columns: pl.BlockSpec((block,columns),lambda i:(i,0))
    def whole(shape):
        return pl.BlockSpec(shape,lambda i:(0,)*len(shape))
    row_block=own_gain.shape[0]
    sums=jax.ShapeDtypeStruct((row_block,width),f32)
    steps=count//block
    by_steps=lambda value: pl.BlockSpec((value.shape[0]//steps,value.shape[1]),lambda i:(i,0))
    wide=lambda value: jax.ShapeDtypeStruct(value.shape,f32)
    small_shape=jax.ShapeDtypeStruct((row_block,128),f32)
    table_shape=jax.ShapeDtypeStruct((groups,)+tables.shape[1:],f32)
    return pl.pallas_call(
        functools.partial(finish_kernel,experts,groups,heads,chunks,inside),
        grid=(count//block,),
        in_specs=[by_rows(1),by_rows(1),whole(returned.shape),by_rows(width),by_rows(width),by_rows(width),by_rows(token_grads.shape[1]),whole(every_weight.shape),whole(gains.shape),whole(router.shape),whole(pieces.shape),whole(weights.shape),whole(tables.shape),by_steps(first),by_steps(second),whole(own_weights.shape),whole(own_gain.shape)],
        out_specs=[by_rows(width),by_rows(width),by_steps(first),by_steps(second),whole(sums.shape),whole(small_shape.shape)]+[whole(sums.shape)]*3+[whole(small_shape.shape),whole(table_shape.shape)],
        out_shape=[jax.ShapeDtypeStruct((count,width),b16),jax.ShapeDtypeStruct((count,width),f32),wide(first),wide(second),sums,small_shape,sums,sums,sums,small_shape,table_shape],
        compiler_params=pltpu.CompilerParams(vmem_limit_bytes=56*MIB),
        cost_estimate=pl.CostEstimate(flops=8*count*width*width,bytes_accessed=24*MIB,transcendentals=0),
        name="finish",
    )(position,pick,returned,hidden,hidden_grad,tokens,token_grads,every_weight,gains,router,pieces,weights,tables,first,second,own_weights,own_gain)

def gelu_pair(u):
    c=0.7978845608028654
    square=u*u
    t=jnp.tanh(c*u*(1.0+0.044715*square))
    half=0.5*(1.0+t)
    return u*half,half+(0.5*c)*u*(1.0-t*t)*(1.0+0.134145*square)

def expert_kernel(experts,cap,width,hidden_width,send_ref,cot_hbm,w1_hbm,w2_hbm,router_ref,home,result_out,dw1,dw2,router_part,
                  rows,cots,grads,results,row_grads,logit_grads,act,slope,w1,w2,rows_t,
                  local_sem,cot_sem,out_sem,s_rows,r_rows,s_home,r_home):
    f32,b16=jnp.float32,jnp.bfloat16
    pairs=experts//2
    me=lax.axis_index("exp")
    seq=lax.axis_index("seq")
    pair,side=me//2,me%2
    other=1-side
    def device(offset,member):
        return lax.rem(pair+offset+pairs,pairs)*2+member
    barrier=pltpu.get_barrier_semaphore()
    for step in range(1,experts):
        pl.semaphore_signal(barrier,inc=1,device_id=(lax.rem(me+step,experts),seq),device_id_type=MESH)
    load1=pltpu.make_async_copy(w1_hbm,w1,local_sem.at[0])
    load2=pltpu.make_async_copy(w2_hbm,w2,local_sem.at[1])
    own_rows=pltpu.make_async_copy(send_ref.at[me],rows.at[side],local_sem.at[2])
    local=[own_rows,load1,load2]
    cot_loads=[pltpu.make_async_copy(cot_hbm.at[device(-j,m)],cots.at[2*j+m],cot_sem.at[2*j+m]) for j in range(pairs) for m in range(2)]
    for copy in local+cot_loads:
        copy.start()
    pl.semaphore_wait(barrier,experts-1)
    def remote(src,dst,s,r,target):
        return pltpu.make_async_remote_copy(src_ref=src,dst_ref=dst,send_sem=s,recv_sem=r,device_id=(target,seq),device_id_type=MESH)
    started=[]
    def launch(copy):
        copy.start()
        started.append(copy)
    visit=[j for step in range(1,pairs//2+1) for j in sorted({step,pairs-step})]
    launch(remote(send_ref.at[device(0,other)],rows.at[side],s_rows.at[1],r_rows.at[side],device(0,other)))
    for j in visit:
        for m in range(2):
            member=side if m==0 else other
            launch(remote(send_ref.at[device(j,member)],rows.at[2*j+side],s_rows.at[2*j+m],r_rows.at[2*j+side],device(j,member)))
    def wait_slot(landing,r,slot):
        remote(landing,landing,s_rows.at[0],r.at[slot],me).wait_recv()
    chunk=512 if hidden_width%512==0 else 128
    steps=hidden_width//chunk
    lanes=lax.broadcasted_iota(jnp.int32,(2*cap,128),1)
    onehot=jnp.where(lanes==me,1.0,0.0)
    outputs=[]
    def process(j):
        x=rows[2*j:2*j+2].reshape(2*cap,width)
        base=2*j*cap
        span=slice(base,base+2*cap)
        logits=jnp.dot(x,router_ref[...],preferred_element_type=f32)
        logits=jnp.where(lanes<experts,logits,-jnp.inf)
        raised=jnp.exp(logits-jnp.max(logits,axis=1,keepdims=True))
        gates=raised/jnp.sum(raised,axis=1,keepdims=True)
        gate=jnp.sum(gates*onehot,axis=1,keepdims=True)
        for m in range(2):
            cot_loads[2*j+m].wait()
        cot=cots[2*j:2*j+2].reshape(2*cap,width).astype(f32)
        grads[span,:]=(gate*cot).astype(b16)
        def forward(step,carry):
            cols=pl.ds(pl.multiple_of(step*chunk,chunk),chunk)
            pre=jnp.dot(x,w1[:,cols],preferred_element_type=f32)
            a,d=gelu_pair(pre)
            act[span,cols]=a.astype(b16)
            slope[span,cols]=d.astype(b16)
            return carry
        lax.fori_loop(0,steps,forward,0)
        result=jnp.dot(act[span,:],w2[...],preferred_element_type=f32).astype(b16)
        results[2*j:2*j+2]=result.reshape(2,cap,width)
        for m in range(2):
            copy=pltpu.make_async_copy(results.at[2*j+m],result_out.at[device(-j,m)],out_sem.at[2*j+m])
            copy.start()
            outputs.append(copy)
        gate_grad=jnp.sum(cots[2*j:2*j+2].reshape(2*cap,width).astype(f32)*result.astype(f32),axis=1,keepdims=True)
        logit_grad=(gates*(onehot-gate)*gate_grad).astype(b16)
        logit_grads[span,:]=logit_grad
        def backward(step,carry):
            cols=pl.ds(pl.multiple_of(step*chunk,chunk),chunk)
            up=lax.dot_general(grads[span,:],w2[cols,:],NT,preferred_element_type=f32)
            up=up.astype(b16).astype(f32)*slope[span,cols].astype(f32)
            slope[span,cols]=up.astype(b16)
            return carry
        lax.fori_loop(0,steps,backward,0)
        back=lax.dot_general(slope[span,:],w1[...],NT,preferred_element_type=f32)
        back=back+lax.dot_general(logit_grad,router_ref[...],NT,preferred_element_type=f32)
        row_grads[2*j:2*j+2]=back.astype(b16).reshape(2,cap,width)
        for m in range(2):
            member=side if m==0 else other
            if j==0 and m==0:
                copy=pltpu.make_async_copy(row_grads.at[side],home.at[me],local_sem.at[3])
                copy.start()
                outputs.append(copy)
            else:
                launch(remote(row_grads.at[2*j+member],home.at[me],s_home.at[2*j+m],r_home.at[2*j+side],device(-j,member)))
    load1.wait()
    load2.wait()
    own_rows.wait()
    wait_slot(rows.at[other],r_rows,other)
    process(0)
    for j in visit:
        for m in range(2):
            wait_slot(rows.at[2*j+m],r_rows,2*j+m)
        process(j)
    rows_t[...]=jnp.transpose(rows[...].reshape(experts*cap,width))
    router_part[...]=jnp.dot(rows_t[...],logit_grads[...],preferred_element_type=f32)
    def weight_grads(step,carry):
        cols=pl.ds(pl.multiple_of(step*chunk,chunk),chunk)
        dw1[:,cols]=jnp.dot(rows_t[...],slope[:,cols],preferred_element_type=f32).astype(b16)
        dw2[cols,:]=lax.dot_general(act[:,cols],grads[...],TN,preferred_element_type=f32).astype(b16)
        return carry
    lax.fori_loop(0,steps,weight_grads,0)
    for j in range(pairs):
        for m in range(2):
            if j:
                wait_slot(home.at[device(j,m)],r_home,2*j+m)
    wait_slot(home.at[device(0,other)],r_home,other)
    for copy in outputs:
        copy.wait()
    for copy in started:
        copy.wait_send()

def expert_layer(send,cot,w1,w2,router,cid=4):
    experts,cap,width=send.shape
    hidden_width=w1.shape[1]
    b16=jnp.bfloat16
    block=jax.ShapeDtypeStruct((experts,cap,width),b16)
    anywhere=pl.BlockSpec(memory_space=pl.ANY)
    vmem=pl.BlockSpec(memory_space=pltpu.VMEM)
    dma=lambda n: pltpu.SemaphoreType.DMA((n,))
    blocks=pltpu.VMEM((experts,cap,width),b16)
    wide=pltpu.VMEM((experts*cap,hidden_width),b16)
    return pl.pallas_call(
        functools.partial(expert_kernel,experts,cap,width,hidden_width),
        in_specs=[anywhere]*4+[vmem],
        out_specs=[anywhere,anywhere,vmem,vmem,vmem],
        out_shape=[block,block,jax.ShapeDtypeStruct(w1.shape,b16),jax.ShapeDtypeStruct(w2.shape,b16),jax.ShapeDtypeStruct((width,128),jnp.float32)],
        scratch_shapes=[blocks,blocks,pltpu.VMEM((experts*cap,width),b16),blocks,blocks,pltpu.VMEM((experts*cap,128),b16),wide,wide,
            pltpu.VMEM(w1.shape,b16),pltpu.VMEM(w2.shape,b16),pltpu.VMEM((width,experts*cap),b16),
            dma(4)]+[dma(experts)]*6,
        compiler_params=pltpu.CompilerParams(collective_id=cid,has_side_effects=True,vmem_limit_bytes=60*MIB),
        cost_estimate=pl.CostEstimate(flops=12*experts*cap*width*hidden_width,bytes_accessed=40*MIB,transcendentals=experts*cap*hidden_width),
        name="expert_layer",
    )(send,cot,w1,w2,router)

def inverse_rms(values):
    return lax.rsqrt(jnp.mean(values*values,axis=-1,keepdims=True)+EPSILON)

def matmul(left,right,dims=NN):
    return lax.dot_general(left,right,dims,preferred_element_type=jnp.float32)

def swap_parts(values,axis):
    return lax.all_to_all(values,axis,split_axis=0,concat_axis=0,tiled=True)

def reversed_ids(ids):
    flip=np.eye(128,dtype=np.float32)[::-1]
    rows=ids.shape[0]//128
    flip_rows=np.eye(rows,dtype=np.float32)[::-1]
    grid=ids.astype(jnp.bfloat16).reshape(rows,128)
    grid=matmul(grid,jnp.asarray(flip,jnp.bfloat16)).astype(jnp.bfloat16)
    return matmul(jnp.asarray(flip_rows,jnp.bfloat16),grid).reshape(-1).astype(jnp.int32)

def shards(tokens,query_weight,key_weight,value_weight,out_weight,router_weight,attn_gain,moe_gain,bias_table,expert_in,expert_out,expert_id,slot_id,bucket_id,cotangent):
    f32,b16=jnp.float32,jnp.bfloat16
    seq_count,stretch,width=tokens.shape
    seq_devs=lax.axis_size("seq")
    experts=lax.axis_size("exp")
    devices=seq_devs*experts
    length=stretch*seq_devs
    count=seq_count*stretch
    capacity=(5*count+4*experts-1)//(4*experts)
    padded_cap=(capacity+15)//16*16
    buckets,heads=bias_table.shape
    head_dim=width//heads
    groups=seq_devs//seq_count
    own_heads=heads//groups
    per_chunk=2 if own_heads%2==0 else 1
    chunks=own_heads//per_chunk
    used=per_chunk*head_dim
    span=chunks*chunk_span(per_chunk)
    heads_width=groups*chunks*128
    row_block=width//devices
    place=lax.axis_index("seq")
    group=place%groups
    def by_group(weight):
        return weight.reshape(row_block,groups,chunks,per_chunk,head_dim)
    query_part=jnp.pad(by_group(query_weight).reshape(row_block,groups,chunks,used),((0,0),(0,0),(0,0),(0,128-used)))
    both_part=jnp.concatenate([by_group(key_weight),by_group(value_weight)],axis=4).reshape(row_block,groups,chunks,per_chunk*128)
    stacked=jnp.concatenate([query_part,both_part],axis=3).reshape(row_block,groups,span)
    gains=jnp.stack([attn_gain,moe_gain],axis=1)
    small=jnp.pad(jnp.concatenate([router_weight,gains],axis=1),((0,0),(0,126-experts)))
    units=jnp.concatenate([stacked,jnp.broadcast_to(small[:,None],(row_block,groups,128))],axis=2)
    expert_pick=expert_id.reshape(count)
    slot_pick=slot_id.reshape(count)
    slots=experts*padded_cap
    position=jnp.where(slot_pick<capacity,expert_pick*padded_cap+slot_pick,slots)
    hot=(position[None,:]==jnp.arange(slots,dtype=jnp.int32)[:,None]).astype(b16)
    out_full=lax.all_gather(out_weight,BOTH,axis=0,tiled=True)
    out_full=jnp.pad(out_full.reshape(groups*chunks,used,width),((0,0),(0,128-used),(0,0))).reshape(heads_width,width)
    plan=(experts,seq_devs,seq_count,stretch,per_chunk,chunks)
    if row_block%8==0 and row_block*seq_devs%16==0:
        units=jnp.pad(jnp.swapaxes(units,0,1),((0,0),(0,-row_block%16),(0,0)))
        projected,normed,cot_rows,own_weight,first_full=gather_start(plan,row_block,tokens,units,expert_in,position[None,:],cotangent.reshape(count,width),padded_cap)
    else:
        copies=jnp.broadcast_to(tokens[:,None],(seq_count,groups,stretch,width)).reshape(seq_devs,stretch,width)
        own_sequence=swap_parts(copies,"seq").reshape(length,width).astype(f32)
        every=lax.all_gather(units,BOTH,axis=0,tiled=True)
        own_weight=lax.dynamic_index_in_dim(every,group,axis=1,keepdims=False)
        normed=(own_sequence*inverse_rms(own_sequence)*own_weight[:,span+experts].astype(f32)).astype(b16)
        projected=matmul(normed,own_weight[:,:span]).astype(b16)
        first_full=lax.all_gather(expert_in[0],"seq",axis=1,tiled=True)
        cot_rows=matmul(hot,cotangent.reshape(count,width)).astype(b16).reshape(experts,padded_cap,width)
    small_full=own_weight[:,span:]
    router_full=small_full[:,:experts]
    router_wide=jnp.where(jnp.arange(128)[None,:]<experts,small_full,jnp.zeros((),b16))
    attn_gain_full=small_full[:,experts].astype(f32)
    moe_gain_full=small_full[:,experts+1].astype(f32)
    no_id=jnp.full((1,),-1,jnp.int32)
    backward_ids=jnp.concatenate([no_id,bucket_id])[None,:]
    forward_ids=reversed_ids(jnp.concatenate([bucket_id,no_id]))[None,:]
    own_table=lax.dynamic_slice_in_dim(bias_table,group*own_heads,own_heads,axis=1)*LOG2E
    own_table=jnp.pad(own_table.T,((0,-own_heads%8),(0,128-buckets)))
    attended,out32,log_total,cot_arrived,every_weight,second_full=attend(plan,projected,forward_ids,own_table,cot_rows,own_weight,expert_out)
    attended=attended.reshape(count,heads_width)
    tokens_f=tokens.astype(f32).reshape(count,width)
    hidden=tokens_f+matmul(attended,out_full)
    moe_inverse=inverse_rms(hidden)
    moe_in=(hidden*moe_inverse*moe_gain_full).astype(b16)
    send_rows=matmul(hot,moe_in).astype(b16).reshape(experts,padded_cap,width)
    home,result,first_grad,second_grad,router_part=expert_layer(send_rows,cot_arrived,first_full,second_full,router_wide)
    expert_in_grad=lax.psum_scatter(first_grad[None],"seq",scatter_dimension=2,tiled=True)[0]
    expert_out_grad=lax.psum_scatter(second_grad[None],"seq",scatter_dimension=1,tiled=True)[0]
    gain_rows=jnp.transpose(small_full[:,experts:experts+2].astype(f32))
    home=home.reshape(slots,width)
    positions=position[:,None]
    hidden_grad,heads_grad,out_part=combine(experts,positions,home,hidden,cotangent.reshape(count,width),attended,out_full,gain_rows[1:2],router_part)
    out_part=jnp.concatenate([out_part[:,:width].reshape(groups*chunks,128,width)[:,:used].reshape(width,width),out_part[:width,width:]],axis=1) if used<128 else out_part
    out_piece=jnp.moveaxis(out_part.reshape(experts*seq_count,groups,row_block,width+128),1,0)
    out_piece=jnp.pad(out_piece,((0,0),(0,0),(0,-row_block%16),(0,0)))
    token_grads,returned,out_pieces,weight_pieces,tables=attend_back(plan,projected,out32,log_total,backward_ids,own_table,normed,heads_grad.reshape(seq_count,stretch,heads_width),result,out_piece)
    inside=row_block%8==0
    token_grads=token_grads.reshape(count,groups*span)
    own_weights=jnp.stack([query_weight,key_weight,value_weight])
    output,input_grad,expert_in_grad,expert_out_grad,out_sum,small_sum,*weight_grads,attn_gain_grad,tables=finish(experts,groups,per_chunk,chunks,inside,positions,expert_pick[:,None],returned.reshape(slots,width),hidden,hidden_grad,tokens.reshape(count,width),token_grads,every_weight,gain_rows,router_wide,out_pieces,weight_pieces,tables,expert_in_grad,expert_out_grad,own_weights,attn_gain.astype(f32)[:,None])
    attn_gain_grad=attn_gain_grad[:,0]
    output=output.reshape(seq_count,stretch,width)
    bias_table_grad=tables[:,:own_heads,:buckets].reshape(heads,buckets).T
    if not inside:
        tokens_f=tokens.astype(f32).reshape(count,width)
        normed_own=(tokens_f*inverse_rms(tokens_f)*attn_gain_full).astype(b16)
        parts=matmul(normed_own,token_grads,TN).astype(b16).reshape(devices,row_block,groups*chunks,1+per_chunk,128)
        summed=jnp.sum(swap_parts(parts,BOTH).astype(f32),axis=0)
        both_sum=summed[:,:,1:].reshape(row_block,groups*chunks,per_chunk,2,head_dim)
        weight_grads=[summed[:,:,0,:used].reshape(row_block,width)]+[both_sum[:,:,:,i].reshape(row_block,width) for i in range(2)]
        attn_gain_grad=jnp.sum(jnp.stack(weight_grads)*own_weights.astype(f32),axis=(0,2))/attn_gain.astype(f32)
    return (
        output,
        input_grad.reshape(seq_count,stretch,width),
        weight_grads[0],weight_grads[1],weight_grads[2],
        out_sum,
        small_sum[:,:experts],
        attn_gain_grad,
        small_sum[:,experts],
        bias_table_grad,
        expert_in_grad[None],
        expert_out_grad[None],
    )

def solution(mesh):
    tokens=P("exp","seq",None)
    rows=P(BOTH,None)
    return jax.shard_map(
        shards,
        mesh=mesh,
        in_specs=(tokens,rows,rows,rows,rows,rows,P(BOTH),P(BOTH),P(),P("exp",None,"seq"),P("exp","seq",None),P("exp","seq"),P("exp","seq"),P(),tokens),
        out_specs=(tokens,tokens,rows,rows,rows,rows,rows,P(BOTH),P(BOTH),P(),P("exp",None,"seq"),P("exp","seq",None)),
        check_vma=False,
    )
```

```python
import functools
import jax
import jax.numpy as jnp
import numpy as np
from jax import lax
from jax.experimental import pallas as pl
from jax.experimental.pallas import tpu as pltpu
from jax.sharding import PartitionSpec as P
NT=(((1,),(1,)),((),()))
NN=(((1,),(0,)),((),()))
LOG2E=1.4426950408889634
MIB=1024*1024
TN=(((0,),(0,)),((),()))
MESH=pl.DeviceIdType.MESH
EPSILON=1e-06
BOTH=("exp","seq")

def lane_iota(rows):
    return lax.broadcasted_iota(jnp.int32,(rows,128),1)

def dup_head(values,head):
    values=values.astype(jnp.float32)
    turned=pltpu.roll(values,64,1)
    low=lane_iota(values.shape[0])<64
    return jnp.where(low,values,turned) if head==0 else jnp.where(low,turned,values)

def three_parts(column):
    first=column.astype(jnp.bfloat16).astype(jnp.float32)
    rest=column-first
    second=rest.astype(jnp.bfloat16).astype(jnp.float32)
    return first,second,rest-second

def columns_at(lanes,start,parts,other):
    out=other
    for place,part in enumerate(parts):
        out=jnp.where(lanes==start+place,part,out)
    return out

def lone_query(query,head):
    both=dup_head(query,head)*0.125
    return jnp.where(lane_iota(query.shape[0])<64,both,0.0).astype(jnp.bfloat16)

def fill_strip(strip,vector,rows,width):
    full=width+rows
    step=8
    spread=jnp.broadcast_to(vector,(rows,full))
    turned=pltpu.roll(spread,0,1,stride=1,stride_axis=0)
    strip[...]=turned[:,rows:]


def head_column(values,index):
    return jnp.sum(jnp.where(lane_iota(values.shape[0])==index,values,0.0),axis=1,keepdims=True)

def remote(src,dst,sent,received,target):
    return pltpu.make_async_remote_copy(src_ref=src,dst_ref=dst,send_sem=sent,recv_sem=received,device_id=target,device_id_type=MESH)

def loop(first,last,body):
    def step(i,carry):
        body(i)
        return carry
    lax.fori_loop(first,last,step,0)

class Spread:
    def __init__(self,axes,seq_count,groups,source,slot,direct,passed,received,own):
        self.me,self.place=axes
        self.counts=(seq_count,groups)
        self.source,self.slot=source,slot
        self.direct,self.passed,self.received,self.own=direct,passed,received,own
        self.sequence,self.group=self.place//groups,self.place%groups
    def at(self,sequence_step,group_step):
        seq_count,groups=self.counts
        return lax.rem(self.sequence+sequence_step,seq_count)*groups+lax.rem(self.group+group_step,groups)
    def copies(self):
        seq_count,groups=self.counts
        targets=[self.at(i,0) for i in range(1,seq_count)]+[self.at(0,i) for i in range(1,groups)]
        return [remote(self.source(target//groups),self.slot(self.place),self.direct.at[i],self.received.at[self.place],(self.me,target)) for i,target in enumerate(targets)]
    def local(self):
        return pltpu.make_async_copy(self.source(self.sequence),self.slot(self.place),self.own)
    def landed(self,place):
        landing=self.slot(place)
        remote(landing,landing,self.own,self.received.at[place],(self.me,self.place)).wait_recv()
    def relays(self):
        seq_count,groups=self.counts
        out=[]
        for i in range(1,seq_count):
            part=self.at(i,0)
            for j in range(1,groups):
                index=(i-1)*(groups-1)+j-1
                out.append(remote(self.slot(part),self.slot(part),self.passed.at[index],self.received.at[part],(self.me,self.at(0,j))))
        return out
    def start(self):
        self.local().start()
        for copy in self.copies():
            copy.start()
    def relay(self):
        seq_count,groups=self.counts
        for i in range(1,seq_count):
            self.landed(self.at(i,0))
        for copy in self.relays():
            copy.start()
    def finish(self):
        seq_count,groups=self.counts
        for j in range(1,groups):
            for i in range(seq_count):
                self.landed(self.at(i,j))
        for copy in self.copies()+self.relays():
            copy.wait_send()
        self.local().wait()

def spread_semaphores(seq_count,groups):
    dma=lambda n: pltpu.SemaphoreType.DMA((n,))
    return [dma(seq_count+groups-2),dma(max((seq_count-1)*(groups-1),1)),dma(seq_count*groups),pltpu.SemaphoreType.DMA]

def start_kernel(plan,rows,span,token_ref,unit_ref,w1_ref,pos_ref,cot_ref,proj_ref,normed_ref,cot_rows_ref,own_out,w1_out,
                 tok,scaled,units,land,s_unit,r_unit,s_block,r_block,s_pass,own_sem,*spread_sems):
    experts,seq_devs,seq_count,stretch,heads,chunks=plan
    groups=seq_devs//seq_count
    length=stretch*seq_devs
    f32,b16=jnp.float32,jnp.bfloat16
    me,place=lax.axis_index("exp"),lax.axis_index("seq")
    pairs=experts//2
    pair,side=me//2,me%2
    other=1-side
    block=seq_devs*rows
    quarter=w1_ref.shape[2]
    def device(offset,member):
        return lax.rem(pair+offset+pairs,pairs)*2+member
    barrier=pltpu.get_barrier_semaphore()
    for i in range(1,experts):
        pl.semaphore_signal(barrier,inc=1,device_id=(lax.rem(me+i,experts),place),device_id_type=MESH)
    for i in range(1,seq_devs):
        pl.semaphore_signal(barrier,inc=1,device_id=(me,lax.rem(place+i,seq_devs)),device_id_type=MESH)
    def stretch_of(owner):
        return tok.at[pl.ds(pl.multiple_of(owner*stretch,128),stretch)]
    def part_of(owner):
        return w1_out.at[:,pl.ds(pl.multiple_of(owner*quarter,128),quarter)]
    tokens=Spread((me,place),seq_count,groups,lambda n: token_ref.at[n],stretch_of,*spread_sems[:4])
    firsts=Spread((me,place),seq_count,groups,lambda n: w1_ref.at[0],part_of,*spread_sems[4:])
    own_unit=pltpu.make_async_copy(unit_ref.at[place%groups],units.at[place],own_sem.at[0])
    own_unit.start()
    pl.semaphore_wait(barrier,experts+seq_devs-2)
    def send_unit(i):
        target=lax.rem(place+i,seq_devs)
        return remote(unit_ref.at[target%groups],units.at[place],s_unit.at[i],r_unit.at[place],(me,target))
    for i in range(1,seq_devs):
        send_unit(i).start()
    tokens.start()
    firsts.start()
    def landed(landing,received):
        remote(landing,landing,own_sem.at[1],received,(me,place)).wait_recv()
    own_unit.wait()
    for i in range(1,seq_devs):
        source=lax.rem(place+i,seq_devs)
        landed(units.at[source],r_unit.at[source])
    def block_of(owner):
        return land.at[pl.ds(pl.multiple_of(owner*block,16),block)]
    joined=jnp.concatenate([units[i].astype(f32)[:rows] for i in range(seq_devs)],axis=0)
    land[pl.ds(pl.multiple_of(me*block,16),block),:]=joined.astype(b16)
    visit=[j for step in range(1,pairs//2+1) for j in sorted({step,pairs-step})]
    def send_block(j,member,index):
        return remote(block_of(me),block_of(me),s_block.at[index],r_block.at[me],(device(j,member),place))
    sends=[send_block(0,other,0)]+[send_block(j,side,j) for j in visit]
    for copy in sends:
        copy.start()
    passes=[remote(block_of(device(j,side)),block_of(device(j,side)),s_pass.at[j],r_block.at[device(j,side)],(device(0,other),place)) for j in visit]
    for j,copy in zip(visit,passes):
        landed(block_of(device(j,side)),r_block.at[device(j,side)])
        copy.start()
    cap=cot_rows_ref.shape[1]
    def place_rows(expert):
        slots=lax.broadcasted_iota(jnp.int32,(cap,pos_ref.shape[1]),0)+expert*cap
        hot=(slots==pos_ref[...]).astype(f32).astype(b16)
        cot_rows_ref[expert]=jnp.dot(hot,cot_ref[...],preferred_element_type=f32).astype(b16)
    loop(0,experts,place_rows)
    piece=512 if length%512==0 else 128
    tokens.relay()
    tokens.finish()
    def scale_rows(step):
        part=pl.ds(pl.multiple_of(step*piece,piece),piece)
        x=tok[part,:].astype(f32)
        scaled[part,:]=x*lax.rsqrt(jnp.mean(x*x,axis=-1,keepdims=True)+EPSILON)
    loop(0,length//piece,scale_rows)
    for j in [0]+visit:
        landed(block_of(device(j,other)),r_block.at[device(j,other)])
    own_copy=pltpu.make_async_copy(land,own_out,own_sem.at[2])
    own_copy.start()
    gain=jnp.transpose(land[:,span:].astype(f32))[experts:experts+1,:]
    def project(step):
        part=pl.ds(pl.multiple_of(step*piece,piece),piece)
        normed=(scaled[part,:]*gain).astype(b16)
        normed_ref[part,:]=normed
        proj_ref[part,:]=jnp.dot(normed,land[:,:span],preferred_element_type=f32).astype(b16)
    loop(0,length//piece,project)
    firsts.relay()
    own_copy.wait()
    firsts.finish()
    for copy in sends+passes:
        copy.wait_send()
    for i in range(1,seq_devs):
        send_unit(i).wait_send()

def gather_start(plan,rows,tokens,units,expert_in,position,cotangent,cap):
    experts,seq_devs,seq_count,stretch,heads,chunks=plan
    groups=seq_devs//seq_count
    length=stretch*seq_devs
    width=tokens.shape[2]
    span=chunk_span(heads)*chunks
    b16=jnp.bfloat16
    vmem=pl.BlockSpec(memory_space=pltpu.VMEM)
    anywhere=pl.BlockSpec(memory_space=pl.ANY)
    dma=lambda n: pltpu.SemaphoreType.DMA((n,))
    shape=lambda *dims: jax.ShapeDtypeStruct(dims,b16)
    return pl.pallas_call(
        functools.partial(start_kernel,plan,rows,span),
        in_specs=[anywhere,anywhere,vmem,vmem,vmem],
        out_specs=[vmem,vmem,vmem,anywhere,anywhere],
        out_shape=[shape(length,span),shape(length,width),shape(experts,cap,width),shape(width,span+128),shape(width,expert_in.shape[2]*seq_devs)],
        scratch_shapes=[pltpu.VMEM((length,width),b16),pltpu.VMEM((length,width),jnp.float32),pltpu.VMEM((seq_devs,)+units.shape[1:],b16),pltpu.VMEM((width,span+128),b16),
            dma(seq_devs),dma(seq_devs),dma(experts),dma(experts),dma(experts),dma(3)]+spread_semaphores(seq_count,groups)*2,
        compiler_params=pltpu.CompilerParams(collective_id=3,has_side_effects=True,vmem_limit_bytes=40*MIB),
        cost_estimate=pl.CostEstimate(flops=2*length*width*span,bytes_accessed=24*MIB,transcendentals=0),
        name="gather_start",
    )(tokens,units,expert_in,position,cotangent)

def one_hot_rows(ids):
    return (lax.broadcasted_iota(jnp.int32,(128,ids.shape[1]),0)==ids).astype(jnp.float32).astype(jnp.bfloat16)

def stack_parts(values):
    return jnp.concatenate(three_parts(values),axis=0).astype(jnp.bfloat16)

def join_parts(product):
    rows=product.shape[0]//3
    return product[:rows]+product[rows:2*rows]+product[2*rows:]

def table_rows(table,hot):
    return join_parts(jnp.dot(stack_parts(table),hot,preferred_element_type=jnp.float32))

def chunk_span(heads):
    return 128*(1+heads)

def forward_kernel(plan,block,srows,proj_ref,ids_ref,rows_ref,cot_ref,own_ref,w2_ref,att_out,o32_ref,lse_ref,cot_out,all_out,w2_out,strip,bias_ref,kd,va,scr,outs,s_cot,r_cot,s_att,r_att,s_all,r_all,local_sem,*spread_sems):
    experts,seq_devs,seq_count,stretch,heads,chunks=plan
    length=stretch*seq_devs
    groups=seq_devs//seq_count
    f32,b16=jnp.float32,jnp.bfloat16
    me,place=lax.axis_index("exp"),lax.axis_index("seq")
    sequence,group=place//groups,place%groups
    barrier=pltpu.get_barrier_semaphore()
    loop(1,experts,lambda i: pl.semaphore_signal(barrier,inc=1,device_id=(lax.rem(me+i,experts),place),device_id_type=MESH))
    loop(1,seq_devs,lambda i: pl.semaphore_signal(barrier,inc=1,device_id=(me,lax.rem(place+i,seq_devs)),device_id_type=MESH))
    own_cot=pltpu.make_async_copy(cot_ref.at[me],cot_out.at[me],local_sem.at[0])
    own_cot.start()
    own_all=pltpu.make_async_copy(own_ref,all_out.at[group],local_sem.at[1+chunks])
    own_all.start()
    deep=w2_ref.shape[1]
    seconds=Spread((me,place),seq_count,groups,lambda n: w2_ref.at[0],lambda owner: w2_out.at[pl.ds(pl.multiple_of(owner*deep,128),deep)],*spread_sems)
    pl.semaphore_wait(barrier,experts+seq_devs-2)
    seconds.start()
    def send_all(i):
        return remote(own_ref,all_out.at[group],s_all.at[i],r_all.at[i],(me,sequence*groups+lax.rem(group+i,groups)))
    loop(1,groups,lambda i: send_all(i).start())
    def send_cot(i):
        target=lax.rem(me+i,experts)
        return remote(cot_ref.at[target],cot_out.at[me],s_cot.at[i],r_cot.at[i],(target,place))
    loop(1,experts,lambda i: send_cot(i).start())
    def lanes_of(owner_group,c,size):
        return pl.ds(pl.multiple_of((owner_group*chunks+c)*size,128),size)
    def send_att(c,i):
        target=lax.rem(place+i,seq_devs)
        rows=pl.ds(pl.multiple_of(target*stretch,128),stretch)
        return remote(outs.at[c,rows],att_out.at[sequence,:,lanes_of(group,c,128)],s_att.at[c,i],r_att.at[c,i],(me,target))
    def own_att(c):
        rows=pl.ds(pl.multiple_of(place*stretch,128),stretch)
        return pltpu.make_async_copy(outs.at[c,rows],att_out.at[sequence,:,lanes_of(group,c,128)],local_sem.at[1+c])
    width=strip.shape[1]
    wide=256
    blocks=length//block
    pieces=length//wide
    lanes=lane_iota(length)
    block_lanes=lane_iota(block)
    lse_ref[...]=jnp.zeros_like(lse_ref)
    bias_ref[...]=table_rows(rows_ref[...],one_hot_rows(ids_ref[...]))
    def attend_head(c,head):
        index=c*heads+head
        def columns(which):
            return slice(c*chunk_span(heads)+which*128,c*chunk_span(heads)+(which+1)*128)
        own=slice(c*128,(c+1)*128)
        fill_strip(strip,bias_ref[index:index+1,:],srows,width)
        kd[...]=dup_head(proj_ref[:,columns(1+head)],0).astype(b16)
        va[...]=jnp.where(lanes<64,dup_head(proj_ref[:,columns(1+head)],1),jnp.where(lanes==64,1.0,0.0)).astype(b16)
        def rows_of(step):
            return slice(step*block,(step+1)*block)
        def score_piece(step,qa,p,slot,top):
            raw=lax.dot_general(qa,kd[p*wide:(p+1)*wide,:],NT,preferred_element_type=f32)
            parts=[]
            for part in range(block//srows):
                start=length-srows-step*block-part*srows+p*wide
                parts.append(raw[part*srows:(part+1)*srows]*LOG2E+strip[:,pl.ds(start,wide)])
            scores=jnp.concatenate(parts,axis=0)
            scr[slot,:,p*wide:(p+1)*wide]=scores
            for j in range(wide//128):
                top=jnp.maximum(top,scores[:,j*128:(j+1)*128])
            return top
        def mix_piece(slot,p,top,total):
            weights=jnp.exp2(scr[slot,:,p*wide:(p+1)*wide]-top).astype(b16)
            return total+jnp.dot(weights,va[p*wide:(p+1)*wide,:],preferred_element_type=f32)
        def finish(step,top,mixed):
            rows=rows_of(step)
            total=mixed[:,64:65]
            result=mixed/total
            lse_ref[rows,:]=jnp.where(block_lanes==index,top+jnp.log2(total),lse_ref[rows,:])
            if head:
                result=jnp.where(block_lanes<64,o32_ref[rows,own],pltpu.roll(result,64,1))
            o32_ref[rows,own]=result
            if head==heads-1:
                outs[c,rows]=result.astype(b16)
        def send_steps(first,last):
            for part in range(first*block//stretch,last*block//stretch):
                distance=lax.rem(part-place+seq_devs,seq_devs)
                @pl.when(distance==0)
                def _():
                    own_att(c).start()
                @pl.when(distance!=0)
                def _():
                    send_att(c,distance).start()
        def advance(step,slot,top):
            mixing=top is not None
            qa=lone_query(proj_ref[rows_of(step),columns(0)],head)
            new=jnp.full((block,128),-jnp.inf,f32)
            mixed=jnp.zeros((block,128),f32)
            for p in range(pieces):
                new=score_piece(step,qa,p,slot,new)
                if mixing:
                    mixed=mix_piece(1-slot,p,top,mixed)
            if mixing:
                finish(step-1,top,mixed)
            return jnp.max(new,axis=1,keepdims=True)
        top=None
        for step in range(blocks):
            top=advance(step,step%2,top)
        if head==heads-1:
            send_steps(0,blocks-1)
        mixed=jnp.zeros((block,128),f32)
        for p in range(pieces):
            mixed=mix_piece((blocks-1)%2,p,top,mixed)
        finish(blocks-1,top,mixed)
        if head==heads-1:
            send_steps(blocks-1,blocks)
    for c in range(chunks):
        for head in range(heads):
            attend_head(c,head)
    seconds.relay()
    def land_att(c,i):
        source=lax.rem(place-i+seq_devs,seq_devs)
        landing=att_out.at[source//groups,:,lanes_of(source%groups,c,128)]
        remote(landing,landing,s_att.at[c,i],r_att.at[c,i],(me,place)).wait_recv()
    def finish_chunk(c):
        own_att(c).wait()
        loop(1,seq_devs,lambda i: land_att(c,i))
        loop(1,seq_devs,lambda i: send_att(c,i).wait_send())
    loop(0,chunks,finish_chunk)
    def land_cot(i):
        landing=cot_out.at[lax.rem(me-i+experts,experts)]
        remote(landing,landing,s_cot.at[i],r_cot.at[i],(me,place)).wait_recv()
    loop(1,experts,land_cot)
    loop(1,experts,lambda i: send_cot(i).wait_send())
    def land_all(i):
        landing=all_out.at[lax.rem(group-i+groups,groups)]
        remote(landing,landing,s_all.at[i],r_all.at[i],(me,place)).wait_recv()
        send_all(i).wait_send()
    loop(1,groups,land_all)
    own_all.wait()
    own_cot.wait()
    seconds.finish()

def attend(plan,projected,ids,table,cot_rows,own_weight,expert_out,block=512,srows=128):
    experts,seq_devs,seq_count,stretch,heads,chunks=plan
    length=stretch*seq_devs
    groups=seq_devs//seq_count
    f32,b16=jnp.float32,jnp.bfloat16
    vmem=pl.BlockSpec(memory_space=pltpu.VMEM)
    anywhere=pl.BlockSpec(memory_space=pl.ANY)
    dma=lambda *shape: pltpu.SemaphoreType.DMA(shape)
    return pl.pallas_call(
        functools.partial(forward_kernel,plan,block,srows),
        in_specs=[vmem,vmem,vmem,anywhere,vmem,vmem],
        out_specs=[anywhere,vmem,vmem]+[anywhere]*3,
        out_shape=[jax.ShapeDtypeStruct((seq_count,stretch,groups*chunks*128),b16),jax.ShapeDtypeStruct((length,chunks*128),f32),jax.ShapeDtypeStruct((length,128),f32),jax.ShapeDtypeStruct(cot_rows.shape,b16),jax.ShapeDtypeStruct((groups,)+own_weight.shape,b16),jax.ShapeDtypeStruct((expert_out.shape[1]*seq_devs,expert_out.shape[2]),b16)],
        scratch_shapes=[pltpu.VMEM((srows,2*length-srows),f32),pltpu.VMEM((table.shape[0],2*length),f32),pltpu.VMEM((length,128),b16),pltpu.VMEM((length,128),b16),pltpu.VMEM((2,block,length),f32),pltpu.VMEM((chunks,length,128),b16),
            dma(experts),dma(experts),dma(chunks,seq_devs),dma(chunks,seq_devs),dma(groups),dma(groups),dma(2+chunks)]+spread_semaphores(seq_count,groups),
        compiler_params=pltpu.CompilerParams(collective_id=1,has_side_effects=True,vmem_limit_bytes=48*MIB),
        cost_estimate=pl.CostEstimate(flops=16*heads*chunks*length*length*64,bytes_accessed=16*MIB,transcendentals=heads*chunks*length*length),
        name="attend_forward",
    )(projected,ids,table,cot_rows,own_weight,expert_out)

def backward_kernel(plan,inside,bq,bk,srows,proj_ref,o32_ref,lse_ref,ids_ref,rows_ref,normed_ref,up_ref,res_ref,piece_ref,
                    grad_out,ret_out,piece_out,weight_out,table_out,
                    strip,grads,kk,kt,da,qd,dkv_acc,lse_t,delta,ups,outs,weight_parts,piece_parts,piece_land,diag,table,normed_t,hot,bias_ref,
                    s_up,r_up,s_res,r_res,s_piece,r_piece,s_grad,r_grad,s_weight,r_weight,s_half,r_half,s_table,r_table,local_sem,own_sem):
    experts,seq_devs,seq_count,stretch,heads,chunks=plan
    length=stretch*seq_devs
    groups=seq_devs//seq_count
    devices=experts*seq_devs
    f32,b16=jnp.float32,jnp.bfloat16
    me,place=lax.axis_index("exp"),lax.axis_index("seq")
    sequence,group=place//groups,place%groups
    rank=me*seq_devs+place
    def other(i):
        target=lax.rem(rank+i,devices)
        return target,(target//seq_devs,target%seq_devs)
    barrier=pltpu.get_barrier_semaphore()
    loop(1,devices,lambda i: pl.semaphore_signal(barrier,inc=1,device_id=other(i)[1],device_id_type=MESH))
    def lanes_of(owner_group,c,size):
        return pl.ds(pl.multiple_of((owner_group*chunks+c)*size,128),size)
    def rows_of(owner):
        return pl.ds(pl.multiple_of(owner*stretch,128),stretch)
    def send_up(c,i):
        target=lax.rem(place+i,seq_devs)
        return remote(up_ref.at[target//groups,:,lanes_of(target%groups,c,128)],ups.at[c,rows_of(place)],s_up.at[c,i],r_up.at[c,i],(me,target))
    def own_up(c):
        return pltpu.make_async_copy(up_ref.at[sequence,:,lanes_of(group,c,128)],ups.at[c,rows_of(place)],local_sem.at[0,c])
    def send_res(i):
        target=lax.rem(me+i,experts)
        return remote(res_ref.at[target],ret_out.at[me],s_res.at[i],r_res.at[i],(target,place))
    half=experts*seq_count
    spot=me*seq_count+sequence
    def fellow(i):
        target=lax.rem(spot+i,half)
        return target,(target//seq_count,(target%seq_count)*groups+group)
    def half_piece(i):
        target=lax.rem(group+i,groups)
        return remote(piece_ref.at[target],piece_land.at[i-1],s_half.at[i],r_half.at[i],(me,sequence*groups+target))
    own_piece=pltpu.make_async_copy(piece_ref.at[group],piece_parts,own_sem.at[2])
    def send_piece(i):
        target,where=fellow(i)
        return remote(piece_parts.at[target],piece_out.at[spot],s_piece.at[i],r_piece.at[i],where)
    keep_piece=pltpu.make_async_copy(piece_parts.at[spot],piece_out.at[spot],own_sem.at[4])
    def meet_pieces():
        own_piece.wait()
        for j in range(1,groups):
            landed(piece_land.at[j-1],r_half.at[j])
        def add(i):
            total=piece_parts[i].astype(f32)
            for j in range(1,groups):
                total=total+piece_land[j-1,i].astype(f32)
            piece_parts[i]=total.astype(b16)
        loop(0,half,add)
        loop(1,half,lambda i: send_piece(i).start())
        keep_piece.start()
    def grad_lanes(owner_group,c,part):
        return pl.ds(pl.multiple_of((owner_group*chunks+c)*chunk_span(heads)+part*128,128),128)
    def send_grad(c,part,i):
        target=lax.rem(place+i,seq_devs)
        return remote(outs.at[c,rows_of(target),part*128:(part+1)*128],grad_out.at[sequence,:,grad_lanes(group,c,part)],s_grad.at[c,part,i],r_grad.at[c,part,i],(me,target))
    def own_grad(c,part):
        return pltpu.make_async_copy(outs.at[c,rows_of(place),part*128:(part+1)*128],grad_out.at[sequence,:,grad_lanes(group,c,part)],local_sem.at[2+part,c])
    def send_weight(c,i):
        target,where=other(i)
        return remote(weight_parts.at[c,target],weight_out.at[c,rank],s_weight.at[c,i],r_weight.at[c,i],where)
    def own_weight(c):
        return pltpu.make_async_copy(weight_parts.at[c,rank],weight_out.at[c,rank],local_sem.at[1,c])
    def send_table(i):
        return remote(table,table_out.at[rank],s_table.at[i],r_table.at[i],other(i)[1])
    own_table=pltpu.make_async_copy(table,table_out.at[rank],own_sem.at[0])
    own_res=pltpu.make_async_copy(res_ref.at[me],ret_out.at[me],own_sem.at[1])
    def landed(landing,received):
        remote(landing,landing,own_sem.at[3],received,(me,place)).wait_recv()
    own_res.start()
    own_piece.start()
    loop(0,chunks,lambda c: own_up(c).start())
    pl.semaphore_wait(barrier,devices-1)
    loop(1,seq_devs,lambda i: send_up(0,i).start())
    width=strip.shape[1]
    full_width=2*length
    lanes=lane_iota(length)
    count=length//bk
    if inside:
        weight_parts[...]=jnp.zeros_like(weight_parts)
        normed_t[...]=jnp.transpose(normed_ref[...])
    diag[...]=jnp.zeros_like(diag)
    lse_t[...]=jnp.transpose(lse_ref[...])
    hot[...]=one_hot_rows(ids_ref[...])
    bias_ref[...]=table_rows(rows_ref[...],hot[...])
    def head_back(c,head):
        index=c*heads+head
        def columns(which):
            return pl.ds(pl.multiple_of(c*chunk_span(heads)+which*128,128),128)
        query,both=proj_ref[:,columns(0)],proj_ref[:,columns(1+head)]
        fill_strip(strip,bias_ref[pl.ds(index,1),:],srows,width)
        grads[...]=jnp.zeros_like(grads)
        low_lanes=lanes<64
        kk[...]=both
        kt[...]=jnp.transpose(both)
        query=query.astype(f32)
        query=jnp.where(low_lanes,pltpu.roll(query,64,1) if head else query,0.0)
        qd[...]=(query*0.125).astype(b16)
        if head==0:
            take_up(c)
            products_sum=ups[c].astype(f32)*o32_ref[:,pl.ds(pl.multiple_of(c*128,128),128)]
            halves=lax.broadcasted_iota(jnp.int32,(8,128),0)==lax.broadcasted_iota(jnp.int32,(8,128),1)//64
            halves=halves.astype(f32).astype(b16)
            delta[...]=sum(lax.dot_general(halves,part.astype(b16),NT,preferred_element_type=f32) for part in three_parts(products_sum))
        upstream=ups[c].astype(f32)
        da[...]=jnp.where(low_lanes,0.0,upstream if head else pltpu.roll(upstream,64,1)).astype(b16)
        dkv_acc[...]=jnp.zeros_like(dkv_acc)
        def query_block(qb):
            qs=pl.ds(pl.multiple_of(qb*bq,bq),bq)
            def products(kb):
                ks=slice(kb*bk,(kb+1)*bk)
                raw=lax.dot_general(kk[ks,:],qd[qs,:],NT,preferred_element_type=f32)
                up=lax.dot_general(kk[ks,:],da[qs,:],NT,preferred_element_type=f32)
                return raw,up
            log_row=lse_t[pl.ds(index,1),qs]
            delta_row=delta[head:head+1,qs]
            def consume(kb,raw,up,dq):
                ks=slice(kb*bk,(kb+1)*bk)
                probs,score_grads=[],[]
                for part in range(bk//srows):
                    start=qb*bq+(length-srows)-kb*bk-part*srows
                    rows=slice(part*srows,(part+1)*srows)
                    prob=jnp.exp2(raw[rows]*LOG2E+strip[:,pl.ds(pl.multiple_of(start,128),bq)]-log_row)
                    grad=prob*(up[rows]-delta_row)
                    grads[:,pl.ds(pl.multiple_of(start+srows,128),bq)]+=grad
                    probs.append(prob.astype(b16))
                    score_grads.append(grad.astype(b16))
                low=jnp.concatenate(score_grads,axis=0)
                dkv_acc[ks,:]+=jnp.dot(jnp.concatenate(probs,axis=0),da[qs,:],preferred_element_type=f32)+jnp.dot(low,qd[qs,:],preferred_element_type=f32)
                return dq+jnp.dot(kt[:,ks],low,preferred_element_type=f32)
            dq=jnp.zeros((128,bq),f32)
            ready=products(0)
            for kb in range(count):
                following=products(kb+1) if kb+1<count else None
                dq=consume(kb,*ready,dq)
                ready=following
            dq=jnp.transpose(dq)*0.125
            if head:
                dq=jnp.where(lane_iota(bq)<64,outs[c,qs,0:128].astype(f32),pltpu.roll(dq,64,1))
            outs[c,qs,0:128]=dq.astype(b16)
            if head==heads-1:
                for part in range(bq//stretch):
                    distance=lax.rem(qb*(bq//stretch)+part-place+seq_devs,seq_devs)
                    @pl.when(distance==0)
                    def _():
                        own_grad(c,0).start()
                    @pl.when(distance!=0)
                    def _():
                        send_grad(c,0,distance).start()
        loop(0,length//bq,query_block)
        outs[c,:,128*(1+head):128*(2+head)]=dkv_acc[...].astype(b16)
        loop(1,seq_devs,lambda i: send_grad(c,1+head,i).start())
        own_grad(c,1+head).start()
        total=grads[0:8,:]
        for part in range(1,srows//8):
            total=total+pltpu.roll(grads[8*part:8*part+8,:],full_width-8*part,1)
        row=lax.broadcasted_iota(jnp.int32,(8,full_width),0)
        for part in range(1,8):
            total=jnp.where(row==part,pltpu.roll(total,full_width-part,1),total)
        diag[pl.ds(index,1),:]=jnp.sum(total,axis=0,keepdims=True)
    def take_up(c):
        loop(1,seq_devs,lambda i: landed(ups.at[c,rows_of(lax.rem(place-i+seq_devs,seq_devs))],r_up.at[c,i]))
        own_up(c).wait()
        @pl.when(c==0)
        def _():
            loop(1,chunks,lambda later: loop(1,seq_devs,lambda i: send_up(later,i).start()))
            loop(1,groups,lambda i: half_piece(i).start())
            loop(1,experts,lambda i: send_res(i).start())
    def one_chunk(c):
        for head in range(heads):
            head_back(c,head)
            if head==0:
                @pl.when(c==0)
                def _():
                    meet_pieces()
        if inside:
            part=jnp.dot(normed_t[...],outs[c],preferred_element_type=f32)
            block=normed_t.shape[0]//devices
            weight_parts[c,:,:block,:]=part.reshape(devices,block,chunk_span(heads)).astype(b16)
            loop(1,devices,lambda i: send_weight(c,i).start())
            own_weight(c).start()
    loop(0,chunks,one_chunk)
    table[...]=join_parts(lax.dot_general(stack_parts(diag[...]),hot[...],NT,preferred_element_type=f32))
    loop(1,devices,lambda i: send_table(i).start())
    own_table.start()
    def finish_chunk(c):
        def grad_landed(i):
            source=lax.rem(place-i+seq_devs,seq_devs)
            for part in range(1+heads):
                landed(grad_out.at[source//groups,:,grad_lanes(source%groups,c,part)],r_grad.at[c,part,i])
                send_grad(c,part,i).wait_send()
            send_up(c,i).wait_send()
        loop(1,seq_devs,grad_landed)
        for part in range(1+heads):
            own_grad(c,part).wait()
        if inside:
            def weight_landed(i):
                landed(weight_out.at[c,lax.rem(rank-i+devices,devices)],r_weight.at[c,i])
                send_weight(c,i).wait_send()
            loop(1,devices,weight_landed)
            own_weight(c).wait()
    loop(0,chunks,finish_chunk)
    def res_landed(i):
        landed(ret_out.at[lax.rem(me-i+experts,experts)],r_res.at[i])
        send_res(i).wait_send()
    loop(1,experts,res_landed)
    def piece_landed(i):
        landed(piece_out.at[lax.rem(spot-i+half,half)],r_piece.at[i])
        send_piece(i).wait_send()
    loop(1,half,piece_landed)
    def table_landed(i):
        landed(table_out.at[lax.rem(rank-i+devices,devices)],r_table.at[i])
        send_table(i).wait_send()
    loop(1,devices,table_landed)
    own_res.wait()
    loop(1,groups,lambda i: half_piece(i).wait_send())
    keep_piece.wait()
    own_table.wait()

def attend_back(plan,projected,o32,lse,ids,table,normed,upstream,result,piece,bq=512,bk=512,srows=128):
    experts,seq_devs,seq_count,stretch,heads,chunks=plan
    length=stretch*seq_devs
    groups=seq_devs//seq_count
    devices=experts*seq_devs
    block=normed.shape[1]//devices
    inside=block%8==0
    rows=(block+15)//16*16
    f32,b16=jnp.float32,jnp.bfloat16
    vm=lambda kind,*shape: pltpu.VMEM(shape,kind)
    vmem=pl.BlockSpec(memory_space=pltpu.VMEM)
    anywhere=pl.BlockSpec(memory_space=pl.ANY)
    dma=lambda *shape: pltpu.SemaphoreType.DMA(shape)
    shape=lambda kind,*dims: jax.ShapeDtypeStruct(dims,kind)
    weight_shape=(chunks,devices,rows,chunk_span(heads)) if inside else (1,1,16,128)
    return pl.pallas_call(
        functools.partial(backward_kernel,plan,inside,bq,bk,srows),
        in_specs=[vmem]*6+[anywhere]*3,
        out_specs=[anywhere]*5,
        out_shape=[shape(b16,seq_count,stretch,groups*chunks*chunk_span(heads)),shape(b16,*result.shape),shape(b16,*piece.shape[1:]),shape(b16,*weight_shape),shape(f32,devices,table.shape[0],128)],
        scratch_shapes=[vm(f32,srows,2*length-srows),vm(f32,srows,2*length),vm(b16,length,128),vm(b16,128,length),vm(b16,length,128),
            vm(b16,length,128),vm(f32,length,128),vm(f32,128,length),vm(f32,8,length),
            vm(b16,chunks,length,128),vm(b16,chunks,length,chunk_span(heads)),vm(b16,*weight_shape),vm(b16,*piece.shape[1:]),vm(b16,max(groups-1,1),*piece.shape[1:]),vm(f32,table.shape[0],2*length),vm(f32,table.shape[0],128),vm(b16,normed.shape[1],length),vm(b16,128,2*length),vm(f32,table.shape[0],2*length),
            dma(chunks,seq_devs),dma(chunks,seq_devs),dma(experts),dma(experts),dma(experts*seq_count),dma(experts*seq_count),dma(chunks,1+heads,seq_devs),dma(chunks,1+heads,seq_devs),
            dma(chunks,devices),dma(chunks,devices),dma(groups),dma(groups),dma(devices),dma(devices),dma(3+heads,chunks),dma(5)],
        compiler_params=pltpu.CompilerParams(collective_id=2,has_side_effects=True,vmem_limit_bytes=58*MIB),
        cost_estimate=pl.CostEstimate(flops=40*heads*chunks*length*length*64,bytes_accessed=24*MIB,transcendentals=heads*chunks*length*length),
        name="attend_backward",
    )(projected,o32,lse,ids,table,normed,upstream,result,piece)


def combine_kernel(experts,pos_ref,home_ref,hidden_ref,cot_ref,att_ref,out_w_ref,gain_ref,router_ref,grad_ref,heads_ref,part_ref,total,gain_total):
    f32,b16=jnp.float32,jnp.bfloat16
    step=pl.program_id(0)
    rows=hidden_ref.shape[0]
    slots=home_ref.shape[0]
    width=hidden_ref.shape[1]
    hot=(pos_ref[...]==lax.broadcasted_iota(jnp.int32,(rows,slots),1)).astype(f32).astype(b16)
    moe_in_grad=jnp.dot(hot,home_ref[...],preferred_element_type=f32)
    hidden=hidden_ref[...]
    inverse=lax.rsqrt(jnp.mean(hidden*hidden,axis=-1,keepdims=True)+EPSILON)
    weighted=moe_in_grad*gain_ref[...]
    inner=jnp.mean(weighted*hidden,axis=-1,keepdims=True)
    hidden_grad=cot_ref[...].astype(f32)+weighted*inverse-hidden*(inverse*inverse*inverse)*inner
    grad_ref[...]=hidden_grad
    branch=hidden_grad.astype(b16)
    heads_ref[...]=lax.dot_general(branch,out_w_ref[...],NT,preferred_element_type=f32).astype(b16)
    part=lax.dot_general(att_ref[...],branch,TN,preferred_element_type=f32)
    gain_part=jnp.sum(moe_in_grad*hidden*inverse,axis=0,keepdims=True)
    @pl.when(step==0)
    def _():
        total[...]=part
        gain_total[...]=jnp.broadcast_to(gain_part,gain_total.shape)
    @pl.when(step>0)
    def _():
        total[...]+=part
        gain_total[...]+=gain_part
    @pl.when(step==pl.num_programs(0)-1)
    def _():
        heads_width=total.shape[0]
        part_ref[:,:width]=total[...].astype(b16)
        column=jnp.transpose(jnp.broadcast_to(gain_total[0:1,:],(128,width)))
        lanes=lax.broadcasted_iota(jnp.int32,(width,128),1)
        part_ref[:width,width:]=jnp.where(lanes==experts,column,router_ref[...]).astype(b16)

def combine(experts,position,home,hidden,cotangent,attended,out_full,gain,router_part,block=256):
    count,width=hidden.shape
    heads_width=attended.shape[1]
    f32,b16=jnp.float32,jnp.bfloat16
    block=min(block,count)
    by_rows=lambda columns: pl.BlockSpec((block,columns),lambda i:(i,0))
    whole=lambda value: pl.BlockSpec(value.shape,lambda i:(0,0))
    return pl.pallas_call(
        functools.partial(combine_kernel,experts),
        grid=(count//block,),
        in_specs=[by_rows(1),whole(home),by_rows(width),by_rows(width),by_rows(heads_width),whole(out_full),whole(gain),whole(router_part)],
        out_specs=[by_rows(width),by_rows(heads_width),pl.BlockSpec((heads_width,width+128),lambda i:(0,0))],
        out_shape=[jax.ShapeDtypeStruct((count,width),f32),jax.ShapeDtypeStruct((count,heads_width),b16),jax.ShapeDtypeStruct((heads_width,width+128),b16)],
        scratch_shapes=[pltpu.VMEM((heads_width,width),f32),pltpu.VMEM((8,width),f32)],
        compiler_params=pltpu.CompilerParams(vmem_limit_bytes=40*MIB),
        cost_estimate=pl.CostEstimate(flops=6*count*width*width,bytes_accessed=16*MIB,transcendentals=0),
        name="combine",
    )(position,home,hidden,cotangent,attended,out_full,gain,router_part)

def finish_kernel(experts,groups,heads,chunks,inside,pos_ref,pick_ref,returned_ref,hidden_ref,grad_ref,token_ref,token_grad_ref,every_ref,gains_ref,router_ref,piece_ref,weight_ref,table_ref,first_ref,second_ref,own_ref,own_gain_ref,
                  output_ref,input_ref,first_out,second_out,out_sum,small_sum,query_sum,key_sum,value_sum,gain_sum,table_sum):
    f32,b16=jnp.float32,jnp.bfloat16
    step=pl.program_id(0)
    rows,width=hidden_ref.shape
    row_block=out_sum.shape[0]
    first_out[...]=first_ref[...].astype(f32)
    second_out[...]=second_ref[...].astype(f32)
    slots=returned_ref.shape[0]
    cw=chunk_span(heads)
    span=chunks*cw
    hidden=hidden_ref[...]
    moe_in=(hidden*lax.rsqrt(jnp.mean(hidden*hidden,axis=-1,keepdims=True)+EPSILON)*gains_ref[1:2,:]).astype(b16)
    lanes=lax.broadcasted_iota(jnp.int32,(rows,128),1)
    logits=jnp.where(lanes<experts,jnp.dot(moe_in,router_ref[...],preferred_element_type=f32),-jnp.inf)
    raised=jnp.exp(logits-jnp.max(logits,axis=1,keepdims=True))
    gate=jnp.sum(jnp.where(lanes==pick_ref[...],raised,0.0),axis=1,keepdims=True)/jnp.sum(raised,axis=1,keepdims=True)
    hot=(pos_ref[...]==lax.broadcasted_iota(jnp.int32,(rows,slots),1)).astype(f32).astype(b16)
    output_ref[...]=(hidden+gate*jnp.dot(hot,returned_ref[...],preferred_element_type=f32)).astype(b16)
    normed_grad=jnp.zeros((rows,width),f32)
    for owner in range(groups):
        normed_grad=normed_grad+lax.dot_general(token_grad_ref[:,owner*span:(owner+1)*span],every_ref[owner,:,:span],NT,preferred_element_type=f32)
    x=token_ref[...].astype(f32)
    inverse=lax.rsqrt(jnp.mean(x*x,axis=-1,keepdims=True)+EPSILON)
    weighted=normed_grad*gains_ref[0:1,:]
    inner=jnp.mean(weighted*x,axis=-1,keepdims=True)
    input_ref[...]=grad_ref[...]+weighted*inverse-x*(inverse*inverse*inverse)*inner
    @pl.when(step==0)
    def _():
        devices=piece_ref.shape[0]
        def add_piece(i,total):
            return total+piece_ref[i].astype(f32)
        total=lax.fori_loop(1,devices,add_piece,piece_ref[0].astype(f32))[:row_block]
        out_sum[...]=total[:,:width]
        small_sum[...]=total[:,width:]
        for owner in range(groups):
            def add_table(i,total):
                return total+table_ref[i*groups+owner]
            table_sum[owner]=lax.fori_loop(1,table_ref.shape[0]//groups,add_table,table_ref[owner])
            if inside:
                for c in range(chunks):
                    def add_weight(i,total):
                        return total+weight_ref[c,i*groups+owner].astype(f32)
                    summed=lax.fori_loop(1,weight_ref.shape[1]//groups,add_weight,weight_ref[c,owner].astype(f32))[:row_block]
                    place=slice((owner*chunks+c)*128,(owner*chunks+c+1)*128)
                    query_sum[:,place]=summed[:,0:128]
                    first=summed[:,128:256]
                    second=summed[:,128*heads:128*(heads+1)]
                    low=lane_iota(summed.shape[0])<64
                    key_sum[:,place]=jnp.where(low,first,pltpu.roll(second,64,1))
                    value_sum[:,place]=jnp.where(low,pltpu.roll(first,64,1),second)
        if inside:
            products=query_sum[...]*own_ref[0].astype(f32)+key_sum[...]*own_ref[1].astype(f32)+value_sum[...]*own_ref[2].astype(f32)
            gain_sum[...]=jnp.broadcast_to(jnp.sum(products,axis=1,keepdims=True),gain_sum.shape)/own_gain_ref[...]

def finish(experts,groups,heads,chunks,inside,position,pick,returned,hidden,hidden_grad,tokens,token_grads,every_weight,gains,router,pieces,weights,tables,first,second,own_weights,own_gain,block=256):
    count,width=hidden.shape
    f32,b16=jnp.float32,jnp.bfloat16
    block=min(block,count)
    by_rows=lambda columns: pl.BlockSpec((block,columns),lambda i:(i,0))
    def whole(shape):
        return pl.BlockSpec(shape,lambda i:(0,)*len(shape))
    row_block=own_gain.shape[0]
    sums=jax.ShapeDtypeStruct((row_block,width),f32)
    steps=count//block
    by_steps=lambda value: pl.BlockSpec((value.shape[0]//steps,value.shape[1]),lambda i:(i,0))
    wide=lambda value: jax.ShapeDtypeStruct(value.shape,f32)
    small_shape=jax.ShapeDtypeStruct((row_block,128),f32)
    table_shape=jax.ShapeDtypeStruct((groups,)+tables.shape[1:],f32)
    return pl.pallas_call(
        functools.partial(finish_kernel,experts,groups,heads,chunks,inside),
        grid=(count//block,),
        in_specs=[by_rows(1),by_rows(1),whole(returned.shape),by_rows(width),by_rows(width),by_rows(width),by_rows(token_grads.shape[1]),whole(every_weight.shape),whole(gains.shape),whole(router.shape),whole(pieces.shape),whole(weights.shape),whole(tables.shape),by_steps(first),by_steps(second),whole(own_weights.shape),whole(own_gain.shape)],
        out_specs=[by_rows(width),by_rows(width),by_steps(first),by_steps(second),whole(sums.shape),whole(small_shape.shape)]+[whole(sums.shape)]*3+[whole(small_shape.shape),whole(table_shape.shape)],
        out_shape=[jax.ShapeDtypeStruct((count,width),b16),jax.ShapeDtypeStruct((count,width),f32),wide(first),wide(second),sums,small_shape,sums,sums,sums,small_shape,table_shape],
        compiler_params=pltpu.CompilerParams(vmem_limit_bytes=56*MIB),
        cost_estimate=pl.CostEstimate(flops=8*count*width*width,bytes_accessed=24*MIB,transcendentals=0),
        name="finish",
    )(position,pick,returned,hidden,hidden_grad,tokens,token_grads,every_weight,gains,router,pieces,weights,tables,first,second,own_weights,own_gain)

def gelu_pair(u):
    c=0.7978845608028654
    square=u*u
    t=jnp.tanh(c*u*(1.0+0.044715*square))
    half=0.5*(1.0+t)
    return u*half,half+(0.5*c)*u*(1.0-t*t)*(1.0+0.134145*square)

def expert_kernel(experts,cap,width,hidden_width,send_ref,cot_hbm,w1_hbm,w2_hbm,router_ref,home,result_out,dw1,dw2,router_part,
                  rows,cots,grads,results,row_grads,logit_grads,act,slope,w1,w2,rows_t,
                  local_sem,cot_sem,out_sem,s_rows,r_rows,s_home,r_home):
    f32,b16=jnp.float32,jnp.bfloat16
    pairs=experts//2
    me=lax.axis_index("exp")
    seq=lax.axis_index("seq")
    pair,side=me//2,me%2
    other=1-side
    def device(offset,member):
        return lax.rem(pair+offset+pairs,pairs)*2+member
    barrier=pltpu.get_barrier_semaphore()
    for step in range(1,experts):
        pl.semaphore_signal(barrier,inc=1,device_id=(lax.rem(me+step,experts),seq),device_id_type=MESH)
    load1=pltpu.make_async_copy(w1_hbm,w1,local_sem.at[0])
    load2=pltpu.make_async_copy(w2_hbm,w2,local_sem.at[1])
    own_rows=pltpu.make_async_copy(send_ref.at[me],rows.at[side],local_sem.at[2])
    local=[own_rows,load1,load2]
    cot_loads=[pltpu.make_async_copy(cot_hbm.at[device(-j,m)],cots.at[2*j+m],cot_sem.at[2*j+m]) for j in range(pairs) for m in range(2)]
    for copy in local+cot_loads:
        copy.start()
    pl.semaphore_wait(barrier,experts-1)
    def remote(src,dst,s,r,target):
        return pltpu.make_async_remote_copy(src_ref=src,dst_ref=dst,send_sem=s,recv_sem=r,device_id=(target,seq),device_id_type=MESH)
    started=[]
    def launch(copy):
        copy.start()
        started.append(copy)
    visit=[j for step in range(1,pairs//2+1) for j in sorted({step,pairs-step})]
    launch(remote(send_ref.at[device(0,other)],rows.at[side],s_rows.at[1],r_rows.at[side],device(0,other)))
    for j in visit:
        for m in range(2):
            member=side if m==0 else other
            launch(remote(send_ref.at[device(j,member)],rows.at[2*j+side],s_rows.at[2*j+m],r_rows.at[2*j+side],device(j,member)))
    def wait_slot(landing,r,slot):
        remote(landing,landing,s_rows.at[0],r.at[slot],me).wait_recv()
    chunk=512 if hidden_width%512==0 else 128
    steps=hidden_width//chunk
    lanes=lax.broadcasted_iota(jnp.int32,(2*cap,128),1)
    onehot=jnp.where(lanes==me,1.0,0.0)
    outputs=[]
    def process(j):
        x=rows[2*j:2*j+2].reshape(2*cap,width)
        base=2*j*cap
        span=slice(base,base+2*cap)
        logits=jnp.dot(x,router_ref[...],preferred_element_type=f32)
        logits=jnp.where(lanes<experts,logits,-jnp.inf)
        raised=jnp.exp(logits-jnp.max(logits,axis=1,keepdims=True))
        gates=raised/jnp.sum(raised,axis=1,keepdims=True)
        gate=jnp.sum(gates*onehot,axis=1,keepdims=True)
        for m in range(2):
            cot_loads[2*j+m].wait()
        cot=cots[2*j:2*j+2].reshape(2*cap,width).astype(f32)
        grads[span,:]=(gate*cot).astype(b16)
        def forward(step,carry):
            cols=pl.ds(pl.multiple_of(step*chunk,chunk),chunk)
            pre=jnp.dot(x,w1[:,cols],preferred_element_type=f32)
            a,d=gelu_pair(pre)
            act[span,cols]=a.astype(b16)
            slope[span,cols]=d.astype(b16)
            return carry
        lax.fori_loop(0,steps,forward,0)
        result=jnp.dot(act[span,:],w2[...],preferred_element_type=f32).astype(b16)
        results[2*j:2*j+2]=result.reshape(2,cap,width)
        for m in range(2):
            copy=pltpu.make_async_copy(results.at[2*j+m],result_out.at[device(-j,m)],out_sem.at[2*j+m])
            copy.start()
            outputs.append(copy)
        gate_grad=jnp.sum(cots[2*j:2*j+2].reshape(2*cap,width).astype(f32)*result.astype(f32),axis=1,keepdims=True)
        logit_grad=(gates*(onehot-gate)*gate_grad).astype(b16)
        logit_grads[span,:]=logit_grad
        def backward(step,carry):
            cols=pl.ds(pl.multiple_of(step*chunk,chunk),chunk)
            up=lax.dot_general(grads[span,:],w2[cols,:],NT,preferred_element_type=f32)
            up=up.astype(b16).astype(f32)*slope[span,cols].astype(f32)
            slope[span,cols]=up.astype(b16)
            return carry
        lax.fori_loop(0,steps,backward,0)
        back=lax.dot_general(slope[span,:],w1[...],NT,preferred_element_type=f32)
        back=back+lax.dot_general(logit_grad,router_ref[...],NT,preferred_element_type=f32)
        row_grads[2*j:2*j+2]=back.astype(b16).reshape(2,cap,width)
        for m in range(2):
            member=side if m==0 else other
            if j==0 and m==0:
                copy=pltpu.make_async_copy(row_grads.at[side],home.at[me],local_sem.at[3])
                copy.start()
                outputs.append(copy)
            else:
                launch(remote(row_grads.at[2*j+member],home.at[me],s_home.at[2*j+m],r_home.at[2*j+side],device(-j,member)))
    load1.wait()
    load2.wait()
    own_rows.wait()
    wait_slot(rows.at[other],r_rows,other)
    process(0)
    for j in visit:
        for m in range(2):
            wait_slot(rows.at[2*j+m],r_rows,2*j+m)
        process(j)
    rows_t[...]=jnp.transpose(rows[...].reshape(experts*cap,width))
    router_part[...]=jnp.dot(rows_t[...],logit_grads[...],preferred_element_type=f32)
    def weight_grads(step,carry):
        cols=pl.ds(pl.multiple_of(step*chunk,chunk),chunk)
        dw1[:,cols]=jnp.dot(rows_t[...],slope[:,cols],preferred_element_type=f32).astype(b16)
        dw2[cols,:]=lax.dot_general(act[:,cols],grads[...],TN,preferred_element_type=f32).astype(b16)
        return carry
    lax.fori_loop(0,steps,weight_grads,0)
    for j in range(pairs):
        for m in range(2):
            if j:
                wait_slot(home.at[device(j,m)],r_home,2*j+m)
    wait_slot(home.at[device(0,other)],r_home,other)
    for copy in outputs:
        copy.wait()
    for copy in started:
        copy.wait_send()

def expert_layer(send,cot,w1,w2,router,cid=4):
    experts,cap,width=send.shape
    hidden_width=w1.shape[1]
    b16=jnp.bfloat16
    block=jax.ShapeDtypeStruct((experts,cap,width),b16)
    anywhere=pl.BlockSpec(memory_space=pl.ANY)
    vmem=pl.BlockSpec(memory_space=pltpu.VMEM)
    dma=lambda n: pltpu.SemaphoreType.DMA((n,))
    blocks=pltpu.VMEM((experts,cap,width),b16)
    wide=pltpu.VMEM((experts*cap,hidden_width),b16)
    return pl.pallas_call(
        functools.partial(expert_kernel,experts,cap,width,hidden_width),
        in_specs=[anywhere]*4+[vmem],
        out_specs=[anywhere,anywhere,vmem,vmem,vmem],
        out_shape=[block,block,jax.ShapeDtypeStruct(w1.shape,b16),jax.ShapeDtypeStruct(w2.shape,b16),jax.ShapeDtypeStruct((width,128),jnp.float32)],
        scratch_shapes=[blocks,blocks,pltpu.VMEM((experts*cap,width),b16),blocks,blocks,pltpu.VMEM((experts*cap,128),b16),wide,wide,
            pltpu.VMEM(w1.shape,b16),pltpu.VMEM(w2.shape,b16),pltpu.VMEM((width,experts*cap),b16),
            dma(4)]+[dma(experts)]*6,
        compiler_params=pltpu.CompilerParams(collective_id=cid,has_side_effects=True,vmem_limit_bytes=60*MIB),
        cost_estimate=pl.CostEstimate(flops=12*experts*cap*width*hidden_width,bytes_accessed=40*MIB,transcendentals=experts*cap*hidden_width),
        name="expert_layer",
    )(send,cot,w1,w2,router)

def inverse_rms(values):
    return lax.rsqrt(jnp.mean(values*values,axis=-1,keepdims=True)+EPSILON)

def matmul(left,right,dims=NN):
    return lax.dot_general(left,right,dims,preferred_element_type=jnp.float32)

def swap_parts(values,axis):
    return lax.all_to_all(values,axis,split_axis=0,concat_axis=0,tiled=True)

def reversed_ids(ids):
    flip=np.eye(128,dtype=np.float32)[::-1]
    rows=ids.shape[0]//128
    flip_rows=np.eye(rows,dtype=np.float32)[::-1]
    grid=ids.astype(jnp.bfloat16).reshape(rows,128)
    grid=matmul(grid,jnp.asarray(flip,jnp.bfloat16)).astype(jnp.bfloat16)
    return matmul(jnp.asarray(flip_rows,jnp.bfloat16),grid).reshape(-1).astype(jnp.int32)

def shards(tokens,query_weight,key_weight,value_weight,out_weight,router_weight,attn_gain,moe_gain,bias_table,expert_in,expert_out,expert_id,slot_id,bucket_id,cotangent):
    f32,b16=jnp.float32,jnp.bfloat16
    seq_count,stretch,width=tokens.shape
    seq_devs=lax.axis_size("seq")
    experts=lax.axis_size("exp")
    devices=seq_devs*experts
    length=stretch*seq_devs
    count=seq_count*stretch
    capacity=(5*count+4*experts-1)//(4*experts)
    padded_cap=(capacity+15)//16*16
    buckets,heads=bias_table.shape
    head_dim=width//heads
    groups=seq_devs//seq_count
    own_heads=heads//groups
    per_chunk=2 if own_heads%2==0 else 1
    chunks=own_heads//per_chunk
    used=per_chunk*head_dim
    span=chunks*chunk_span(per_chunk)
    heads_width=groups*chunks*128
    row_block=width//devices
    place=lax.axis_index("seq")
    group=place%groups
    def by_group(weight):
        return weight.reshape(row_block,groups,chunks,per_chunk,head_dim)
    query_part=jnp.pad(by_group(query_weight).reshape(row_block,groups,chunks,used),((0,0),(0,0),(0,0),(0,128-used)))
    both_part=jnp.concatenate([by_group(key_weight),by_group(value_weight)],axis=4).reshape(row_block,groups,chunks,per_chunk*128)
    stacked=jnp.concatenate([query_part,both_part],axis=3).reshape(row_block,groups,span)
    gains=jnp.stack([attn_gain,moe_gain],axis=1)
    small=jnp.pad(jnp.concatenate([router_weight,gains],axis=1),((0,0),(0,126-experts)))
    units=jnp.concatenate([stacked,jnp.broadcast_to(small[:,None],(row_block,groups,128))],axis=2)
    expert_pick=expert_id.reshape(count)
    slot_pick=slot_id.reshape(count)
    slots=experts*padded_cap
    position=jnp.where(slot_pick<capacity,expert_pick*padded_cap+slot_pick,slots)
    hot=(position[None,:]==jnp.arange(slots,dtype=jnp.int32)[:,None]).astype(b16)
    out_full=lax.all_gather(out_weight,BOTH,axis=0,tiled=True)
    out_full=jnp.pad(out_full.reshape(groups*chunks,used,width),((0,0),(0,128-used),(0,0))).reshape(heads_width,width)
    plan=(experts,seq_devs,seq_count,stretch,per_chunk,chunks)
    if row_block%8==0 and row_block*seq_devs%16==0:
        units=jnp.pad(jnp.swapaxes(units,0,1),((0,0),(0,-row_block%16),(0,0)))
        projected,normed,cot_rows,own_weight,first_full=gather_start(plan,row_block,tokens,units,expert_in,position[None,:],cotangent.reshape(count,width),padded_cap)
    else:
        copies=jnp.broadcast_to(tokens[:,None],(seq_count,groups,stretch,width)).reshape(seq_devs,stretch,width)
        own_sequence=swap_parts(copies,"seq").reshape(length,width).astype(f32)
        every=lax.all_gather(units,BOTH,axis=0,tiled=True)
        own_weight=lax.dynamic_index_in_dim(every,group,axis=1,keepdims=False)
        normed=(own_sequence*inverse_rms(own_sequence)*own_weight[:,span+experts].astype(f32)).astype(b16)
        projected=matmul(normed,own_weight[:,:span]).astype(b16)
        first_full=lax.all_gather(expert_in[0],"seq",axis=1,tiled=True)
        cot_rows=matmul(hot,cotangent.reshape(count,width)).astype(b16).reshape(experts,padded_cap,width)
    small_full=own_weight[:,span:]
    router_full=small_full[:,:experts]
    router_wide=jnp.where(jnp.arange(128)[None,:]<experts,small_full,jnp.zeros((),b16))
    attn_gain_full=small_full[:,experts].astype(f32)
    moe_gain_full=small_full[:,experts+1].astype(f32)
    no_id=jnp.full((1,),-1,jnp.int32)
    backward_ids=jnp.concatenate([no_id,bucket_id])[None,:]
    forward_ids=reversed_ids(jnp.concatenate([bucket_id,no_id]))[None,:]
    own_table=lax.dynamic_slice_in_dim(bias_table,group*own_heads,own_heads,axis=1)*LOG2E
    own_table=jnp.pad(own_table.T,((0,-own_heads%8),(0,128-buckets)))
    attended,out32,log_total,cot_arrived,every_weight,second_full=attend(plan,projected,forward_ids,own_table,cot_rows,own_weight,expert_out)
    attended=attended.reshape(count,heads_width)
    tokens_f=tokens.astype(f32).reshape(count,width)
    hidden=tokens_f+matmul(attended,out_full)
    moe_inverse=inverse_rms(hidden)
    moe_in=(hidden*moe_inverse*moe_gain_full).astype(b16)
    send_rows=matmul(hot,moe_in).astype(b16).reshape(experts,padded_cap,width)
    home,result,first_grad,second_grad,router_part=expert_layer(send_rows,cot_arrived,first_full,second_full,router_wide)
    expert_in_grad=lax.psum_scatter(first_grad[None],"seq",scatter_dimension=2,tiled=True)[0]
    expert_out_grad=lax.psum_scatter(second_grad[None],"seq",scatter_dimension=1,tiled=True)[0]
    gain_rows=jnp.transpose(small_full[:,experts:experts+2].astype(f32))
    home=home.reshape(slots,width)
    positions=position[:,None]
    hidden_grad,heads_grad,out_part=combine(experts,positions,home,hidden,cotangent.reshape(count,width),attended,out_full,gain_rows[1:2],router_part)
    out_part=jnp.concatenate([out_part[:,:width].reshape(groups*chunks,128,width)[:,:used].reshape(width,width),out_part[:width,width:]],axis=1) if used<128 else out_part
    out_piece=jnp.moveaxis(out_part.reshape(experts*seq_count,groups,row_block,width+128),1,0)
    out_piece=jnp.pad(out_piece,((0,0),(0,0),(0,-row_block%16),(0,0)))
    token_grads,returned,out_pieces,weight_pieces,tables=attend_back(plan,projected,out32,log_total,backward_ids,own_table,normed,heads_grad.reshape(seq_count,stretch,heads_width),result,out_piece)
    inside=row_block%8==0
    token_grads=token_grads.reshape(count,groups*span)
    own_weights=jnp.stack([query_weight,key_weight,value_weight])
    output,input_grad,expert_in_grad,expert_out_grad,out_sum,small_sum,*weight_grads,attn_gain_grad,tables=finish(experts,groups,per_chunk,chunks,inside,positions,expert_pick[:,None],returned.reshape(slots,width),hidden,hidden_grad,tokens.reshape(count,width),token_grads,every_weight,gain_rows,router_wide,out_pieces,weight_pieces,tables,expert_in_grad,expert_out_grad,own_weights,attn_gain.astype(f32)[:,None])
    attn_gain_grad=attn_gain_grad[:,0]
    output=output.reshape(seq_count,stretch,width)
    bias_table_grad=tables[:,:own_heads,:buckets].reshape(heads,buckets).T
    if not inside:
        tokens_f=tokens.astype(f32).reshape(count,width)
        normed_own=(tokens_f*inverse_rms(tokens_f)*attn_gain_full).astype(b16)
        parts=matmul(normed_own,token_grads,TN).astype(b16).reshape(devices,row_block,groups*chunks,1+per_chunk,128)
        summed=jnp.sum(swap_parts(parts,BOTH).astype(f32),axis=0)
        both_sum=summed[:,:,1:].reshape(row_block,groups*chunks,per_chunk,2,head_dim)
        weight_grads=[summed[:,:,0,:used].reshape(row_block,width)]+[both_sum[:,:,:,i].reshape(row_block,width) for i in range(2)]
        attn_gain_grad=jnp.sum(jnp.stack(weight_grads)*own_weights.astype(f32),axis=(0,2))/attn_gain.astype(f32)
    return (
        output,
        input_grad.reshape(seq_count,stretch,width),
        weight_grads[0],weight_grads[1],weight_grads[2],
        out_sum,
        small_sum[:,:experts],
        attn_gain_grad,
        small_sum[:,experts],
        bias_table_grad,
        expert_in_grad[None],
        expert_out_grad[None],
    )

def solution(mesh):
    tokens=P("exp","seq",None)
    rows=P(BOTH,None)
    return jax.shard_map(
        shards,
        mesh=mesh,
        in_specs=(tokens,rows,rows,rows,rows,rows,P(BOTH),P(BOTH),P(),P("exp",None,"seq"),P("exp","seq",None),P("exp","seq"),P("exp","seq"),P(),tokens),
        out_specs=(tokens,tokens,rows,rows,rows,rows,rows,P(BOTH),P(BOTH),P(),P("exp",None,"seq"),P("exp","seq",None)),
        check_vma=False,
    )
```
